256 devices in a mesh: row: 16 (over z, x_hi), col: 4 (over y), depth: 4 (over x_lo, core).
Axes of the slice: x: 4 (x_hi: 2, x_lo: 2; x = x_hi * 2 + x_lo), y: 4, z: 8, core: 2. Of those that a mesh axis runs over, the one named last changes fastest.
Arguments:
- grad_partial: bfloat16 [4, 8192, 8192], P('depth', 'row', 'col'), may hold values from -6 to 6
- grad_scale: float32 [4, 64, 8192], P('depth', 'row', 'col'), may hold values from 0.01 to 3
- momentum: float32 [8192, 8192], P('row', ('col', 'depth')), may hold values from -6 to 6
Outputs:
- new_momentum: float32 [8192, 8192], P('row', ('col', 'depth'))
- update: float32 [8192, 8192], P('row', ('col', 'depth'))
The draws below stay inside these ranges and needn't reach their ends.
All inputs are finite; a program needn't handle non-finite values.
Results may differ from the reference program's by a relative error of at most 0.023.
Values may be sent and summed in bfloat16 or wider, within the bound.
No kernel may reach another device: no remote copies, remote signals or barrier semaphores. Data moves between devices by JAX's collectives and lax.ppermute only.
A program may use at most 64 MiB of HBM per device.

```python
import math
import jax
import jax.numpy as jnp
from jax import lax

M = 8192
QBLOCK = 128
PARTIALS = 4
PIECE = 128


def draw_grad_scale(key, part):
    key = jax.random.fold_in(key, 7)
    blocks = M // QBLOCK
    ramp = 3.0 ** (jnp.arange(blocks, dtype=jnp.float32) / max(blocks - 1, 1))
    noise = jnp.exp(jax.random.uniform(key, (PARTIALS, blocks, M), jnp.float32, math.log(0.1), math.log(1.0)))
    return noise * ramp[None, :, None]


def raised(result, own_key, source, target, parts, factor):
    owner, partner = [(jnp.arange(result.shape[position]) // (result.shape[position] // parts)).reshape([-1 if axis == position else 1 for axis in range(result.ndim)]) for position in (source, target)]
    chosen = jax.random.permutation(own_key, parts)[partner]
    strong = (owner == chosen) | (owner == (partner + parts // 2) % parts)
    return jnp.where(strong, factor * result, result)


def levels(key, dims, split, smallest, largest):
    gain = 1.0
    for dim, blocks in split:
        draws = jax.random.uniform(jax.random.fold_in(jax.random.fold_in(key, 6), dim), (blocks,), jnp.float32, smallest / len(split), largest / len(split))
        gain = gain * jnp.repeat(jnp.exp(draws), dims[dim] // blocks).reshape((-1,) + (1,) * (len(dims) - 1 - dim))
    return gain


def normal_values(own_key, shape, scale, bound, pieces=(), kind=jnp.bfloat16):
    drawn = scale * jax.random.normal(own_key, shape, jnp.float32)
    if pieces:
        drawn = drawn * levels(own_key, shape, pieces, -0.22, 0.18)
    return jnp.clip(drawn, -bound, bound).astype(kind)


def gaussian_with(stream_key, shape, deviation, bound, pieces, heavy, held_as=jnp.bfloat16):
    values = deviation * jax.random.normal(stream_key, shape, jnp.float32)
    if pieces:
        values = values * levels(stream_key, shape, pieces, -0.22, 0.18)
    return jnp.clip(raised(values, jax.random.fold_in(stream_key, 3), *heavy), -bound, bound).astype(held_as)


def setup_inputs(seed: int = 0) -> dict:
    key_list = jax.random.split(jax.random.key(seed), 4)
    grad_partial = gaussian_with(key_list[0], (PARTIALS, M, M), 1.0, 6.0, ((0, 4), (1, 16), (2, 4)), (0, 2, 4, 2.0))
    grad_scale = draw_grad_scale(jax.random.fold_in(key_list[3], 71), 0)
    momentum = normal_values(key_list[2], (M, M), 1.0, 6.0, ((0, 16), (1, 16)), jnp.float32)
    return {"grad_partial": grad_partial, "grad_scale": grad_scale, "momentum": momentum}


BETA = 0.95
EPSILON = 1e-07

def reference(grad_partial, grad_scale, momentum):
    groups = M // QBLOCK
    quant_values = grad_partial.astype(jnp.float32).reshape(PARTIALS, groups, QBLOCK, M)
    gradient = lax.optimization_barrier(jnp.sum((quant_values * grad_scale[:, :, None, :]).reshape(PARTIALS, M, M), axis=0))
    new_momentum = BETA * momentum + gradient
    nesterov = gradient + BETA * new_momentum
    total_sq = jnp.sum(nesterov * nesterov)
    ortho_input = (nesterov * (math.sqrt(M) / (1.5 * (jnp.sqrt(total_sq) + EPSILON)))).astype(jnp.bfloat16)
    grouped = ortho_input.reshape(M, M // (PARTIALS * PIECE), PARTIALS, PIECE)

    def add_part(running, index):
        columns = lax.dynamic_index_in_dim(grouped, index, 2, keepdims=False).reshape(M, M // PARTIALS)
        term = lax.dot_general(columns, columns, (((1,), (1,)), ((), ())), preferred_element_type=jnp.float32)
        rounded = lax.optimization_barrier(term.astype(jnp.bfloat16)).astype(jnp.float32)
        return (running + rounded, None)
    gram_sum, unused_out = lax.scan(add_part, jnp.zeros((M, M), jnp.float32), jnp.arange(PARTIALS, dtype=jnp.int32))
    gram_matrix = gram_sum.astype(jnp.bfloat16)
    product = jnp.dot(gram_matrix, ortho_input, preferred_element_type=jnp.float32)
    update = math.sqrt(M) * (1.5 * ortho_input.astype(jnp.float32) - 0.5 * product)
    return (new_momentum, update)
```

```python
import math

import jax
import jax.numpy as jnp
from jax import lax
from jax.sharding import PartitionSpec as P

M = 8192
BETA = 0.95
EPSILON = 1e-07
F32 = jnp.float32
BF16 = jnp.bfloat16

NZ, NX, NY, NC = 8, 4, 4, 2
ZPERM = {
    s: [(r, (r + 2 * s) % 16) for r in range(16)] for s in (1, -1)
}
YPERM = {s: [(y, (y + s) % 4) for y in range(4)] for s in (1, -1)}
SIB = [(d, d ^ 1) for d in range(4)]
INNER = [(d, d ^ 2) for d in range(4)]
OUTER = [(r * 4 + d, (r ^ 1) * 4 + (d ^ 2)) for r in range(16) for d in range(4)]


def sib(v):
    return lax.ppermute(v, "depth", SIB)


def inner(v):
    return lax.ppermute(v, "depth", INNER)


def outer(v):
    return lax.ppermute(v, ("row", "depth"), OUTER)


def zhop(v, s):
    return lax.ppermute(v, "row", ZPERM[s])


def yhop(v, s):
    return lax.ppermute(v, "col", YPERM[s])


def add(*vs):
    total = vs[0].astype(F32)
    for v in vs[1:]:
        total = total + v.astype(F32)
    return total


def all_sum(v):
    for bit in (1, 2):
        v = v + lax.ppermute(v, "depth", [(d, d ^ bit) for d in range(4)])
    for bit in (1, 2):
        v = v + lax.ppermute(v, "col", [(d, d ^ bit) for d in range(4)])
    for bit in (1, 2, 4, 8):
        v = v + lax.ppermute(v, "row", [(d, d ^ bit) for d in range(16)])
    return v


def dot_t(a, b):
    return lax.dot_general(a, b, (((1,), (1,)), ((), ())), preferred_element_type=F32)


def gram_all_reduce(panel, columns, y):
    q = panel.shape[0] // NY
    h = q // 2

    def term(k):
        rows = lax.dynamic_slice_in_dim(panel, ((y + k) % NY) * q, q, 0)
        return dot_t(rows, columns)

    far = term(2).astype(BF16)
    r1 = yhop(far[:h], 1)
    l1 = yhop(far[h:], -1)
    right = term(1)
    left = term(3)
    right = jnp.concatenate([add(right[:h], r1), right[h:]], 0).astype(BF16)
    left = jnp.concatenate([left[:h], add(left[h:], l1)], 0).astype(BF16)
    r2 = yhop(right, 1)
    l2 = yhop(left, -1)
    own = add(term(0), r2, l2).astype(BF16)
    r3 = yhop(own, 1)
    l3 = yhop(own, -1)
    r4 = yhop(r3[:h], 1)
    l4 = yhop(l3[h:], -1)
    whole = jnp.zeros((NY * q, columns.shape[0]), BF16)
    for k, part in ((0, own), (3, r3), (1, l3), (2, jnp.concatenate([r4, l4], 0))):
        whole = lax.dynamic_update_slice_in_dim(whole, part, ((y + k) % NY) * q, 0)
    return whole


def body(grad_partial, grad_scale, momentum):
    y = lax.axis_index("col")
    depth = lax.axis_index("depth")
    xl, c = depth // 2, depth % 2
    quant = grad_partial[0].reshape(4, 128, 2, 2, 512)
    scale = grad_scale[0].reshape(4, 1, 2, 2, 512)

    def pick(v, axis, index):
        return lax.dynamic_index_in_dim(v, index, axis, keepdims=False)

    def scaled(col_core):
        return (
            pick(quant, 3, col_core).astype(F32) * pick(scale, 3, col_core)
        ).reshape(512, 2, 512)

    arrived = sib(scaled(1 - c).astype(BF16))
    pair = scaled(c) + arrived.astype(F32)
    arrived = inner(pick(pair, 1, 1 - xl).astype(BF16))
    gradient = pick(pair, 1, xl) + arrived.astype(F32)
    new_momentum = BETA * momentum + gradient
    nesterov = gradient + BETA * new_momentum
    squares = jnp.sum((nesterov * nesterov).reshape(64, 8, 4, 128), axis=(0, 2))
    tile = nesterov.astype(BF16)

    rows4 = tile.reshape(2, 2, 128, 512)
    mine = pick(rows4, 1, c)
    theirs = sib(pick(rows4, 1, 1 - c))
    both = jnp.concatenate([mine, theirs], axis=2)
    keep = pick(both, 0, xl)
    got = inner(pick(both, 0, 1 - xl))
    piece = jnp.concatenate([keep, got], axis=1)

    t_in = inner(tile)
    t_out = outer(tile)
    t_far = jnp.concatenate([outer(t_in[:256]), inner(t_out[256:])], axis=0)
    grid = [[tile, t_in], [t_far, t_out]]
    panel = jnp.concatenate(
        [
            jnp.concatenate([part for t in line for part in (t, sib(t))], axis=1)
            for line in grid
        ],
        axis=0,
    )

    right, left = piece, piece
    pieces = [[piece]]
    for hop in range(3):
        right = zhop(right, 1)
        left = zhop(left, -1)
        pieces.append([right, left])
    pieces.append([zhop(right[:64], 1), zhop(left[64:], -1)])
    groups = [pieces[0] + pieces[1] + pieces[2], pieces[3] + pieces[4]]
    columns = [jnp.concatenate(g, axis=0) for g in groups]

    gram = [gram_all_reduce(panel, cols, y) for cols in columns]
    gram = jnp.concatenate(gram, axis=1)
    inner_rows = jnp.concatenate(columns, axis=0).reshape(1024, 2, 2, 512)

    def product(core):
        return jnp.dot(
            gram, inner_rows[:, :, core].reshape(1024, 1024), preferred_element_type=F32
        )

    arrived = sib(product(1).astype(BF16))
    total = product(0) + arrived.astype(F32)
    t_own, t_in = total[:512, :512], total[:512, 512:]
    t_far, t_out = total[512:, :512], total[512:, 512:]
    t_far = t_far.astype(BF16)
    a1 = inner(t_far[:256])
    b1 = outer(t_far[256:])
    to_out = jnp.concatenate([add(t_out[:256], a1), t_out[256:]], 0).astype(BF16)
    to_in = jnp.concatenate([t_in[:256], add(t_in[256:], b1)], 0).astype(BF16)
    prod = add(t_own, inner(to_in), outer(to_out))

    total_sq = jnp.sum(all_sum(squares))
    gain = math.sqrt(M) / (1.5 * (jnp.sqrt(total_sq) + EPSILON))
    update = math.sqrt(M) * (
        (1.5 * gain) * nesterov - (0.5 * gain * gain * gain) * prod
    )
    return (new_momentum, update)


def solution(mesh):
    placed = (P("depth", "row", "col"), P("depth", "row", "col"), P("row", ("col", "depth")))
    return jax.shard_map(
        body,
        mesh=mesh,
        in_specs=placed,
        out_specs=(P("row", ("col", "depth")), P("row", ("col", "depth"))),
        check_vma=False,
    )
```

```python
import functools
import math

import jax
import jax.numpy as jnp
from jax import lax
from jax.experimental import pallas as pl
from jax.experimental.pallas import tpu as pltpu
from jax.sharding import PartitionSpec as P

M = 8192
BETA = 0.95
EPSILON = 1e-07
F32 = jnp.float32
BF16 = jnp.bfloat16

NY = 4
TILE = 512
PIECE = 128
ZPERM = {s: [(r, (r + 2 * s) % 16) for r in range(16)] for s in (1, -1)}
YPERM = {s: [(y, (y + s) % 4) for y in range(4)] for s in (1, -1)}
SIB = [(d, d ^ 1) for d in range(4)]
INNER = [(d, d ^ 2) for d in range(4)]
OUTER = [(r * 4 + d, (r ^ 1) * 4 + (d ^ 2)) for r in range(16) for d in range(4)]


def sib(v):
    return lax.ppermute(v, "depth", SIB)


def inner(v):
    return lax.ppermute(v, "depth", INNER)


def outer(v):
    return lax.ppermute(v, ("row", "depth"), OUTER)


def zhop(v, s):
    return lax.ppermute(v, "row", ZPERM[s])


def yhop(v, s):
    return lax.ppermute(v, "col", YPERM[s])


def swap_add(v, axis, bit):
    return v + lax.ppermute(v, axis, [(i, i ^ bit) for i in range(lax.axis_size(axis))])


def add(*vs):
    total = vs[0].astype(F32)
    for v in vs[1:]:
        total = total + v.astype(F32)
    return total


VMEM = pl.BlockSpec(memory_space=pltpu.VMEM)
SMEM = pl.BlockSpec(memory_space=pltpu.SMEM)


def gram_kernel(sources, y_ref, *refs):
    n_in = 8 + max(i for piece in sources for _, parts in enumerate(piece) for i, _, _ in parts) + 1
    tiles, parts_in = refs[:8], refs[8:n_in]
    joined, far0, far1, right, left, own, held = refs[n_in:]
    for p, piece in enumerate(sources):
        for half, parts in enumerate(piece):
            row = p * PIECE
            for i, start, size in parts:
                joined[row : row + size, half * 1024 : half * 1024 + 1024] = parts_in[i][
                    start : start + size, :
                ]
                row += size
    y = y_ref[0]
    for block in range(4):
        line, start = block // 2, (block % 2) * 256
        total = None
        for k in range(4):
            term = lax.dot_general(
                tiles[line * 4 + k][start : start + 256, :],
                joined[:, k * TILE : (k + 1) * TILE],
                (((1,), (1,)), ((), ())),
                preferred_element_type=F32,
            )
            total = term if total is None else total + term
        held[lax.rem(block + 4 - y, 4)] = total.astype(BF16)
    own[...] = held[0]
    right[...] = held[1]
    far0[...] = held[2, :128]
    far1[...] = held[2, 128:]
    left[...] = held[3]


def gram(y, tiles, arrays, sources):
    n = len(sources) * PIECE
    shapes = [(n, 2048), (128, n), (128, n), (256, n), (256, n), (256, n)]
    return pl.pallas_call(
        functools.partial(gram_kernel, sources),
        out_shape=[jax.ShapeDtypeStruct(s, BF16) for s in shapes],
        in_specs=[SMEM] + [VMEM] * (8 + len(arrays)),
        out_specs=[VMEM] * 6,
        scratch_shapes=[pltpu.VMEM((4, 256, n), BF16)],
        compiler_params=pltpu.CompilerParams(vmem_limit_bytes=32 << 20),
        cost_estimate=pl.CostEstimate(
            flops=2 * 1024 * 2048 * n, bytes_accessed=8 << 20, transcendentals=0
        ),
    )(y, *tiles, *arrays)


def product_kernel(core, widths, y_ref, *refs):
    out = refs[-1]
    y = y_ref[0]
    for k in range(4):
        rows = pl.ds(pl.multiple_of(lax.rem(y + k, 4) * 256, 256), 256)
        for half in range(2):
            cols = slice(half * 1024 + core * TILE, half * 1024 + core * TILE + TILE)
            total = None
            for chunk in range(len(widths)):
                own, r3, l3, r4, l4, joined = refs[chunk * 6 : chunk * 6 + 6]
                if k == 2:
                    left = jnp.concatenate([r4[...], l4[...]], axis=0)
                else:
                    left = (own, l3, None, r3)[k][...]
                term = jnp.dot(left, joined[:, cols], preferred_element_type=F32)
                total = term if total is None else total + term
            out[half, rows, :] = total.astype(BF16)


def product(y, core, chunks):
    widths = [c[0].shape[1] for c in chunks]
    return pl.pallas_call(
        functools.partial(product_kernel, core, widths),
        out_shape=jax.ShapeDtypeStruct((2, 1024, TILE), BF16),
        in_specs=[SMEM] + [VMEM] * (6 * len(chunks)),
        out_specs=VMEM,
        compiler_params=pltpu.CompilerParams(vmem_limit_bytes=32 << 20),
        cost_estimate=pl.CostEstimate(
            flops=2 * 1024 * 1024 * 1024, bytes_accessed=8 << 20, transcendentals=0
        ),
    )(y, *[a for c in chunks for a in c])


def gram_all_reduce(far0, far1, right, left, own):
    r1 = yhop(far0, 1)
    l1 = yhop(far1, -1)
    right = jnp.concatenate([add(right[:128], r1).astype(BF16), right[128:]], 0)
    left = jnp.concatenate([left[:128], add(left[128:], l1).astype(BF16)], 0)
    r2 = yhop(right, 1)
    l2 = yhop(left, -1)
    own = add(own, r2, l2).astype(BF16)
    r3 = yhop(own, 1)
    l3 = yhop(own, -1)
    r4 = yhop(r3[:128], 1)
    l4 = yhop(l3[128:], -1)
    return own, r3, l3, r4, l4


def body(grad_partial, grad_scale, momentum):
    y = lax.axis_index("col").astype(jnp.int32).reshape(1)
    depth = lax.axis_index("depth")
    xl, c = depth // 2, depth % 2
    quant, scale = grad_partial[0], grad_scale[0]

    def column_part(v, half, core):
        return v[:, (half * 2 + core) * TILE : (half * 2 + core + 1) * TILE]

    def scaled(half, mine):
        pick = (c == 0) if mine else (c == 1)
        q = jnp.where(pick, column_part(quant, half, 0), column_part(quant, half, 1))
        s = jnp.where(pick, column_part(scale, half, 0), column_part(scale, half, 1))
        return (q.astype(F32).reshape(4, 128, TILE) * s[:, None, :]).reshape(TILE, TILE)

    arrived = sib(jnp.stack([scaled(0, False), scaled(1, False)]).astype(BF16))
    low = scaled(0, True) + arrived[0].astype(F32)
    high = scaled(1, True) + arrived[1].astype(F32)
    arrived = inner(jnp.where(xl == 0, high, low).astype(BF16))
    gradient = jnp.where(xl == 0, low, high) + arrived.astype(F32)
    new_momentum = BETA * momentum + gradient
    nesterov = gradient + BETA * new_momentum
    squares = jnp.sum((nesterov * nesterov).reshape(64, 8, TILE), axis=0)
    squares = squares[:, :128] + squares[:, 128:256] + squares[:, 256:384] + squares[:, 384:]
    tile = nesterov.astype(BF16)

    tile_s = sib(tile)

    def rows_of(half):
        start = (half * 2 + c) * PIECE
        return jnp.concatenate(
            [lax.dynamic_slice_in_dim(v, start, PIECE, 0) for v in (tile, tile_s)], axis=1
        )

    a = rows_of(xl)
    b = inner(rows_of(1 - xl))
    ra = zhop(a, 1)
    la = zhop(a, -1)
    t_in = inner(tile)
    t_out = outer(tile)
    v = swap_add(squares, "depth", 1)
    b, v = lax.optimization_barrier((b, v))
    r2 = zhop(jnp.concatenate([b, ra], axis=0), 1)
    l2 = zhop(jnp.concatenate([la, b], axis=0), -1)
    t_far = jnp.concatenate([outer(t_in[:256]), inner(t_out[256:])], axis=0)
    tiles = [t for v in (t_in, t_far, t_out) for t in (v, sib(v))]
    tiles = [tile, tile_s] + tiles
    v = swap_add(swap_add(swap_add(v, "depth", 2), "col", 1), "col", 2)
    r2, l2, v = lax.optimization_barrier((r2, l2, v))
    r3 = zhop(r2, 1)
    l3 = zhop(l2, -1)
    v = swap_add(swap_add(v, "row", 1), "row", 2)
    r3, l3, v = lax.optimization_barrier((r3, l3, v))
    r4 = zhop(r3[:192], 1)
    l4 = zhop(l3[64:], -1)
    v = swap_add(v, "row", 4)
    r4, l4, v = lax.optimization_barrier((r4, l4, v))
    r5 = zhop(r4[:64], 1)
    l5 = zhop(l4[128:], -1)
    v = swap_add(v, "row", 8)
    r5, l5, v = lax.optimization_barrier((r5, l5, v))

    first = gram(
        y,
        tiles,
        [a, b, ra, la, r2, l2, r3, l3],
        [
            [[(0, 0, 128)], [(1, 0, 128)]],
            [[(2, 0, 128)], [(4, 0, 128)]],
            [[(3, 0, 128)], [(5, 128, 128)]],
            [[(4, 128, 128)], [(6, 0, 128)]],
            [[(5, 0, 128)], [(7, 128, 128)]],
        ],
    )
    chunk1 = gram_all_reduce(*first[1:]) + (first[0],)
    second = gram(
        y,
        tiles,
        [r3, l3, r4, l4, r5, l5],
        [
            [[(0, 128, 128)], [(2, 0, 128)]],
            [[(1, 0, 128)], [(3, 64, 128)]],
            [[(2, 128, 64), (3, 0, 64)], [(4, 0, 64), (5, 0, 64)]],
        ],
    )
    chunk2 = gram_all_reduce(*second[1:]) + (second[0],)

    arrived = sib(product(y, 1, [chunk1, chunk2]))
    mine = product(y, 0, [chunk1, chunk2])
    total = mine.astype(F32) + arrived.astype(F32)
    t_own, t_far = total[0, :512], total[0, 512:].astype(BF16)
    t_in, t_out = total[1, :512], total[1, 512:]
    a1 = inner(t_far[:256])
    b1 = outer(t_far[256:])
    to_out = jnp.concatenate([add(t_out[:256], a1), t_out[256:]], 0).astype(BF16)
    to_in = jnp.concatenate([t_in[:256], add(t_in[256:], b1)], 0).astype(BF16)
    prod = add(t_own, inner(to_in), outer(to_out))

    total_sq = jnp.sum(v)
    gain = math.sqrt(M) / (1.5 * (jnp.sqrt(total_sq) + EPSILON))
    update = math.sqrt(M) * (
        (1.5 * gain) * nesterov - (0.5 * gain * gain * gain) * prod
    )
    return (new_momentum, update)


def solution(mesh):
    placed = (P("depth", "row", "col"), P("depth", "row", "col"), P("row", ("col", "depth")))
    return jax.shard_map(
        body,
        mesh=mesh,
        in_specs=placed,
        out_specs=(P("row", ("col", "depth")), P("row", ("col", "depth"))),
        check_vma=False,
    )
```

```python
import functools
import math

import jax
import jax.numpy as jnp
from jax import lax
from jax.experimental import pallas as pl
from jax.experimental.pallas import tpu as pltpu
from jax.sharding import PartitionSpec as P

M = 8192
BETA = 0.95
EPSILON = 1e-07
F32 = jnp.float32
BF16 = jnp.bfloat16

NY = 4
TILE = 512
PIECE = 128
ZPERM = {s: [(r, (r + 2 * s) % 16) for r in range(16)] for s in (1, -1)}
YPERM = {s: [(y, (y + s) % 4) for y in range(4)] for s in (1, -1)}
SIB = [(d, d ^ 1) for d in range(4)]
INNER = [(d, d ^ 2) for d in range(4)]
OUTER = [(r * 4 + d, (r ^ 1) * 4 + (d ^ 2)) for r in range(16) for d in range(4)]


def sib(v):
    return lax.ppermute(v, "depth", SIB)


def inner(v):
    return lax.ppermute(v, "depth", INNER)


def outer(v):
    return lax.ppermute(v, ("row", "depth"), OUTER)


def zhop(v, s):
    return lax.ppermute(v, "row", ZPERM[s])


def yhop(v, s):
    return lax.ppermute(v, "col", YPERM[s])


def swap_add(v, axis, bit):
    return v + lax.ppermute(v, axis, [(i, i ^ bit) for i in range(lax.axis_size(axis))])


def add(*vs):
    total = vs[0].astype(F32)
    for v in vs[1:]:
        total = total + v.astype(F32)
    return total


VMEM = pl.BlockSpec(memory_space=pltpu.VMEM)
SMEM = pl.BlockSpec(memory_space=pltpu.SMEM)


def gram_kernel(sources, y_ref, *refs):
    n_in = 8 + max(i for piece in sources for _, parts in enumerate(piece) for i, _, _ in parts) + 1
    tiles, parts_in = refs[:8], refs[8:n_in]
    joined, far0, far1, right, left, own, held = refs[n_in:]
    for p, piece in enumerate(sources):
        for half, parts in enumerate(piece):
            row = p * PIECE
            for i, start, size in parts:
                joined[row : row + size, half * 1024 : half * 1024 + 1024] = parts_in[i][
                    start : start + size, :
                ]
                row += size
    y = y_ref[0]
    for block in range(4):
        line, start = block // 2, (block % 2) * 256
        total = None
        for k in range(4):
            term = lax.dot_general(
                tiles[line * 4 + k][start : start + 256, :],
                joined[:, k * TILE : (k + 1) * TILE],
                (((1,), (1,)), ((), ())),
                preferred_element_type=F32,
            )
            total = term if total is None else total + term
        held[lax.rem(block + 4 - y, 4)] = total.astype(BF16)
    own[...] = held[0]
    right[...] = held[1]
    far0[...] = held[2, :128]
    far1[...] = held[2, 128:]
    left[...] = held[3]


def gram(y, tiles, arrays, sources):
    n = len(sources) * PIECE
    shapes = [(n, 2048), (128, n), (128, n), (256, n), (256, n), (256, n)]
    return pl.pallas_call(
        functools.partial(gram_kernel, sources),
        out_shape=[jax.ShapeDtypeStruct(s, BF16) for s in shapes],
        in_specs=[SMEM] + [VMEM] * (8 + len(arrays)),
        out_specs=[VMEM] * 6,
        scratch_shapes=[pltpu.VMEM((4, 256, n), BF16)],
        compiler_params=pltpu.CompilerParams(vmem_limit_bytes=32 << 20),
        cost_estimate=pl.CostEstimate(
            flops=2 * 1024 * 2048 * n, bytes_accessed=8 << 20, transcendentals=0
        ),
    )(y, *tiles, *arrays)


def product_kernel(core, widths, y_ref, *refs):
    out = refs[-1]
    y = y_ref[0]
    for k in range(4):
        rows = pl.ds(pl.multiple_of(lax.rem(y + k, 4) * 256, 256), 256)
        for half in range(2):
            cols = slice(half * 1024 + core * TILE, half * 1024 + core * TILE + TILE)
            total = None
            for chunk in range(len(widths)):
                own, r3, l3, r4, l4, joined = refs[chunk * 6 : chunk * 6 + 6]
                if k == 2:
                    left = jnp.concatenate([r4[...], l4[...]], axis=0)
                else:
                    left = (own, l3, None, r3)[k][...]
                term = jnp.dot(left, joined[:, cols], preferred_element_type=F32)
                total = term if total is None else total + term
            out[half, rows, :] = total.astype(BF16)


def product(y, core, chunks):
    widths = [c[0].shape[1] for c in chunks]
    return pl.pallas_call(
        functools.partial(product_kernel, core, widths),
        out_shape=jax.ShapeDtypeStruct((2, 1024, TILE), BF16),
        in_specs=[SMEM] + [VMEM] * (6 * len(chunks)),
        out_specs=VMEM,
        compiler_params=pltpu.CompilerParams(vmem_limit_bytes=32 << 20),
        cost_estimate=pl.CostEstimate(
            flops=2 * 1024 * 1024 * 1024, bytes_accessed=8 << 20, transcendentals=0
        ),
    )(y, *[a for c in chunks for a in c])


def together(steps, v, *arrays):
    for axis, bit in steps:
        v = swap_add(v, axis, bit)
    return lax.optimization_barrier((v, *arrays))


def start_sum(far0, far1):
    return yhop(far0, 1), yhop(far1, -1)


def gram_all_reduce(r1, l1, right, left, own, v=None):
    steps = [("depth", 1), ("depth", 2), ("col", 1), ("col", 2), ("row", 1), ("row", 2)]
    if v is not None:
        v, r1, l1 = together(steps[:1], v, r1, l1)
    right = jnp.concatenate([add(right[:128], r1).astype(BF16), right[128:]], 0)
    left = jnp.concatenate([left[:128], add(left[128:], l1).astype(BF16)], 0)
    r2 = yhop(right, 1)
    l2 = yhop(left, -1)
    if v is not None:
        v, r2, l2 = together(steps[1:3], v, r2, l2)
    own = add(own, r2, l2).astype(BF16)
    r3 = yhop(own, 1)
    l3 = yhop(own, -1)
    if v is not None:
        v, r3, l3 = together(steps[3:5], v, r3, l3)
    r4 = yhop(r3[:128], 1)
    l4 = yhop(l3[128:], -1)
    if v is not None:
        v, r4, l4 = together(steps[5:], v, r4, l4)
        return v, (own, r3, l3, r4, l4)
    return own, r3, l3, r4, l4


def body(grad_partial, grad_scale, momentum):
    y = lax.axis_index("col").astype(jnp.int32).reshape(1)
    depth = lax.axis_index("depth")
    xl, c = depth // 2, depth % 2
    quant, scale = grad_partial[0], grad_scale[0]

    def column_part(v, half, core):
        return v[:, (half * 2 + core) * TILE : (half * 2 + core + 1) * TILE]

    def scaled(half, mine):
        pick = (c == 0) if mine else (c == 1)
        q = jnp.where(pick, column_part(quant, half, 0), column_part(quant, half, 1))
        s = jnp.where(pick, column_part(scale, half, 0), column_part(scale, half, 1))
        return (q.astype(F32).reshape(4, 128, TILE) * s[:, None, :]).reshape(TILE, TILE)

    arrived = sib(jnp.stack([scaled(0, False), scaled(1, False)]).astype(BF16))
    low = scaled(0, True) + arrived[0].astype(F32)
    high = scaled(1, True) + arrived[1].astype(F32)
    arrived = inner(jnp.where(xl == 0, high, low).astype(BF16))
    gradient = jnp.where(xl == 0, low, high) + arrived.astype(F32)
    new_momentum = BETA * momentum + gradient
    nesterov = gradient + BETA * new_momentum
    squares = jnp.sum((nesterov * nesterov).reshape(64, 8, TILE), axis=0)
    squares = squares[:, :128] + squares[:, 128:256] + squares[:, 256:384] + squares[:, 384:]
    tile = nesterov.astype(BF16)

    tile_s = sib(tile)

    def rows_of(half):
        start = (half * 2 + c) * PIECE
        return jnp.concatenate(
            [lax.dynamic_slice_in_dim(v, start, PIECE, 0) for v in (tile, tile_s)], axis=1
        )

    a = rows_of(xl)
    b = inner(rows_of(1 - xl))
    ra = zhop(a, 1)
    la = zhop(a, -1)
    t_in = inner(tile)
    t_out = outer(tile)
    r2 = zhop(jnp.concatenate([b, ra], axis=0), 1)
    l2 = zhop(jnp.concatenate([la, b], axis=0), -1)
    far_a, far_b = outer(t_in[:256]), inner(t_out[256:])
    r3 = zhop(r2, 1)
    l3 = zhop(l2, -1)
    far_a, far_b, r3, l3 = lax.optimization_barrier((far_a, far_b, r3, l3))
    t_far = jnp.concatenate([far_a, far_b], axis=0)
    t_in, t_out, r2, l2 = lax.optimization_barrier((t_in, t_out, r2, l2))
    tiles = [t for v in (t_in, t_far, t_out) for t in (v, sib(v))]
    tiles = [tile, tile_s] + tiles
    r4 = zhop(r3[:192], 1)
    l4 = zhop(l3[64:], -1)
    first = gram(
        y,
        tiles,
        [a, b, ra, la, r2, l2, r3, l3],
        [
            [[(0, 0, 128)], [(1, 0, 128)]],
            [[(2, 0, 128)], [(4, 0, 128)]],
            [[(3, 0, 128)], [(5, 128, 128)]],
            [[(4, 128, 128)], [(6, 0, 128)]],
            [[(5, 0, 128)], [(7, 128, 128)]],
        ],
    )
    r4, l4, *first = lax.optimization_barrier((r4, l4, *first))
    r5 = zhop(r4[:64], 1)
    l5 = zhop(l4[128:], -1)
    v = squares
    started = start_sum(first[1], first[2])
    chunk1 = gram_all_reduce(*started, *first[3:]) + (first[0],)
    r5, l5, *_ = lax.optimization_barrier((r5, l5, *started))
    second = gram(
        y,
        tiles,
        [r3, l3, r4, l4, r5, l5],
        [
            [[(0, 128, 128)], [(2, 0, 128)]],
            [[(1, 0, 128)], [(3, 64, 128)]],
            [[(2, 128, 64), (3, 0, 64)], [(4, 0, 64), (5, 0, 64)]],
        ],
    )
    v, chunk2 = gram_all_reduce(*start_sum(*second[1:3]), *second[3:], v)
    chunk2 = chunk2 + (second[0],)

    arrived = sib(product(y, 1, [chunk1, chunk2]))
    mine = product(y, 0, [chunk1, chunk2])
    total = mine.astype(F32) + arrived.astype(F32)
    t_own, t_far = total[0, :512], total[0, 512:].astype(BF16)
    t_in, t_out = total[1, :512], total[1, 512:]
    a1 = inner(t_far[:256])
    b1 = outer(t_far[256:])
    v, a1, b1 = together([("row", 4)], v, a1, b1)
    to_out = jnp.concatenate([add(t_out[:256], a1), t_out[256:]], 0).astype(BF16)
    to_in = jnp.concatenate([t_in[:256], add(t_in[256:], b1)], 0).astype(BF16)
    from_in, from_out = inner(to_in), outer(to_out)
    v, from_in, from_out = together([("row", 8)], v, from_in, from_out)
    prod = add(t_own, from_in, from_out)

    total_sq = jnp.sum(v)
    gain = math.sqrt(M) / (1.5 * (jnp.sqrt(total_sq) + EPSILON))
    update = math.sqrt(M) * (
        (1.5 * gain) * nesterov - (0.5 * gain * gain * gain) * prod
    )
    return (new_momentum, update)


def solution(mesh):
    placed = (P("depth", "row", "col"), P("depth", "row", "col"), P("row", ("col", "depth")))
    return jax.shard_map(
        body,
        mesh=mesh,
        in_specs=placed,
        out_specs=(P("row", ("col", "depth")), P("row", ("col", "depth"))),
        check_vma=False,
    )
```

```python
import functools
import math

import jax
import jax.numpy as jnp
from jax import lax
from jax.experimental import pallas as pl
from jax.experimental.pallas import tpu as pltpu
from jax.sharding import PartitionSpec as P

M = 8192
BETA = 0.95
EPSILON = 1e-07
F32 = jnp.float32
BF16 = jnp.bfloat16

NY = 4
TILE = 512
PIECE = 128
ZPERM = {s: [(r, (r + 2 * s) % 16) for r in range(16)] for s in (1, -1)}
YPERM = {s: [(y, (y + s) % 4) for y in range(4)] for s in (1, -1)}
SIB = [(d, d ^ 1) for d in range(4)]
INNER = [(d, d ^ 2) for d in range(4)]
OUTER = [(r * 4 + d, (r ^ 1) * 4 + (d ^ 2)) for r in range(16) for d in range(4)]


def sib(v):
    return lax.ppermute(v, "depth", SIB)


def inner(v):
    return lax.ppermute(v, "depth", INNER)


def outer(v):
    return lax.ppermute(v, ("row", "depth"), OUTER)


def zhop(v, s):
    return lax.ppermute(v, "row", ZPERM[s])


def yhop(v, s):
    return lax.ppermute(v, "col", YPERM[s])


def swap_add(v, axis, bit):
    return v + lax.ppermute(v, axis, [(i, i ^ bit) for i in range(lax.axis_size(axis))])


def add(*vs):
    total = vs[0].astype(F32)
    for v in vs[1:]:
        total = total + v.astype(F32)
    return total


VMEM = pl.BlockSpec(memory_space=pltpu.VMEM)
SMEM = pl.BlockSpec(memory_space=pltpu.SMEM)


def gram_kernel(sources, y_ref, *refs):
    n_in = 8 + max(i for piece in sources for _, parts in enumerate(piece) for i, _, _ in parts) + 1
    tiles, parts_in = refs[:8], refs[8:n_in]
    joined, far0, far1, right, left, own, held = refs[n_in:]
    for p, piece in enumerate(sources):
        for half, parts in enumerate(piece):
            row = p * PIECE
            for i, start, size in parts:
                joined[row : row + size, half * 1024 : half * 1024 + 1024] = parts_in[i][
                    start : start + size, :
                ]
                row += size
    y = y_ref[0]
    for block in range(4):
        line, start = block // 2, (block % 2) * 256
        total = None
        for k in range(4):
            term = lax.dot_general(
                tiles[line * 4 + k][start : start + 256, :],
                joined[:, k * TILE : (k + 1) * TILE],
                (((1,), (1,)), ((), ())),
                preferred_element_type=F32,
            )
            total = term if total is None else total + term
        held[lax.rem(block + 4 - y, 4)] = total.astype(BF16)
    own[...] = held[0]
    right[...] = held[1]
    far0[...] = held[2, :128]
    far1[...] = held[2, 128:]
    left[...] = held[3]


def gram(y, tiles, arrays, sources):
    n = len(sources) * PIECE
    shapes = [(n, 2048), (128, n), (128, n), (256, n), (256, n), (256, n)]
    return pl.pallas_call(
        functools.partial(gram_kernel, sources),
        out_shape=[jax.ShapeDtypeStruct(s, BF16) for s in shapes],
        in_specs=[SMEM] + [VMEM] * (8 + len(arrays)),
        out_specs=[VMEM] * 6,
        scratch_shapes=[pltpu.VMEM((4, 256, n), BF16)],
        compiler_params=pltpu.CompilerParams(vmem_limit_bytes=16 << 20),
        cost_estimate=pl.CostEstimate(
            flops=2 * 1024 * 2048 * n, bytes_accessed=8 << 20, transcendentals=0
        ),
    )(y, *tiles, *arrays)


def far_kernel(widths, y_ref, *refs):
    far, whole, theirs, mine = refs[-4:]
    y = y_ref[0]
    at = 0
    for chunk, width in enumerate(widths):
        own, r3, l3, r4, l4, joined = refs[chunk * 6 : chunk * 6 + 6]
        cols = slice(at, at + width)

        def rows(k):
            return pl.multiple_of(lax.rem(y + k, 4) * 256, 256)

        for k, part in ((0, own), (1, l3), (3, r3)):
            whole[pl.ds(rows(k), 256), cols] = part[...]
        whole[pl.ds(rows(2), 128), cols] = r4[...]
        whole[pl.ds(rows(2) + 128, 128), cols] = l4[...]
        for half in range(2):
            start = half * 1024
            mine[half, cols, :] = joined[:, start : start + TILE]
            theirs[half, cols, :] = joined[:, start + TILE : start + 2 * TILE]
        at += width
    far[...] = jnp.dot(whole[512:], theirs[0], preferred_element_type=F32).astype(BF16)


def rest_kernel(whole, theirs, own, near, out):
    own[...] = jnp.dot(whole[:512], theirs[0], preferred_element_type=F32).astype(BF16)
    near[...] = jnp.dot(whole[:512], theirs[1], preferred_element_type=F32).astype(BF16)
    out[...] = jnp.dot(whole[512:], theirs[1], preferred_element_type=F32).astype(BF16)


def far_sum_kernel(whole, mine, arrived, upper, lower):
    total = jnp.dot(whole[512:], mine[0], preferred_element_type=F32) + arrived[...].astype(F32)
    upper[...] = total[:256].astype(BF16)
    lower[...] = total[256:].astype(BF16)


def rest_sum_kernel(whole, mine, a_own, a_near, a_out, own, near, out):
    def term(rows, half, arrived):
        return jnp.dot(whole[rows], mine[half], preferred_element_type=F32) + arrived[...].astype(F32)

    own[...] = term(slice(0, 512), 0, a_own)
    near[...] = term(slice(0, 512), 1, a_near).astype(BF16)
    out[...] = term(slice(512, 1024), 1, a_out).astype(BF16)


def call(kernel, operands, shapes, flops, limit=16, name=None):
    return pl.pallas_call(
        kernel,
        out_shape=[jax.ShapeDtypeStruct(*s) for s in shapes],
        in_specs=[SMEM if v.dtype == jnp.int32 else VMEM for v in operands],
        out_specs=[VMEM] * len(shapes),
        compiler_params=pltpu.CompilerParams(vmem_limit_bytes=limit << 20),
        cost_estimate=pl.CostEstimate(flops=flops, bytes_accessed=4 << 20, transcendentals=0),
        name=name,
    )(*operands)


def send_kernel(at_ref, q_ref, s_ref, out_ref, *, first):
    for r in range(2):
        rows = slice(r * 128, r * 128 + 128)
        scale = s_ref[0, first + r : first + r + 1, :]
        out_ref[0, rows, :] = (q_ref[0, rows, :].astype(F32) * scale).astype(BF16)


def pair_kernel(at_ref, q_send, q_keep, s_send, s_keep, arrived, to_inner, kept, *, first):
    xl = at_ref[1]
    for r in range(2):
        rows = slice(r * 128, r * 128 + 128)
        for q, s, part, out in ((q_send, s_send, 1 - xl, to_inner), (q_keep, s_keep, xl, kept)):
            value = q[0, rows, :].astype(F32) * s[0, first + r : first + r + 1, :]
            out[rows, :] = (value + arrived[part, rows, :].astype(F32)).astype(out.dtype)


def send_part(at, quant, scale, half):
    return pl.pallas_call(
        functools.partial(send_kernel, first=half * 2),
        grid_spec=pltpu.PrefetchScalarGridSpec(
            num_scalar_prefetch=1,
            grid=(2,),
            in_specs=[
                pl.BlockSpec((1, 256, TILE), lambda i, at: (0, half, 2 * i + 1 - at[0])),
                pl.BlockSpec((1, 4, TILE), lambda i, at: (0, 0, 2 * i + 1 - at[0])),
            ],
            out_specs=pl.BlockSpec((1, 256, TILE), lambda i, at: (i, 0, 0)),
        ),
        out_shape=jax.ShapeDtypeStruct((2, 256, TILE), BF16),
        compiler_params=pltpu.CompilerParams(vmem_limit_bytes=8 << 20),
        name="send_part",
    )(at, quant, scale)


def pair_part(at, quant, scale, arrived, half):
    def send(i, at):
        return 2 * (1 - at[1]) + at[0]

    def keep(i, at):
        return 2 * at[1] + at[0]

    return pl.pallas_call(
        functools.partial(pair_kernel, first=half * 2),
        grid_spec=pltpu.PrefetchScalarGridSpec(
            num_scalar_prefetch=1,
            grid=(1,),
            in_specs=[
                pl.BlockSpec((1, 256, TILE), lambda i, at: (0, half, send(i, at))),
                pl.BlockSpec((1, 256, TILE), lambda i, at: (0, half, keep(i, at))),
                pl.BlockSpec((1, 4, TILE), lambda i, at: (0, 0, send(i, at))),
                pl.BlockSpec((1, 4, TILE), lambda i, at: (0, 0, keep(i, at))),
                pl.BlockSpec((2, 256, TILE), lambda i, at: (0, 0, 0)),
            ],
            out_specs=[pl.BlockSpec((256, TILE), lambda i, at: (0, 0))] * 2,
        ),
        out_shape=[
            jax.ShapeDtypeStruct((256, TILE), BF16),
            jax.ShapeDtypeStruct((256, TILE), F32),
        ],
        compiler_params=pltpu.CompilerParams(vmem_limit_bytes=8 << 20),
        name="pair_part",
    )(at, quant, quant, scale, scale, arrived)


def momentum_kernel(kept0, kept1, arrived0, arrived1, momentum, new_ref, tile_ref, squares_ref):
    total = jnp.zeros((8, TILE), F32)
    for half, (kept, arrived) in enumerate(((kept0, arrived0), (kept1, arrived1))):
        rows = slice(half * 256, half * 256 + 256)
        gradient = kept[...] + arrived[...].astype(F32)
        new = BETA * momentum[rows, :] + gradient
        nesterov = gradient + BETA * new
        new_ref[rows, :] = new
        tile_ref[rows, :] = nesterov.astype(BF16)
        total = total + jnp.sum((nesterov * nesterov).reshape(32, 8, TILE), axis=0)
    squares_ref[...] = total[:, :128] + total[:, 128:256] + total[:, 256:384] + total[:, 384:]


def together(steps, v, *arrays):
    for axis, bit in steps:
        v = swap_add(v, axis, bit)
    return lax.optimization_barrier((v, *arrays))


def start_sum(far0, far1):
    return yhop(far0, 1), yhop(far1, -1)


def near_sums(r1, l1, right, left):
    right = jnp.concatenate([add(right[:128], r1).astype(BF16), right[128:]], 0)
    left = jnp.concatenate([left[:128], add(left[128:], l1).astype(BF16)], 0)
    return right, left


def finish_sum(right, left, own, v=None):
    r2, l2 = yhop(right, 1), yhop(left, -1)
    if v is not None:
        v, r2, l2 = together([("depth", 2)], v, r2, l2)
    own = add(own, r2, l2).astype(BF16)
    r3, l3 = yhop(own, 1), yhop(own, -1)
    if v is not None:
        v, r3, l3 = together([("row", 1)], v, r3, l3)
    return v, (own, r3, l3, yhop(r3[:128], 1), yhop(l3[128:], -1))


def body(grad_partial, grad_scale, momentum):
    y = lax.axis_index("col").astype(jnp.int32).reshape(1)
    depth = lax.axis_index("depth").astype(jnp.int32)
    xl, c = depth // 2, depth % 2
    at = jnp.stack([c, xl])
    arrived = [sib(send_part(at, grad_partial, grad_scale, h)) for h in range(2)]
    pairs = [pair_part(at, grad_partial, grad_scale, arrived[h], h) for h in range(2)]
    arrived = [inner(p[0]) for p in pairs]
    new_momentum, tile, v = call(
        momentum_kernel,
        [pairs[0][1], pairs[1][1], *arrived, momentum],
        [((TILE, TILE), F32), ((TILE, TILE), BF16), ((8, 128), F32)],
        1 << 20,
        name="momentum",
    )

    tile_s = sib(tile)

    def rows_of(half):
        start = (half * 2 + c) * PIECE
        return jnp.concatenate(
            [lax.dynamic_slice_in_dim(t, start, PIECE, 0) for t in (tile, tile_s)], axis=1
        )

    a = rows_of(xl)
    b = inner(rows_of(1 - xl))
    ra, la = zhop(a, 1), zhop(a, -1)
    t_out = outer(tile)
    v, b = together([("depth", 1)], v, b)
    r2 = zhop(jnp.concatenate([b, ra], axis=0), 1)
    l2 = zhop(jnp.concatenate([la, b], axis=0), -1)
    t_in = inner(lax.optimization_barrier((tile, b))[0])
    v, t_in, t_out = together([("col", 1)], v, t_in, t_out)
    t_in, t_out, t_in_s, t_out_s = lax.optimization_barrier((t_in, t_out, sib(t_in), sib(t_out)))
    far_a, far_b = outer(t_in[:256]), inner(t_out[256:])
    v, r2, l2 = together([("col", 2)], v, r2, l2)
    r3, l3 = zhop(r2, 1), zhop(l2, -1)
    far_a, far_b, r2, l2 = lax.optimization_barrier((far_a, far_b, r2, l2))
    t_far = jnp.concatenate([far_a, far_b], axis=0)
    tiles = [tile, tile_s, t_in, t_in_s, t_far, sib(t_far), t_out, t_out_s]
    r4, l4 = zhop(r3[:192], 1), zhop(l3[64:], -1)
    first = gram(
        y,
        tiles,
        [a, b, ra, la, r2, l2, r3, l3],
        [
            [[(0, 0, 128)], [(1, 0, 128)]],
            [[(2, 0, 128)], [(4, 0, 128)]],
            [[(3, 0, 128)], [(5, 128, 128)]],
            [[(4, 128, 128)], [(6, 0, 128)]],
            [[(5, 0, 128)], [(7, 128, 128)]],
        ],
    )
    r4, l4, *first = lax.optimization_barrier((r4, l4, *first))
    r5, l5 = zhop(r4[:64], 1), zhop(l4[128:], -1)
    r1, l1 = start_sum(first[1], first[2])
    right, left = near_sums(r1, l1, first[3], first[4])
    r5, l5, right, left = lax.optimization_barrier((r5, l5, right, left))
    second = gram(
        y,
        tiles,
        [r3, l3, r4, l4, r5, l5],
        [
            [[(0, 128, 128)], [(2, 0, 128)]],
            [[(1, 0, 128)], [(3, 64, 128)]],
            [[(2, 128, 64), (3, 0, 64)], [(4, 0, 64), (5, 0, 64)]],
        ],
    )
    _, chunk1 = finish_sum(right, left, first[5])
    r1, l1 = start_sum(second[1], second[2])
    right, left = near_sums(r1, l1, second[3], second[4])
    v, chunk2 = finish_sum(right, left, second[5], v)

    far, whole, theirs, mine = call(
        functools.partial(far_kernel, [640, 384]),
        [y, *chunk1, first[0], *chunk2, second[0]],
        [((TILE, TILE), BF16), ((1024, 1024), BF16)] + [((2, 1024, TILE), BF16)] * 2,
        1 << 29,
        name="far",
    )
    far = sib(far)
    rest = call(rest_kernel, [whole, theirs], [((TILE, TILE), BF16)] * 3, 3 << 29, name="rest")
    rest = [sib(t) for t in rest]
    upper, lower = call(
        far_sum_kernel, [whole, mine, far], [((256, TILE), BF16)] * 2, 1 << 29, name="far_sum"
    )
    a1, b1 = inner(upper), outer(lower)
    t_own, t_in, t_out = call(
        rest_sum_kernel,
        [whole, mine, *rest],
        [((TILE, TILE), F32)] + [((TILE, TILE), BF16)] * 2,
        3 << 29,
        name="rest_sum",
    )
    v, a1, b1 = together([("row", 2), ("row", 4)], v, a1, b1)
    to_out = jnp.concatenate([add(t_out[:256], a1).astype(BF16), t_out[256:]], 0)
    to_in = jnp.concatenate([t_in[:256], add(t_in[256:], b1).astype(BF16)], 0)
    from_in, from_out = inner(to_in), outer(to_out)
    v, from_in, from_out = together([("row", 8)], v, from_in, from_out)
    prod = add(t_own, from_in, from_out)

    gain = math.sqrt(M) / (1.5 * (jnp.sqrt(jnp.sum(v)) + EPSILON))
    update = math.sqrt(M) * (
        (1.5 * gain) * tile.astype(F32) - (0.5 * gain * gain * gain) * prod
    )
    return (new_momentum, update)


def solution(mesh):
    placed = (P("depth", "row", "col"), P("depth", "row", "col"), P("row", ("col", "depth")))
    return jax.shard_map(
        body,
        mesh=mesh,
        in_specs=placed,
        out_specs=(P("row", ("col", "depth")), P("row", ("col", "depth"))),
        check_vma=False,
    )
```

```python
import functools
import math

import jax
import jax.numpy as jnp
from jax import lax
from jax.experimental import pallas as pl
from jax.experimental.pallas import tpu as pltpu
from jax.sharding import PartitionSpec as P

M = 8192
BETA = 0.95
EPSILON = 1e-07
F32 = jnp.float32
BF16 = jnp.bfloat16

NY = 4
TILE = 512
PIECE = 128
ZPERM = {s: [(r, (r + 2 * s) % 16) for r in range(16)] for s in (1, -1)}
YPERM = {s: [(y, (y + s) % 4) for y in range(4)] for s in (1, -1)}
SIB = [(d, d ^ 1) for d in range(4)]
INNER = [(d, d ^ 2) for d in range(4)]
OUTER = [(r * 4 + d, (r ^ 1) * 4 + (d ^ 2)) for r in range(16) for d in range(4)]


def sib(v):
    return lax.ppermute(v, "depth", SIB)


def inner(v):
    return lax.ppermute(v, "depth", INNER)


def outer(v):
    return lax.ppermute(v, ("row", "depth"), OUTER)


def zhop(v, s):
    return lax.ppermute(v, "row", ZPERM[s])


def yhop(v, s):
    return lax.ppermute(v, "col", YPERM[s])


def swap_add(v, axis, bit):
    return v + lax.ppermute(v, axis, [(i, i ^ bit) for i in range(lax.axis_size(axis))])


def add(*vs):
    total = vs[0].astype(F32)
    for v in vs[1:]:
        total = total + v.astype(F32)
    return total


VMEM = pl.BlockSpec(memory_space=pltpu.VMEM)
SMEM = pl.BlockSpec(memory_space=pltpu.SMEM)


def gram_kernel(sources, y_ref, *refs):
    n_in = 8 + max(i for piece in sources for parts in piece for i, _, _ in parts) + 1
    tiles, parts_in = refs[:8], refs[8:n_in]
    joined, far0, far1, right, left, own, held, panel, sems = refs[n_in:]
    copies = []

    def copy(source, target):
        copies.append(pltpu.make_async_copy(source, target, sems.at[len(copies)]))
        copies[-1].start()

    for p, piece in enumerate(sources):
        for half, parts in enumerate(piece):
            row = p * PIECE
            for i, start, size in parts:
                copy(
                    parts_in[i].at[pl.ds(start, size)],
                    joined.at[pl.ds(row, size), pl.ds(half * 1024, 1024)],
                )
                row += size
    n_parts = len(copies)
    for i, tile in enumerate(tiles):
        copy(tile, panel.at[pl.ds(i // 4 * TILE, TILE), pl.ds(i % 4 * TILE, TILE)])
    y = y_ref[0]
    for c in copies[: n_parts + 4]:
        c.wait()
    for block in range(4):
        if block == 2:
            for c in copies[n_parts + 4 :]:
                c.wait()
        total = lax.dot_general(
            panel[block * 256 : block * 256 + 256, :],
            joined[...],
            (((1,), (1,)), ((), ())),
            preferred_element_type=F32,
        )
        held[lax.rem(block + 4 - y, 4)] = total.astype(BF16)
    own[...] = held[0]
    right[...] = held[1]
    far0[...] = held[2, :128]
    far1[...] = held[2, 128:]
    left[...] = held[3]


def gram(y, tiles, arrays, sources):
    n = len(sources) * PIECE
    shapes = [(n, 2048), (128, n), (128, n), (256, n), (256, n), (256, n)]
    n_copies = 8 + sum(len(parts) for piece in sources for parts in piece)
    return pl.pallas_call(
        functools.partial(gram_kernel, sources),
        out_shape=[jax.ShapeDtypeStruct(s, BF16) for s in shapes],
        in_specs=[SMEM] + [pl.BlockSpec(memory_space=pl.ANY)] * (8 + len(arrays)),
        out_specs=[VMEM] * 6,
        scratch_shapes=[
            pltpu.VMEM((4, 256, n), BF16),
            pltpu.VMEM((1024, 2048), BF16),
            pltpu.SemaphoreType.DMA((n_copies,)),
        ],
        compiler_params=pltpu.CompilerParams(vmem_limit_bytes=16 << 20),
        cost_estimate=pl.CostEstimate(
            flops=2 * 1024 * 2048 * n, bytes_accessed=8 << 20, transcendentals=0
        ),
        name="gram",
    )(y, *tiles, *arrays)


def far_kernel(widths, y_ref, *refs):
    far, whole, theirs, mine = refs[-4:]
    y = y_ref[0]
    at = 0
    for chunk, width in enumerate(widths):
        own, r3, l3, r4, l4, joined = refs[chunk * 6 : chunk * 6 + 6]
        cols = slice(at, at + width)

        def rows(k):
            return pl.multiple_of(lax.rem(y + k, 4) * 256, 256)

        for k, part in ((0, own), (1, l3), (3, r3)):
            whole[pl.ds(rows(k), 256), cols] = part[...]
        whole[pl.ds(rows(2), 128), cols] = r4[...]
        whole[pl.ds(rows(2) + 128, 128), cols] = l4[...]
        for half in range(2):
            start = half * 1024
            mine[half, cols, :] = joined[:, start : start + TILE]
            theirs[half, cols, :] = joined[:, start + TILE : start + 2 * TILE]
        at += width
    far[...] = jnp.dot(whole[512:], theirs[0], preferred_element_type=F32).astype(BF16)


def rest_kernel(whole, theirs, own, near, out):
    own[...] = jnp.dot(whole[:512], theirs[0], preferred_element_type=F32).astype(BF16)
    near[...] = jnp.dot(whole[:512], theirs[1], preferred_element_type=F32).astype(BF16)
    out[...] = jnp.dot(whole[512:], theirs[1], preferred_element_type=F32).astype(BF16)


def far_sum_kernel(whole, mine, arrived, upper, lower):
    total = jnp.dot(whole[512:], mine[0], preferred_element_type=F32) + arrived[...].astype(F32)
    upper[...] = total[:256].astype(BF16)
    lower[...] = total[256:].astype(BF16)


def rest_sum_kernel(whole, mine, a_own, a_near, a_out, own, near, out):
    def term(rows, half, arrived):
        return jnp.dot(whole[rows], mine[half], preferred_element_type=F32) + arrived[...].astype(F32)

    own[...] = term(slice(0, 512), 0, a_own)
    near[...] = term(slice(0, 512), 1, a_near).astype(BF16)
    out[...] = term(slice(512, 1024), 1, a_out).astype(BF16)


def call(kernel, operands, shapes, flops, limit=16, name=None):
    return pl.pallas_call(
        kernel,
        out_shape=[jax.ShapeDtypeStruct(*s) for s in shapes],
        in_specs=[SMEM if v.dtype == jnp.int32 else VMEM for v in operands],
        out_specs=[VMEM] * len(shapes),
        compiler_params=pltpu.CompilerParams(vmem_limit_bytes=limit << 20),
        cost_estimate=pl.CostEstimate(flops=flops, bytes_accessed=4 << 20, transcendentals=0),
        name=name,
    )(*operands)


def scaled_kernel(at_ref, q_send, q_keep, s_send, s_keep, send0, send1, keep):
    step = pl.program_id(0)
    for r in range(2):
        rows = slice(r * 128, r * 128 + 128)

        def value(q, s):
            scale = jnp.where(step < 2, s[0, r : r + 1, :], s[0, 2 + r : 3 + r, :])
            return q[0, rows, :].astype(F32) * scale

        keep[0, rows, :] = value(q_keep, s_keep)
        sent = value(q_send, s_send).astype(BF16)

        @pl.when(step < 2)
        def _():
            send0[0, rows, :] = sent

        @pl.when(step >= 2)
        def _():
            send1[0, rows, :] = sent


def scaled_parts(at, quant, scale):
    def q_spec(column):
        return pl.BlockSpec((1, 256, TILE), lambda i, at: (0, i // 2, 2 * (i % 2) + column(at)))

    def s_spec(column):
        return pl.BlockSpec((1, 4, TILE), lambda i, at: (0, 0, 2 * (i % 2) + column(at)))

    def theirs(at):
        return 1 - at[0]

    def mine(at):
        return at[0]

    return pl.pallas_call(
        scaled_kernel,
        grid_spec=pltpu.PrefetchScalarGridSpec(
            num_scalar_prefetch=1,
            grid=(4,),
            in_specs=[q_spec(theirs), q_spec(mine), s_spec(theirs), s_spec(mine)],
            out_specs=[
                pl.BlockSpec((1, 256, TILE), lambda i, at: (jnp.minimum(i, 1), 0, 0)),
                pl.BlockSpec((1, 256, TILE), lambda i, at: (jnp.maximum(i - 2, 0), 0, 0)),
                pl.BlockSpec((1, 256, TILE), lambda i, at: (i, 0, 0)),
            ],
        ),
        out_shape=[
            jax.ShapeDtypeStruct((2, 256, TILE), BF16),
            jax.ShapeDtypeStruct((2, 256, TILE), BF16),
            jax.ShapeDtypeStruct((4, 256, TILE), F32),
        ],
        compiler_params=pltpu.CompilerParams(vmem_limit_bytes=16 << 20),
        name="scaled",
    )(at, quant, quant, scale, scale)


def pair_kernel(half, at_ref, keep, arrived, to_inner, kept):
    xl = at_ref[1]
    to_inner[...] = (keep[2 * half + 1 - xl] + arrived[1 - xl].astype(F32)).astype(BF16)
    kept[...] = keep[2 * half + xl] + arrived[xl].astype(F32)


def momentum_kernel(kept0, kept1, arrived0, arrived1, momentum, new_ref, tile_ref, squares_ref):
    total = jnp.zeros((8, TILE), F32)
    for half, (kept, arrived) in enumerate(((kept0, arrived0), (kept1, arrived1))):
        rows = slice(half * 256, half * 256 + 256)
        gradient = kept[...] + arrived[...].astype(F32)
        new = BETA * momentum[rows, :] + gradient
        nesterov = gradient + BETA * new
        new_ref[rows, :] = new
        tile_ref[rows, :] = nesterov.astype(BF16)
        total = total + jnp.sum((nesterov * nesterov).reshape(32, 8, TILE), axis=0)
    squares_ref[...] = total[:, :128] + total[:, 128:256] + total[:, 256:384] + total[:, 384:]


def together(steps, v, *arrays):
    for axis, bit in steps:
        v = swap_add(v, axis, bit)
    return lax.optimization_barrier((v, *arrays))


def start_sum(far0, far1):
    return yhop(far0, 1), yhop(far1, -1)


def near_sums(r1, l1, right, left):
    right = jnp.concatenate([add(right[:128], r1).astype(BF16), right[128:]], 0)
    left = jnp.concatenate([left[:128], add(left[128:], l1).astype(BF16)], 0)
    return right, left


def second_step(right, left, own, v=None):
    if v is not None:
        v, right, left = lax.optimization_barrier((v, right, left))
    r2, l2 = yhop(right, 1), yhop(left, -1)
    if v is not None:
        v, r2, l2 = together([("depth", 2)], v, r2, l2)
    return add(own, r2, l2).astype(BF16), v


def gather_near(own, v=None):
    if v is not None:
        v, own = lax.optimization_barrier((v, own))
    r3, l3 = yhop(own, 1), yhop(own, -1)
    if v is not None:
        v, r3, l3 = together([("row", 1)], v, r3, l3)
    return own, r3, l3, v


def gather_far(own, r3, l3, v=None):
    r4, l4 = yhop(r3[:128], 1), yhop(l3[128:], -1)
    if v is not None:
        v, r4, l4 = together([("row", 2)], v, r4, l4)
    return (own, r3, l3, r4, l4), v


def body(grad_partial, grad_scale, momentum):
    y = lax.axis_index("col").astype(jnp.int32).reshape(1)
    depth = lax.axis_index("depth").astype(jnp.int32)
    xl, c = depth // 2, depth % 2
    at = jnp.stack([c, xl])
    send0, send1, keep = scaled_parts(at, grad_partial, grad_scale)
    arrived = [sib(send0), sib(send1)]
    pairs = [
        call(
            functools.partial(pair_kernel, h),
            [at, keep, arrived[h]],
            [((256, TILE), BF16), ((256, TILE), F32)],
            1 << 20,
            name="pair",
        )
        for h in range(2)
    ]
    arrived = [inner(p[0]) for p in pairs]
    new_momentum, tile, v = call(
        momentum_kernel,
        [pairs[0][1], pairs[1][1], *arrived, momentum],
        [((TILE, TILE), F32), ((TILE, TILE), BF16), ((8, 128), F32)],
        1 << 20,
        name="momentum",
    )

    tile_s = sib(tile)

    def rows_of(half):
        start = (half * 2 + c) * PIECE
        return jnp.concatenate(
            [lax.dynamic_slice_in_dim(t, start, PIECE, 0) for t in (tile, tile_s)], axis=1
        )

    a = rows_of(xl)
    b = inner(rows_of(1 - xl))
    ra, la = zhop(a, 1), zhop(a, -1)
    t_out = outer(tile)
    v, b = together([("depth", 1)], v, b)
    r2 = zhop(jnp.concatenate([b, ra], axis=0), 1)
    l2 = zhop(jnp.concatenate([la, b], axis=0), -1)
    t_in = inner(lax.optimization_barrier((tile, b))[0])
    v, r2, l2 = together([("col", 1)], v, r2, l2)
    r3, l3 = zhop(r2, 1), zhop(l2, -1)
    t_in, t_out, r2, l2 = lax.optimization_barrier((t_in, t_out, r2, l2))
    far_a, far_b = outer(t_in[:256]), inner(t_out[256:])
    t_in, t_out, far_a, far_b = lax.optimization_barrier((t_in, t_out, far_a, far_b))
    t_far = jnp.concatenate([far_a, far_b], axis=0)
    tiles = [tile, tile_s] + [t for v_ in (t_in, t_far, t_out) for t in (v_, sib(v_))]
    v, r3, l3 = together([("col", 2)], v, r3, l3)
    r4, l4 = zhop(r3[:192], 1), zhop(l3[64:], -1)
    first = gram(
        y,
        tiles,
        [a, b, ra, la, r2, l2, r3, l3],
        [
            [[(0, 0, 128)], [(1, 0, 128)]],
            [[(2, 0, 128)], [(4, 0, 128)]],
            [[(3, 0, 128)], [(5, 128, 128)]],
            [[(4, 128, 128)], [(6, 0, 128)]],
            [[(5, 0, 128)], [(7, 128, 128)]],
        ],
    )
    r4, l4, *first = lax.optimization_barrier((r4, l4, *first))
    r5, l5 = zhop(r4[:64], 1), zhop(l4[128:], -1)
    r1, l1 = start_sum(first[1], first[2])
    right, left = near_sums(r1, l1, first[3], first[4])
    r5, l5, right, left = lax.optimization_barrier((r5, l5, right, left))
    second = gram(
        y,
        tiles,
        [r3, l3, r4, l4, r5, l5],
        [
            [[(0, 128, 128)], [(2, 0, 128)]],
            [[(1, 0, 128)], [(3, 64, 128)]],
            [[(2, 128, 64), (3, 0, 64)], [(4, 0, 64), (5, 0, 64)]],
        ],
    )
    own, _ = second_step(right, left, first[5])
    own, far0, far1 = lax.optimization_barrier((own, second[1], second[2]))
    own, r3, l3, _ = gather_near(own)
    right, left = near_sums(*start_sum(far0, far1), second[3], second[4])
    r3, l3, right, left = lax.optimization_barrier((r3, l3, right, left))
    chunk1, _ = gather_far(own, r3, l3)
    own, v = second_step(right, left, second[5], v)
    own, *chunk1 = lax.optimization_barrier((own, *chunk1))
    chunk2, v = gather_far(*gather_near(own, v))

    far, whole, theirs, mine = call(
        functools.partial(far_kernel, [640, 384]),
        [y, *chunk1, first[0], *chunk2, second[0]],
        [((TILE, TILE), BF16), ((1024, 1024), BF16)] + [((2, 1024, TILE), BF16)] * 2,
        1 << 29,
        name="far",
    )
    far = sib(far)
    rest = call(rest_kernel, [whole, theirs], [((TILE, TILE), BF16)] * 3, 3 << 29, name="rest")
    rest = [sib(t) for t in rest]
    upper, lower = call(
        far_sum_kernel, [whole, mine, far], [((256, TILE), BF16)] * 2, 1 << 29, name="far_sum"
    )
    v, upper, lower = lax.optimization_barrier((v, upper, lower))
    a1, b1 = inner(upper), outer(lower)
    t_own, t_in, t_out = call(
        rest_sum_kernel,
        [whole, mine, *rest],
        [((TILE, TILE), F32)] + [((TILE, TILE), BF16)] * 2,
        3 << 29,
        name="rest_sum",
    )
    v, a1, b1 = together([("row", 4)], v, a1, b1)
    to_out = jnp.concatenate([add(t_out[:256], a1).astype(BF16), t_out[256:]], 0)
    to_in = jnp.concatenate([t_in[:256], add(t_in[256:], b1).astype(BF16)], 0)
    v, to_in, to_out = lax.optimization_barrier((v, to_in, to_out))
    from_in, from_out = inner(to_in), outer(to_out)
    v, from_in, from_out = together([("row", 8)], v, from_in, from_out)
    prod = add(t_own, from_in, from_out)

    gain = math.sqrt(M) / (1.5 * (jnp.sqrt(jnp.sum(v)) + EPSILON))
    update = math.sqrt(M) * (
        (1.5 * gain) * tile.astype(F32) - (0.5 * gain * gain * gain) * prod
    )
    return (new_momentum, update)


def solution(mesh):
    placed = (P("depth", "row", "col"), P("depth", "row", "col"), P("row", ("col", "depth")))
    return jax.shard_map(
        body,
        mesh=mesh,
        in_specs=placed,
        out_specs=(P("row", ("col", "depth")), P("row", ("col", "depth"))),
        check_vma=False,
    )
```

```python
import functools
import math

import jax
import jax.numpy as jnp
from jax import lax
from jax.experimental import pallas as pl
from jax.experimental.pallas import tpu as pltpu
from jax.sharding import PartitionSpec as P

M = 8192
BETA = 0.95
EPSILON = 1e-07
F32 = jnp.float32
BF16 = jnp.bfloat16

NY = 4
TILE = 512
PIECE = 128
ZPERM = {s: [(r, (r + 2 * s) % 16) for r in range(16)] for s in (1, -1)}
YPERM = {s: [(y, (y + s) % 4) for y in range(4)] for s in (1, -1)}
SIB = [(d, d ^ 1) for d in range(4)]
INNER = [(d, d ^ 2) for d in range(4)]
OUTER = [(r * 4 + d, (r ^ 1) * 4 + (d ^ 2)) for r in range(16) for d in range(4)]


def sib(v):
    return lax.ppermute(v, "depth", SIB)


def inner(v):
    return lax.ppermute(v, "depth", INNER)


def outer(v):
    return lax.ppermute(v, ("row", "depth"), OUTER)


def across(v):
    return lax.ppermute(v, "row", [(r, r ^ 1) for r in range(16)])


def zhop(v, s):
    return lax.ppermute(v, "row", ZPERM[s])


def yhop(v, s):
    return lax.ppermute(v, "col", YPERM[s])


def swap_add(v, axis, bit):
    return v + lax.ppermute(v, axis, [(i, i ^ bit) for i in range(lax.axis_size(axis))])


def add(*vs):
    total = vs[0].astype(F32)
    for v in vs[1:]:
        total = total + v.astype(F32)
    return total


VMEM = pl.BlockSpec(memory_space=pltpu.VMEM)
SMEM = pl.BlockSpec(memory_space=pltpu.SMEM)
HBM = pl.BlockSpec(memory_space=pltpu.HBM)
ANY = pl.BlockSpec(memory_space=pl.ANY)


def gram_rows(sources, tiles, parts_in, joined, panel, sems, finish):
    copies = []

    def copy(source, target):
        copies.append(pltpu.make_async_copy(source, target, sems.at[len(copies)]))
        copies[-1].start()

    for p, piece in enumerate(sources):
        for half, parts in enumerate(piece):
            row = p * PIECE
            for i, start, size in parts:
                copy(
                    parts_in[i].at[pl.ds(start, size)],
                    joined.at[pl.ds(row, size), pl.ds(half * 1024, 1024)],
                )
                row += size
    n_parts = len(copies)
    for i, tile in enumerate(tiles):
        copy(tile, panel.at[pl.ds(i // 4 * TILE, TILE), pl.ds(i % 4 * TILE, TILE)])
    for c in copies[: n_parts + 4]:
        c.wait()
    for block in range(4):
        if block == 2:
            for c in copies[n_parts + 4 :]:
                c.wait()
        total = lax.dot_general(
            panel[block * 256 : block * 256 + 256, :],
            joined[...],
            (((1,), (1,)), ((), ())),
            preferred_element_type=F32,
        )
        finish(block, total.astype(BF16))


def first_kernel(sources, *refs):
    tiles, parts = refs[:8], refs[8:-4]
    joined, held, panel, sems = refs[-4:]

    def finish(block, total):
        held[block] = total

    gram_rows(sources, tiles, parts, joined, panel, sems, finish)


def last_kernel(sources, y_ref, held, *refs):
    tiles, parts = refs[:8], refs[8:-9]
    joined, far0, far1, right, left, own, last, panel, sems = refs[-9:]

    def finish(block, total):
        last[block] = total

    gram_rows(sources, tiles, parts, joined, panel, sems, finish)
    y = y_ref[0]
    wide = held.shape[2]
    for k, out in ((0, own), (1, right), (3, left)):
        block = lax.rem(y + k, 4)
        out[:, :wide] = held[block]
        out[:, wide:] = last[block]
    block = lax.rem(y + 2, 4)
    for out, rows in ((far0, slice(0, 128)), (far1, slice(128, 256))):
        out[:, :wide] = held[block, rows, :]
        out[:, wide:] = last[block, rows, :]


def gram_call(kernel, extra, extra_specs, tiles, arrays, specs, n, n_copies, shapes, scratch, name):
    return pl.pallas_call(
        kernel,
        out_shape=[jax.ShapeDtypeStruct(s, BF16) for s in shapes],
        in_specs=extra_specs + [ANY] * 8 + specs,
        out_specs=[VMEM] * len(shapes),
        scratch_shapes=scratch
        + [pltpu.VMEM((1024, 2048), BF16), pltpu.SemaphoreType.DMA((n_copies,))],
        compiler_params=pltpu.CompilerParams(vmem_limit_bytes=24 << 20),
        cost_estimate=pl.CostEstimate(
            flops=2 * 1024 * 2048 * n, bytes_accessed=8 << 20, transcendentals=0
        ),
        name=name,
    )(*extra, *tiles, *arrays)


def count(sources):
    return 8 + sum(len(parts) for piece in sources for parts in piece)


def gram_first(tiles, arrays, specs, sources):
    n = len(sources) * PIECE
    return gram_call(
        functools.partial(first_kernel, sources), [], [], tiles, arrays, specs, n, count(sources),
        [(n, 2048), (4, 256, n)], [], "gram_first",
    )


def gram_last(y, held, tiles, arrays, sources):
    n = len(sources) * PIECE
    w = held.shape[2] + n
    return gram_call(
        functools.partial(last_kernel, sources), [y, held], [SMEM, VMEM], tiles, arrays,
        [ANY] * len(arrays), n, count(sources),
        [(n, 2048), (128, w), (128, w), (256, w), (256, w), (256, w)],
        [pltpu.VMEM((4, 256, n), BF16)], "gram_last",
    )


def far_kernel(y_ref, own, r3, l3, r4, l4, joined0, joined1, far, whole, theirs, mine):
    y = y_ref[0]

    def rows(k):
        return pl.multiple_of(lax.rem(y + k, 4) * 256, 256)

    for k, part in ((0, own), (1, l3), (3, r3)):
        whole[pl.ds(rows(k), 256), :] = part[...]
    whole[pl.ds(rows(2), 128), :] = r4[...]
    whole[pl.ds(rows(2) + 128, 128), :] = l4[...]
    at = 0
    for joined in (joined0, joined1):
        size = joined.shape[0]
        for half in range(2):
            start = half * 1024
            mine[half, at : at + size, :] = joined[:, start : start + TILE]
            theirs[half, at : at + size, :] = joined[:, start + TILE : start + 2 * TILE]
        at += size
    far[...] = jnp.dot(whole[512:], theirs[0], preferred_element_type=F32).astype(BF16)


def rest_kernel(whole, theirs, own, near, out):
    own[...] = jnp.dot(whole[:512], theirs[0], preferred_element_type=F32).astype(BF16)
    near[...] = jnp.dot(whole[:512], theirs[1], preferred_element_type=F32).astype(BF16)
    out[...] = jnp.dot(whole[512:], theirs[1], preferred_element_type=F32).astype(BF16)


def far_sum_kernel(whole, mine, arrived, upper, lower):
    total = jnp.dot(whole[512:], mine[0], preferred_element_type=F32) + arrived[...].astype(F32)
    upper[...] = total[:256].astype(BF16)
    lower[...] = total[256:].astype(BF16)


def rest_sum_kernel(whole, mine, a_own, a_near, a_out, own, near, out):
    def term(rows, half, arrived):
        return jnp.dot(whole[rows], mine[half], preferred_element_type=F32) + arrived[...].astype(F32)

    own[...] = term(slice(0, 512), 0, a_own)
    near[...] = term(slice(0, 512), 1, a_near).astype(BF16)
    out[...] = term(slice(512, 1024), 1, a_out).astype(BF16)


def call(kernel, operands, shapes, flops, limit=16, name=None):
    return pl.pallas_call(
        kernel,
        out_shape=[jax.ShapeDtypeStruct(*s) for s in shapes],
        in_specs=[SMEM if v.dtype == jnp.int32 else VMEM for v in operands],
        out_specs=[VMEM] * len(shapes),
        compiler_params=pltpu.CompilerParams(vmem_limit_bytes=limit << 20),
        cost_estimate=pl.CostEstimate(flops=flops, bytes_accessed=4 << 20, transcendentals=0),
        name=name,
    )(*operands)


def scaled_kernel(at_ref, q_ref, s_ref, send0, send1, keep, q_buf, s_buf, sems):
    c = at_ref[0]
    scales = pltpu.make_async_copy(s_ref.at[0], s_buf, sems.at[8])
    scales.start()
    copies = []
    for step in range(4):
        for side, core in enumerate((1 - c, c)):
            start = pl.multiple_of((step % 2 * 2 + core) * TILE, TILE)
            copies.append(
                pltpu.make_async_copy(
                    q_ref.at[0, pl.ds(step // 2 * 256, 256), pl.ds(start, TILE)],
                    q_buf.at[2 * step + side],
                    sems.at[2 * step + side],
                )
            )
            copies[-1].start()
    scales.wait()
    for step in range(4):
        for side, core in enumerate((1 - c, c)):
            copies[2 * step + side].wait()
            start = pl.multiple_of((step % 2 * 2 + core) * TILE, TILE)
            for r in range(2):
                rows = slice(r * 128, r * 128 + 128)
                row = step // 2 * 2 + r
                scale = s_buf[row : row + 1, pl.ds(start, TILE)]
                value = q_buf[2 * step + side, rows, :].astype(F32) * scale
                if side:
                    keep[step, rows, :] = value
                else:
                    (send0, send1)[step // 2][step % 2, rows, :] = value.astype(BF16)


def scaled_parts(at, quant, scale):
    return pl.pallas_call(
        scaled_kernel,
        in_specs=[SMEM, HBM, HBM],
        out_specs=[VMEM] * 3,
        out_shape=[
            jax.ShapeDtypeStruct((2, 256, TILE), BF16),
            jax.ShapeDtypeStruct((2, 256, TILE), BF16),
            jax.ShapeDtypeStruct((4, 256, TILE), F32),
        ],
        scratch_shapes=[
            pltpu.VMEM((8, 256, TILE), BF16),
            pltpu.VMEM((4, 4 * TILE), F32),
            pltpu.SemaphoreType.DMA((9,)),
        ],
        compiler_params=pltpu.CompilerParams(vmem_limit_bytes=16 << 20),
        name="scaled",
    )(at, quant, scale)


def pair_kernel(half, at_ref, keep, arrived, to_inner, kept):
    xl = at_ref[1]
    to_inner[...] = (keep[2 * half + 1 - xl] + arrived[1 - xl].astype(F32)).astype(BF16)
    kept[...] = keep[2 * half + xl] + arrived[xl].astype(F32)


def momentum_kernel(kept0, kept1, arrived0, arrived1, momentum, new_ref, tile_ref, squares_ref):
    total = jnp.zeros((8, TILE), F32)
    for half, (kept, arrived) in enumerate(((kept0, arrived0), (kept1, arrived1))):
        rows = slice(half * 256, half * 256 + 256)
        gradient = kept[...] + arrived[...].astype(F32)
        new = BETA * momentum[rows, :] + gradient
        nesterov = gradient + BETA * new
        new_ref[rows, :] = new
        tile_ref[rows, :] = nesterov.astype(BF16)
        total = total + jnp.sum((nesterov * nesterov).reshape(32, 8, TILE), axis=0)
    squares_ref[...] = total[:, :128] + total[:, 128:256] + total[:, 256:384] + total[:, 384:]


def together(steps, v, *arrays):
    for axis, bit in steps:
        v = swap_add(v, axis, bit)
    return lax.optimization_barrier((v, *arrays))


def start_sum(far0, far1):
    return yhop(far0, 1), yhop(far1, -1)


def near_sums(r1, l1, right, left):
    right = jnp.concatenate([add(right[:128], r1).astype(BF16), right[128:]], 0)
    left = jnp.concatenate([left[:128], add(left[128:], l1).astype(BF16)], 0)
    return right, left


def second_step(right, left, own, v=None):
    if v is not None:
        v, right, left = lax.optimization_barrier((v, right, left))
    r2, l2 = yhop(right, 1), yhop(left, -1)
    if v is not None:
        v, r2, l2 = together([("depth", 2)], v, r2, l2)
    return add(own, r2, l2).astype(BF16), v


def gather_near(own, v=None):
    if v is not None:
        v, own = lax.optimization_barrier((v, own))
    r3, l3 = yhop(own, 1), yhop(own, -1)
    if v is not None:
        v, r3, l3 = together([("row", 1)], v, r3, l3)
    return own, r3, l3, v


def gather_far(own, r3, l3, v=None):
    r4, l4 = yhop(r3[:128], 1), yhop(l3[128:], -1)
    if v is not None:
        v, r4, l4 = together([("row", 2)], v, r4, l4)
    return (own, r3, l3, r4, l4), v


def body(grad_partial, grad_scale, momentum):
    y = lax.axis_index("col").astype(jnp.int32).reshape(1)
    depth = lax.axis_index("depth").astype(jnp.int32)
    xl, c = depth // 2, depth % 2
    at = jnp.stack([c, xl])
    send0, send1, keep = scaled_parts(at, grad_partial, grad_scale)
    arrived = [sib(send0), sib(send1)]
    pairs = [
        call(
            functools.partial(pair_kernel, h),
            [at, keep, arrived[h]],
            [((256, TILE), BF16), ((256, TILE), F32)],
            1 << 20,
            name="pair",
        )
        for h in range(2)
    ]
    arrived = [inner(p[0]) for p in pairs]
    new_momentum, tile, v = call(
        momentum_kernel,
        [pairs[0][1], pairs[1][1], *arrived, momentum],
        [((TILE, TILE), F32), ((TILE, TILE), BF16), ((8, 128), F32)],
        1 << 20,
        name="momentum",
    )

    tile_s = sib(tile)

    def rows_of(half):
        start = (half * 2 + c) * PIECE
        return jnp.concatenate(
            [lax.dynamic_slice_in_dim(t, start, PIECE, 0) for t in (tile, tile_s)], axis=1
        )

    a = rows_of(xl)
    b = inner(rows_of(1 - xl))
    ra, la = zhop(a, 1), zhop(a, -1)
    t_out = outer(tile)
    v, b = together([("depth", 1)], v, b)
    r2 = zhop(jnp.concatenate([b, ra], axis=0), 1)
    l2 = zhop(jnp.concatenate([la, b], axis=0), -1)
    t_in = inner(lax.optimization_barrier((tile, b))[0])
    v, r2, l2, t_out = together([("col", 1)], v, r2, l2, t_out)
    v, t_in, r2, l2 = lax.optimization_barrier((v, t_in, r2, l2))
    r3, l3 = zhop(r2, 1), zhop(l2, -1)
    v, t_in, t_out = together([("col", 2)], v, t_in, t_out)
    far_a, far_b = outer(t_in[:256]), inner(t_out[256:])
    r3, l3, t_in, t_out, far_a, far_b = lax.optimization_barrier(
        (r3, l3, t_in, t_out, far_a, far_b)
    )
    t_far = jnp.concatenate([far_a, far_b], axis=0)
    r4, l4 = zhop(r3[:192], 1), zhop(l3[64:], -1)
    tiles = [tile, tile_s] + [t for v_ in (t_in, t_far, t_out) for t in (v_, sib(v_))]
    r5, l5 = zhop(r4[:64], 1), zhop(l4[128:], -1)
    joined0, held = gram_first(
        tiles,
        [a, b, ra, la, r2, l2, r3, l3, r4, l4],
        [HBM] * 6 + [ANY] * 4,
        [
            [[(0, 0, 128)], [(1, 0, 128)]],
            [[(2, 0, 128)], [(4, 0, 128)]],
            [[(3, 0, 128)], [(5, 128, 128)]],
            [[(4, 128, 128)], [(6, 0, 128)]],
            [[(5, 0, 128)], [(7, 128, 128)]],
            [[(6, 128, 128)], [(8, 0, 128)]],
            [[(7, 0, 128)], [(9, 64, 128)]],
        ],
    )
    r5, l5, held = lax.optimization_barrier((r5, l5, held))
    joined1, far0, far1, right, left, own = gram_last(
        y,
        held,
        tiles,
        [r4, l4, r5, l5],
        [[[(0, 128, 64), (1, 0, 64)], [(2, 0, 64), (3, 0, 64)]]],
    )
    right, left = near_sums(*start_sum(far0, far1), right, left)
    own, v = second_step(right, left, own, v)
    whole_rows, v = gather_far(*gather_near(own, v))

    far, whole, theirs, mine = call(
        far_kernel,
        [y, *whole_rows, joined0, joined1],
        [((TILE, TILE), BF16), ((1024, 1024), BF16)] + [((2, 1024, TILE), BF16)] * 2,
        1 << 29,
        name="far",
    )
    far = sib(far)
    rest = call(rest_kernel, [whole, theirs], [((TILE, TILE), BF16)] * 3, 3 << 29, name="rest")
    rest = [sib(t) for t in rest]
    upper, lower = call(
        far_sum_kernel, [whole, mine, far], [((256, TILE), BF16)] * 2, 1 << 29, name="far_sum"
    )
    v, upper, lower = lax.optimization_barrier((v, upper, lower))
    a1, b1 = inner(upper), outer(lower)
    t_own, t_in, t_out = call(
        rest_sum_kernel,
        [whole, mine, *rest],
        [((TILE, TILE), F32)] + [((TILE, TILE), BF16)] * 2,
        3 << 29,
        name="rest_sum",
    )
    v, a1, b1 = together([("row", 4)], v, a1, b1)
    to_out = jnp.concatenate([add(t_out[:256], a1).astype(BF16), t_out[256:]], 0)
    to_in = jnp.concatenate([t_in[:256], add(t_in[256:], b1).astype(BF16)], 0)
    v, to_in, to_out = lax.optimization_barrier((v, to_in, to_out))
    from_in, from_out = inner(to_in), outer(to_out)
    v, from_in, from_out = together([("row", 8)], v, from_in, from_out)
    prod = add(t_own, from_in, from_out)

    gain = math.sqrt(M) / (1.5 * (jnp.sqrt(jnp.sum(v)) + EPSILON))
    update = math.sqrt(M) * (
        (1.5 * gain) * tile.astype(F32) - (0.5 * gain * gain * gain) * prod
    )
    return (new_momentum, update)


def solution(mesh):
    placed = (P("depth", "row", "col"), P("depth", "row", "col"), P("row", ("col", "depth")))
    return jax.shard_map(
        body,
        mesh=mesh,
        in_specs=placed,
        out_specs=(P("row", ("col", "depth")), P("row", ("col", "depth"))),
        check_vma=False,
    )
```

```python
import functools
import math

import jax
import jax.numpy as jnp
from jax import lax
from jax.experimental import pallas as pl
from jax.experimental.pallas import tpu as pltpu
from jax.sharding import PartitionSpec as P

M = 8192
BETA = 0.95
EPSILON = 1e-07
F32 = jnp.float32
BF16 = jnp.bfloat16

NY = 4
TILE = 512
PIECE = 128
ZPERM = {s: [(r, (r + 2 * s) % 16) for r in range(16)] for s in (1, -1)}
YPERM = {s: [(y, (y + s) % 4) for y in range(4)] for s in (1, -1)}
SIB = [(d, d ^ 1) for d in range(4)]
INNER = [(d, d ^ 2) for d in range(4)]
OUTER = [(r * 4 + d, (r ^ 1) * 4 + (d ^ 2)) for r in range(16) for d in range(4)]


def sib(v):
    return lax.ppermute(v, "depth", SIB)


def inner(v):
    return lax.ppermute(v, "depth", INNER)


def outer(v):
    return lax.ppermute(v, ("row", "depth"), OUTER)


def across(v):
    return lax.ppermute(v, "row", [(r, r ^ 1) for r in range(16)])


def zhop(v, s):
    return lax.ppermute(v, "row", ZPERM[s])


def yhop(v, s):
    return lax.ppermute(v, "col", YPERM[s])


def in_hbm(v):
    return pltpu.with_memory_space_constraint(v, pltpu.HBM)


def swap_add(v, axis, bit):
    return v + lax.ppermute(v, axis, [(i, i ^ bit) for i in range(lax.axis_size(axis))])


def add(*vs):
    total = vs[0].astype(F32)
    for v in vs[1:]:
        total = total + v.astype(F32)
    return total


VMEM = pl.BlockSpec(memory_space=pltpu.VMEM)
SMEM = pl.BlockSpec(memory_space=pltpu.SMEM)
HBM = pl.BlockSpec(memory_space=pltpu.HBM)
ANY = pl.BlockSpec(memory_space=pl.ANY)


def start_parts(sources, parts_in, joined, sems):
    copies = []
    for p, piece in enumerate(sources):
        for half, parts in enumerate(piece):
            row = p * PIECE
            for i, start, size in parts:
                copies.append(
                    pltpu.make_async_copy(
                        parts_in[i].at[pl.ds(start, size)],
                        joined.at[pl.ds(row, size), pl.ds(half * 1024, 1024)],
                        sems.at[len(copies)],
                    )
                )
                copies[-1].start()
                row += size
    return copies


def gram_block(panel, joined, block):
    return lax.dot_general(
        panel[block * 256 : block * 256 + 256, :],
        joined[...],
        (((1,), (1,)), ((), ())),
        preferred_element_type=F32,
    ).astype(BF16)


def first_kernel(sources, *refs):
    tiles, parts_in = refs[:8], refs[8:-4]
    joined, panel, held, sems = refs[-4:]
    copies = start_parts(sources, parts_in, joined, sems)
    for i, tile in enumerate(tiles):
        target = panel.at[pl.ds(i // 4 * TILE, TILE), pl.ds(i % 4 * TILE, TILE)]
        copies.append(pltpu.make_async_copy(tile, target, sems.at[len(copies)]))
        copies[-1].start()
    for c in copies[:-4]:
        c.wait()
    for block in range(4):
        if block == 2:
            for c in copies[-4:]:
                c.wait()
        held[block] = gram_block(panel, joined, block)


def last_kernel(sources, y_ref, panel, held, *refs):
    parts_in = refs[:-8]
    joined, far0, far1, right, left, own, last, sems = refs[-8:]
    copies = start_parts(sources, parts_in, joined, sems)
    y = y_ref[0]
    wide = held.shape[2]
    for k, out in ((0, own), (1, right), (3, left)):
        out[:, :wide] = held[lax.rem(y + k, 4)]
    block = lax.rem(y + 2, 4)
    for out, rows in ((far0, slice(0, 128)), (far1, slice(128, 256))):
        out[:, :wide] = held[block, rows, :]
    for c in copies:
        c.wait()
    for block in range(4):
        last[block] = gram_block(panel, joined, block)
    for k, out in ((0, own), (1, right), (3, left)):
        out[:, wide:] = last[lax.rem(y + k, 4)]
    block = lax.rem(y + 2, 4)
    for out, rows in ((far0, slice(0, 128)), (far1, slice(128, 256))):
        out[:, wide:] = last[block, rows, :]


def count(sources):
    return sum(len(parts) for piece in sources for parts in piece)


def gram_cost(n):
    return pl.CostEstimate(flops=2 * 1024 * 2048 * n, bytes_accessed=8 << 20, transcendentals=0)


def gram_first(tiles, arrays, sources):
    n = len(sources) * PIECE
    return pl.pallas_call(
        functools.partial(first_kernel, sources),
        out_shape=[jax.ShapeDtypeStruct(s, BF16) for s in ((n, 2048), (1024, 2048), (4, 256, n))],
        in_specs=[ANY] * (8 + len(arrays)),
        out_specs=[VMEM] * 3,
        scratch_shapes=[pltpu.SemaphoreType.DMA((8 + count(sources),))],
        compiler_params=pltpu.CompilerParams(vmem_limit_bytes=8 << 20),
        cost_estimate=gram_cost(n),
        name="gram_first",
    )(*tiles, *arrays)


def gram_last(y, panel, held, arrays, sources):
    n = len(sources) * PIECE
    w = held.shape[2] + n
    shapes = [(n, 2048), (128, w), (128, w), (256, w), (256, w), (256, w)]
    return pl.pallas_call(
        functools.partial(last_kernel, sources),
        out_shape=[jax.ShapeDtypeStruct(s, BF16) for s in shapes],
        in_specs=[SMEM, VMEM, VMEM] + [ANY] * len(arrays),
        out_specs=[VMEM] * len(shapes),
        scratch_shapes=[
            pltpu.VMEM((4, 256, n), BF16),
            pltpu.SemaphoreType.DMA((count(sources),)),
        ],
        compiler_params=pltpu.CompilerParams(vmem_limit_bytes=8 << 20),
        cost_estimate=gram_cost(n),
        name="gram_last",
    )(y, panel, held, *arrays)


def far_kernel(y_ref, own, r3, l3, r4, l4, joined0, joined1, far, whole, theirs, mine):
    y = y_ref[0]

    def rows(k):
        return pl.multiple_of(lax.rem(y + k, 4) * 256, 256)

    for k, part in ((0, own), (1, l3), (3, r3)):
        whole[pl.ds(rows(k), 256), :] = part[...]
    whole[pl.ds(rows(2), 128), :] = r4[...]
    whole[pl.ds(rows(2) + 128, 128), :] = l4[...]
    at = 0
    for joined in (joined0, joined1):
        size = joined.shape[0]
        for half in range(2):
            start = half * 1024
            mine[half, at : at + size, :] = joined[:, start : start + TILE]
            theirs[half, at : at + size, :] = joined[:, start + TILE : start + 2 * TILE]
        at += size
    far[...] = jnp.dot(whole[512:], theirs[0], preferred_element_type=F32).astype(BF16)


def rest_kernel(whole, theirs, own, near, out):
    own[...] = jnp.dot(whole[:512], theirs[0], preferred_element_type=F32).astype(BF16)
    near[...] = jnp.dot(whole[:512], theirs[1], preferred_element_type=F32).astype(BF16)
    out[...] = jnp.dot(whole[512:], theirs[1], preferred_element_type=F32).astype(BF16)


def far_sum_kernel(whole, mine, arrived, upper, lower):
    total = jnp.dot(whole[512:], mine[0], preferred_element_type=F32) + arrived[...].astype(F32)
    upper[...] = total[:256].astype(BF16)
    lower[...] = total[256:].astype(BF16)


def rest_sum_kernel(whole, mine, a_own, a_near, a_out, own, near, out):
    def term(rows, half, arrived):
        return jnp.dot(whole[rows], mine[half], preferred_element_type=F32) + arrived[...].astype(F32)

    own[...] = term(slice(0, 512), 0, a_own)
    near[...] = term(slice(0, 512), 1, a_near).astype(BF16)
    out[...] = term(slice(512, 1024), 1, a_out).astype(BF16)


def call(kernel, operands, shapes, flops, limit=8, name=None):
    return pl.pallas_call(
        kernel,
        out_shape=[jax.ShapeDtypeStruct(*s) for s in shapes],
        in_specs=[SMEM if v.dtype == jnp.int32 else VMEM for v in operands],
        out_specs=[VMEM] * len(shapes),
        compiler_params=pltpu.CompilerParams(vmem_limit_bytes=limit << 20),
        cost_estimate=pl.CostEstimate(flops=flops, bytes_accessed=4 << 20, transcendentals=0),
        name=name,
    )(*operands)


def scaled_kernel(at_ref, q_ref, s_ref, send0, send1, keep, q_buf, s_buf, sems):
    c = at_ref[0]
    scales = pltpu.make_async_copy(s_ref.at[0], s_buf, sems.at[8])
    scales.start()
    copies = []
    for step in range(4):
        for side, core in enumerate((1 - c, c)):
            start = pl.multiple_of((step % 2 * 2 + core) * TILE, TILE)
            copies.append(
                pltpu.make_async_copy(
                    q_ref.at[0, pl.ds(step // 2 * 256, 256), pl.ds(start, TILE)],
                    q_buf.at[2 * step + side],
                    sems.at[2 * step + side],
                )
            )
            copies[-1].start()
    scales.wait()
    for step in range(4):
        for side, core in enumerate((1 - c, c)):
            copies[2 * step + side].wait()
            start = pl.multiple_of((step % 2 * 2 + core) * TILE, TILE)
            for r in range(2):
                rows = slice(r * 128, r * 128 + 128)
                row = step // 2 * 2 + r
                scale = s_buf[row : row + 1, pl.ds(start, TILE)]
                value = q_buf[2 * step + side, rows, :].astype(F32) * scale
                if side:
                    keep[step, rows, :] = value
                else:
                    (send0, send1)[step // 2][step % 2, rows, :] = value.astype(BF16)


def scaled_parts(at, quant, scale):
    return pl.pallas_call(
        scaled_kernel,
        in_specs=[SMEM, HBM, HBM],
        out_specs=[VMEM] * 3,
        out_shape=[
            jax.ShapeDtypeStruct((2, 256, TILE), BF16),
            jax.ShapeDtypeStruct((2, 256, TILE), BF16),
            jax.ShapeDtypeStruct((4, 256, TILE), F32),
        ],
        scratch_shapes=[
            pltpu.VMEM((8, 256, TILE), BF16),
            pltpu.VMEM((4, 4 * TILE), F32),
            pltpu.SemaphoreType.DMA((9,)),
        ],
        compiler_params=pltpu.CompilerParams(vmem_limit_bytes=8 << 20),
        name="scaled",
    )(at, in_hbm(quant), in_hbm(scale))


def pair_kernel(half, at_ref, keep, arrived, to_inner, kept):
    xl = at_ref[1]
    to_inner[...] = (keep[2 * half + 1 - xl] + arrived[1 - xl].astype(F32)).astype(BF16)
    kept[...] = keep[2 * half + xl] + arrived[xl].astype(F32)


def momentum_kernel(kept0, kept1, arrived0, arrived1, momentum, new_ref, tile_ref, squares_ref):
    total = jnp.zeros((8, TILE), F32)
    for half, (kept, arrived) in enumerate(((kept0, arrived0), (kept1, arrived1))):
        rows = slice(half * 256, half * 256 + 256)
        gradient = kept[...] + arrived[...].astype(F32)
        new = BETA * momentum[rows, :] + gradient
        nesterov = gradient + BETA * new
        new_ref[rows, :] = new
        tile_ref[rows, :] = nesterov.astype(BF16)
        total = total + jnp.sum((nesterov * nesterov).reshape(32, 8, TILE), axis=0)
    squares_ref[...] = total[:, :128] + total[:, 128:256] + total[:, 256:384] + total[:, 384:]


def together(steps, v, *arrays):
    for axis, bit in steps:
        v = swap_add(v, axis, bit)
    return lax.optimization_barrier((v, *arrays))


def start_sum(far0, far1):
    return yhop(far0, 1), yhop(far1, -1)


def near_sums(r1, l1, right, left):
    right = jnp.concatenate([add(right[:128], r1).astype(BF16), right[128:]], 0)
    left = jnp.concatenate([left[:128], add(left[128:], l1).astype(BF16)], 0)
    return right, left


def second_step(right, left, own, v=None):
    if v is not None:
        v, right, left = lax.optimization_barrier((v, right, left))
    r2, l2 = yhop(right, 1), yhop(left, -1)
    if v is not None:
        v, r2, l2 = together([("depth", 2)], v, r2, l2)
    return add(own, r2, l2).astype(BF16), v


def gather_near(own, v=None):
    if v is not None:
        v, own = lax.optimization_barrier((v, own))
    r3, l3 = yhop(own, 1), yhop(own, -1)
    if v is not None:
        v, r3, l3 = together([("row", 1)], v, r3, l3)
    return own, r3, l3, v


def gather_far(own, r3, l3, v=None):
    r4, l4 = yhop(r3[:128], 1), yhop(l3[128:], -1)
    if v is not None:
        v, r4, l4 = together([("row", 2)], v, r4, l4)
    return (own, r3, l3, r4, l4), v


def body(grad_partial, grad_scale, momentum):
    y = lax.axis_index("col").astype(jnp.int32).reshape(1)
    depth = lax.axis_index("depth").astype(jnp.int32)
    xl, c = depth // 2, depth % 2
    at = jnp.stack([c, xl])
    send0, send1, keep = scaled_parts(at, grad_partial, grad_scale)
    arrived = [sib(send0), sib(send1)]
    pairs = [
        call(
            functools.partial(pair_kernel, h),
            [at, keep, arrived[h]],
            [((256, TILE), BF16), ((256, TILE), F32)],
            1 << 20,
            name="pair",
        )
        for h in range(2)
    ]
    arrived = [inner(p[0]) for p in pairs]
    new_momentum, tile, v = call(
        momentum_kernel,
        [pairs[0][1], pairs[1][1], *arrived, momentum],
        [((TILE, TILE), F32), ((TILE, TILE), BF16), ((8, 128), F32)],
        1 << 20,
        name="momentum",
    )

    tile_s = sib(tile)

    def rows_of(half):
        start = (half * 2 + c) * PIECE
        return jnp.concatenate(
            [lax.dynamic_slice_in_dim(t, start, PIECE, 0) for t in (tile, tile_s)], axis=1
        )

    a = rows_of(xl)
    b = inner(rows_of(1 - xl))
    ra, la = zhop(a, 1), zhop(a, -1)
    t_out = outer(tile)
    v, b = together([("depth", 1)], v, b)
    r2 = zhop(jnp.concatenate([b, ra], axis=0), 1)
    l2 = zhop(jnp.concatenate([la, b], axis=0), -1)
    t_in = inner(lax.optimization_barrier((tile, b))[0])
    v, r2, l2, t_out = together([("col", 1)], v, r2, l2, t_out)
    v, t_in, r2, l2 = lax.optimization_barrier((v, t_in, r2, l2))
    r3, l3 = zhop(r2, 1), zhop(l2, -1)
    v, t_in, t_out = together([("col", 2)], v, t_in, t_out)
    far_a, far_b = outer(t_in[:256]), inner(t_out[256:])
    r3, l3, t_in, t_out, far_a, far_b = lax.optimization_barrier(
        (r3, l3, t_in, t_out, far_a, far_b)
    )
    t_far = jnp.concatenate([far_a, far_b], axis=0)
    r4, l4 = zhop(r3[:192], 1), zhop(l3[64:], -1)
    tiles = [tile, tile_s] + [t for v_ in (t_in, t_far, t_out) for t in (v_, sib(v_))]
    r5, l5 = zhop(r4[:64], 1), zhop(l4[128:], -1)
    joined0, panel, held = gram_first(
        tiles,
        [in_hbm(t) for t in (a, b, ra, la, r2, l2)] + [r3, l3, r4, l4],
        [
            [[(0, 0, 128)], [(1, 0, 128)]],
            [[(2, 0, 128)], [(4, 0, 128)]],
            [[(3, 0, 128)], [(5, 128, 128)]],
            [[(4, 128, 128)], [(6, 0, 128)]],
            [[(5, 0, 128)], [(7, 128, 128)]],
            [[(6, 128, 128)], [(8, 0, 128)]],
            [[(7, 0, 128)], [(9, 64, 128)]],
        ],
    )
    r5, l5, held = lax.optimization_barrier((r5, l5, held))
    joined1, far0, far1, right, left, own = gram_last(
        y,
        panel,
        held,
        [r4, l4, r5, l5],
        [[[(0, 128, 64), (1, 0, 64)], [(2, 0, 64), (3, 0, 64)]]],
    )
    right, left = near_sums(*start_sum(far0, far1), right, left)
    own, v = second_step(right, left, own, v)
    whole_rows, v = gather_far(*gather_near(own, v))

    far, whole, theirs, mine = call(
        far_kernel,
        [y, *whole_rows, joined0, joined1],
        [((TILE, TILE), BF16), ((1024, 1024), BF16)] + [((2, 1024, TILE), BF16)] * 2,
        1 << 29,
        name="far",
    )
    far = sib(far)
    rest = call(rest_kernel, [whole, theirs], [((TILE, TILE), BF16)] * 3, 3 << 29, name="rest")
    rest = [sib(t) for t in rest]
    upper, lower = call(
        far_sum_kernel, [whole, mine, far], [((256, TILE), BF16)] * 2, 1 << 29, name="far_sum"
    )
    v, upper, lower = lax.optimization_barrier((v, upper, lower))
    a1, b1 = inner(upper), outer(lower)
    t_own, t_in, t_out = call(
        rest_sum_kernel,
        [whole, mine, *rest],
        [((TILE, TILE), F32)] + [((TILE, TILE), BF16)] * 2,
        3 << 29,
        name="rest_sum",
    )
    v, a1, b1 = together([("row", 4)], v, a1, b1)
    to_out = jnp.concatenate([add(t_out[:256], a1).astype(BF16), t_out[256:]], 0)
    to_in = jnp.concatenate([t_in[:256], add(t_in[256:], b1).astype(BF16)], 0)
    v, to_in, to_out = lax.optimization_barrier((v, to_in, to_out))
    from_in, from_out = inner(to_in), outer(to_out)
    v, from_in, from_out = together([("row", 8)], v, from_in, from_out)
    prod = add(t_own, from_in, from_out)

    gain = math.sqrt(M) / (1.5 * (jnp.sqrt(jnp.sum(v)) + EPSILON))
    update = math.sqrt(M) * (
        (1.5 * gain) * tile.astype(F32) - (0.5 * gain * gain * gain) * prod
    )
    return (new_momentum, update)


def solution(mesh):
    placed = (P("depth", "row", "col"), P("depth", "row", "col"), P("row", ("col", "depth")))
    return jax.shard_map(
        body,
        mesh=mesh,
        in_specs=placed,
        out_specs=(P("row", ("col", "depth")), P("row", ("col", "depth"))),
        check_vma=False,
    )
```

```python
import functools
import math

import jax
import jax.numpy as jnp
from jax import lax
from jax.experimental import pallas as pl
from jax.experimental.pallas import tpu as pltpu
from jax.sharding import PartitionSpec as P

M = 8192
BETA = 0.95
EPSILON = 1e-07
F32 = jnp.float32
BF16 = jnp.bfloat16

NY = 4
TILE = 512
PIECE = 128
ZPERM = {s: [(r, (r + 2 * s) % 16) for r in range(16)] for s in (1, -1)}
YPERM = {s: [(y, (y + s) % 4) for y in range(4)] for s in (1, -1)}
SIB = [(d, d ^ 1) for d in range(4)]
INNER = [(d, d ^ 2) for d in range(4)]
OUTER = [(r * 4 + d, (r ^ 1) * 4 + (d ^ 2)) for r in range(16) for d in range(4)]


def sib(v):
    return lax.ppermute(v, "depth", SIB)


def inner(v):
    return lax.ppermute(v, "depth", INNER)


def outer(v):
    return lax.ppermute(v, ("row", "depth"), OUTER)


def across(v):
    return lax.ppermute(v, "row", [(r, r ^ 1) for r in range(16)])


def zhop(v, s):
    return lax.ppermute(v, "row", ZPERM[s])


def yhop(v, s):
    return lax.ppermute(v, "col", YPERM[s])


def in_hbm(v):
    return pltpu.with_memory_space_constraint(v, pltpu.HBM)


def swap_add(v, axis, bit):
    return v + lax.ppermute(v, axis, [(i, i ^ bit) for i in range(lax.axis_size(axis))])


def add(*vs):
    total = vs[0].astype(F32)
    for v in vs[1:]:
        total = total + v.astype(F32)
    return total


VMEM = pl.BlockSpec(memory_space=pltpu.VMEM)
SMEM = pl.BlockSpec(memory_space=pltpu.SMEM)
HBM = pl.BlockSpec(memory_space=pltpu.HBM)
ANY = pl.BlockSpec(memory_space=pl.ANY)


def gram_kernel(sources, with_panel, y_ref, *refs):
    n_tiles = 10 if with_panel else 1
    n_in = n_tiles + 1 + max(i for piece in sources for parts in piece for i, _, _ in parts)
    tiles, parts_in, outs = refs[:n_tiles], refs[n_tiles:n_in], list(refs[n_in:])
    held, sems = outs[-2:]
    joined, right, left, own, *far = outs[:-2]
    copies = []

    def copy(source, target):
        copies.append(pltpu.make_async_copy(source, target, sems.at[len(copies)]))
        copies[-1].start()

    for p, piece in enumerate(sources):
        for half, parts in enumerate(piece):
            row = p * PIECE
            for i, start, size in parts:
                copy(
                    parts_in[i].at[pl.ds(start, size)],
                    joined.at[pl.ds(row, size), pl.ds(half * 1024, 1024)],
                )
                row += size
    late = 0
    if with_panel:
        panel = far.pop()
        for i in range(4):
            copy(tiles[i], panel.at[pl.ds(0, TILE), pl.ds(i * TILE, TILE)])
        late = len(copies)
        for i in range(2):
            for part in range(2):
                copy(
                    tiles[4 + 2 * i + part],
                    panel.at[pl.ds(TILE + 256 * part, 256), pl.ds(i * TILE, TILE)],
                )
            copy(tiles[8 + i], panel.at[pl.ds(TILE, TILE), pl.ds((2 + i) * TILE, TILE)])
        late -= len(copies)
    else:
        panel = tiles[0]
    for c in copies[: late or None]:
        c.wait()
    y = y_ref[0]
    for block in range(4):
        if late and block == 2:
            for c in copies[late:]:
                c.wait()
        held[lax.rem(block + 4 - y, 4)] = lax.dot_general(
            panel[block * 256 : block * 256 + 256, :],
            joined[...],
            (((1,), (1,)), ((), ())),
            preferred_element_type=F32,
        ).astype(BF16)
    own[...] = held[0]
    right[...] = held[1]
    left[...] = held[3]
    rows = 256 // len(far)
    for i, out in enumerate(far):
        out[...] = held[2, i * rows : (i + 1) * rows]


def gram(y, tiles, arrays, sources, far_parts=2):
    n = len(sources) * PIECE
    with_panel = len(tiles) > 1
    shapes = [(n, 2048)] + [(256, n)] * 3 + [(256 // far_parts, n)] * far_parts
    n_copies = sum(len(parts) for piece in sources for parts in piece)
    if with_panel:
        shapes.append((1024, 2048))
        n_copies += 10
    return pl.pallas_call(
        functools.partial(gram_kernel, sources, with_panel),
        out_shape=[jax.ShapeDtypeStruct(s, BF16) for s in shapes],
        in_specs=[SMEM] + ([ANY] * 10 if with_panel else [VMEM]) + [ANY] * len(arrays),
        out_specs=[VMEM] * len(shapes),
        scratch_shapes=[
            pltpu.VMEM((4, 256, n), BF16),
            pltpu.SemaphoreType.DMA((n_copies,)),
        ],
        compiler_params=pltpu.CompilerParams(vmem_limit_bytes=8 << 20),
        cost_estimate=pl.CostEstimate(
            flops=2 * 1024 * 2048 * n, bytes_accessed=8 << 20, transcendentals=0
        ),
        name="gram",
    )(y, *tiles, *arrays)


def near_kernel(*refs):
    rights, lefts, from_left, from_right = refs[0:3], refs[3:6], refs[6:8], refs[8:10]
    to_right, to_left = refs[10:]
    at = 0
    for i in range(3):
        cols = slice(at, at + rights[i].shape[1])
        to_right[:, cols] = rights[i][...]
        to_left[:, cols] = lefts[i][...]
        if i < 2:
            to_right[:128, cols] = add(rights[i][:128, :], from_left[i][...]).astype(BF16)
            to_left[128:, cols] = add(lefts[i][128:, :], from_right[i][...]).astype(BF16)
        at = cols.stop


def own_kernel(own0, own1, own2, from_left, from_right, from_far, total):
    at = 0
    for i, own in enumerate((own0, own1, own2)):
        cols = slice(at, at + own.shape[1])
        value = add(own[...], from_left[:, cols], from_right[:, cols])
        if i == 2:
            value = value + from_far[...].astype(F32)
        total[:, cols] = value.astype(BF16)
        at = cols.stop


def far_kernel(y_ref, own, r3, l3, r4, l4, joined0, joined1, joined2, far, whole, theirs, mine):
    y = y_ref[0]

    def rows(k):
        return pl.multiple_of(lax.rem(y + k, 4) * 256, 256)

    for k, part in ((0, own), (1, l3), (3, r3)):
        whole[pl.ds(rows(k), 256), :] = part[...]
    whole[pl.ds(rows(2), 128), :] = r4[...]
    whole[pl.ds(rows(2) + 128, 128), :] = l4[...]
    at = 0
    for joined in (joined0, joined1, joined2):
        size = joined.shape[0]
        for half in range(2):
            start = half * 1024
            mine[half, at : at + size, :] = joined[:, start : start + TILE]
            theirs[half, at : at + size, :] = joined[:, start + TILE : start + 2 * TILE]
        at += size
    far[...] = jnp.dot(whole[512:], theirs[0], preferred_element_type=F32).astype(BF16)


def rest_kernel(whole, theirs, own, near, out):
    own[...] = jnp.dot(whole[:512], theirs[0], preferred_element_type=F32).astype(BF16)
    near[...] = jnp.dot(whole[:512], theirs[1], preferred_element_type=F32).astype(BF16)
    out[...] = jnp.dot(whole[512:], theirs[1], preferred_element_type=F32).astype(BF16)


def far_sum_kernel(whole, mine, arrived, upper, lower):
    total = jnp.dot(whole[512:], mine[0], preferred_element_type=F32) + arrived[...].astype(F32)
    upper[...] = total[:256].astype(BF16)
    lower[...] = total[256:].astype(BF16)


def rest_sum_kernel(whole, mine, a_own, a_near, a_out, own, near, out):
    def term(rows, half, arrived):
        return jnp.dot(whole[rows], mine[half], preferred_element_type=F32) + arrived[...].astype(F32)

    own[...] = term(slice(0, 512), 0, a_own)
    near[...] = term(slice(0, 512), 1, a_near).astype(BF16)
    out[...] = term(slice(512, 1024), 1, a_out).astype(BF16)


def call(kernel, operands, shapes, flops, limit=8, name=None):
    return pl.pallas_call(
        kernel,
        out_shape=[jax.ShapeDtypeStruct(*s) for s in shapes],
        in_specs=[SMEM if v.dtype == jnp.int32 else VMEM for v in operands],
        out_specs=[VMEM] * len(shapes),
        compiler_params=pltpu.CompilerParams(vmem_limit_bytes=limit << 20),
        cost_estimate=pl.CostEstimate(flops=flops, bytes_accessed=4 << 20, transcendentals=0),
        name=name,
    )(*operands)


def scaled_kernel(at_ref, q_ref, s_ref, send0, send1, keep, q_buf, s_buf, sems):
    c = at_ref[0]
    scales = pltpu.make_async_copy(s_ref.at[0], s_buf, sems.at[8])
    scales.start()
    copies = []
    for step in range(4):
        for side, core in enumerate((1 - c, c)):
            start = pl.multiple_of((step % 2 * 2 + core) * TILE, TILE)
            copies.append(
                pltpu.make_async_copy(
                    q_ref.at[0, pl.ds(step // 2 * 256, 256), pl.ds(start, TILE)],
                    q_buf.at[2 * step + side],
                    sems.at[2 * step + side],
                )
            )
            copies[-1].start()
    scales.wait()
    for step in range(4):
        for side, core in enumerate((1 - c, c)):
            copies[2 * step + side].wait()
            start = pl.multiple_of((step % 2 * 2 + core) * TILE, TILE)
            for r in range(2):
                rows = slice(r * 128, r * 128 + 128)
                row = step // 2 * 2 + r
                scale = s_buf[row : row + 1, pl.ds(start, TILE)]
                value = q_buf[2 * step + side, rows, :].astype(F32) * scale
                if side:
                    keep[step, rows, :] = value
                else:
                    (send0, send1)[step // 2][step % 2, rows, :] = value.astype(BF16)


def scaled_parts(at, quant, scale):
    return pl.pallas_call(
        scaled_kernel,
        in_specs=[SMEM, HBM, HBM],
        out_specs=[VMEM] * 3,
        out_shape=[
            jax.ShapeDtypeStruct((2, 256, TILE), BF16),
            jax.ShapeDtypeStruct((2, 256, TILE), BF16),
            jax.ShapeDtypeStruct((4, 256, TILE), F32),
        ],
        scratch_shapes=[
            pltpu.VMEM((8, 256, TILE), BF16),
            pltpu.VMEM((4, 4 * TILE), F32),
            pltpu.SemaphoreType.DMA((9,)),
        ],
        compiler_params=pltpu.CompilerParams(vmem_limit_bytes=8 << 20),
        name="scaled",
    )(at, in_hbm(quant), in_hbm(scale))


def pair_kernel(half, at_ref, keep, arrived, to_inner, kept):
    xl = at_ref[1]
    to_inner[...] = (keep[2 * half + 1 - xl] + arrived[1 - xl].astype(F32)).astype(BF16)
    kept[...] = keep[2 * half + xl] + arrived[xl].astype(F32)


def momentum_kernel(kept0, kept1, arrived0, arrived1, momentum, new_ref, tile_ref, squares_ref):
    total = jnp.zeros((8, TILE), F32)
    for half, (kept, arrived) in enumerate(((kept0, arrived0), (kept1, arrived1))):
        rows = slice(half * 256, half * 256 + 256)
        gradient = kept[...] + arrived[...].astype(F32)
        new = BETA * momentum[rows, :] + gradient
        nesterov = gradient + BETA * new
        new_ref[rows, :] = new
        tile_ref[rows, :] = nesterov.astype(BF16)
        total = total + jnp.sum((nesterov * nesterov).reshape(32, 8, TILE), axis=0)
    squares_ref[...] = total[:, :128] + total[:, 128:256] + total[:, 256:384] + total[:, 384:]


def together(steps, v, *arrays):
    for axis, bit in steps:
        v = swap_add(v, axis, bit)
    return lax.optimization_barrier((v, *arrays))


def start_sum(far0, far1):
    return yhop(far0, 1), yhop(far1, -1)


def gather_near(own, v=None):
    if v is not None:
        v, own = lax.optimization_barrier((v, own))
    r3, l3 = yhop(own, 1), yhop(own, -1)
    if v is not None:
        v, r3, l3 = together([("row", 1)], v, r3, l3)
    return own, r3, l3, v


def gather_far(own, r3, l3, v=None):
    r4, l4 = yhop(r3[:128], 1), yhop(l3[128:], -1)
    if v is not None:
        v, r4, l4 = together([("row", 2)], v, r4, l4)
    return (own, r3, l3, r4, l4), v


def body(grad_partial, grad_scale, momentum):
    y = lax.axis_index("col").astype(jnp.int32).reshape(1)
    depth = lax.axis_index("depth").astype(jnp.int32)
    xl, c = depth // 2, depth % 2
    at = jnp.stack([c, xl])
    send0, send1, keep = scaled_parts(at, grad_partial, grad_scale)
    arrived = [sib(send0), sib(send1)]
    pairs = [
        call(
            functools.partial(pair_kernel, h),
            [at, keep, arrived[h]],
            [((256, TILE), BF16), ((256, TILE), F32)],
            1 << 20,
            name="pair",
        )
        for h in range(2)
    ]
    arrived = [inner(p[0]) for p in pairs]
    new_momentum, tile, v = call(
        momentum_kernel,
        [pairs[0][1], pairs[1][1], *arrived, momentum],
        [((TILE, TILE), F32), ((TILE, TILE), BF16), ((8, 128), F32)],
        1 << 20,
        name="momentum",
    )

    tile_s = sib(tile)

    def rows_of(half):
        start = (half * 2 + c) * PIECE
        return jnp.concatenate(
            [lax.dynamic_slice_in_dim(t, start, PIECE, 0) for t in (tile, tile_s)], axis=1
        )

    a = rows_of(xl)
    b = inner(rows_of(1 - xl))
    ra, la = zhop(a, 1), zhop(a, -1)
    t_out = outer(tile)
    v, b = together([("depth", 1)], v, b)
    r2 = zhop(jnp.concatenate([b, ra], axis=0), 1)
    l2 = zhop(jnp.concatenate([la, b], axis=0), -1)
    t_in = inner(lax.optimization_barrier((tile, b))[0])
    v, r2, l2, t_out = together([("col", 1)], v, r2, l2, t_out)
    v, t_in, r2, l2 = lax.optimization_barrier((v, t_in, r2, l2))
    r3, l3 = zhop(r2, 1), zhop(l2, -1)
    v, t_in, t_out, t_in_s, t_out_s = together(
        [("col", 2)], v, t_in, t_out, sib(t_in), sib(t_out)
    )
    far_a, far_b = outer(t_in[:256]), inner(t_out[256:])
    far_a, far_b, *_ = lax.optimization_barrier((far_a, far_b, r3, l3))
    r4, l4 = zhop(r3[:192], 1), zhop(l3[64:], -1)
    tiles = [tile, tile_s, t_in, t_in_s, far_a, far_b, sib(far_a), sib(far_b), t_out, t_out_s]
    joined0, right0, left0, own0, far0, far1, panel = gram(
        y,
        tiles,
        [in_hbm(t) for t in (a, b, ra, la, r2, l2)] + [r3, l3],
        [
            [[(0, 0, 128)], [(1, 0, 128)]],
            [[(2, 0, 128)], [(4, 0, 128)]],
            [[(3, 0, 128)], [(5, 128, 128)]],
            [[(4, 128, 128)], [(6, 0, 128)]],
            [[(5, 0, 128)], [(7, 128, 128)]],
        ],
    )
    r4, l4, far0, far1, panel = lax.optimization_barrier((r4, l4, far0, far1, panel))
    r5, l5 = zhop(r4[:64], 1), zhop(l4[128:], -1)
    from_left0, from_right0 = start_sum(far0, far1)
    joined1, right1, left1, own1, far0, far1 = gram(
        y,
        [panel],
        [r3, l3, r4, l4],
        [[[(0, 128, 128)], [(2, 0, 128)]], [[(1, 0, 128)], [(3, 64, 128)]]],
    )
    r5, l5, from_left0, from_right0, far0, far1 = lax.optimization_barrier(
        (r5, l5, from_left0, from_right0, far0, far1)
    )
    from_left1, from_right1 = start_sum(far0, far1)
    joined2, right2, left2, own2, far2 = gram(
        y,
        [panel],
        [r4, l4, r5, l5],
        [[[(0, 128, 64), (1, 0, 64)], [(2, 0, 64), (3, 0, 64)]]],
        far_parts=1,
    )
    right, left = call(
        near_kernel,
        [right0, right1, right2, left0, left1, left2]
        + [from_left0, from_left1, from_right0, from_right1],
        [((256, 1024), BF16)] * 2,
        1 << 20,
        name="near",
    )
    v, right, left = lax.optimization_barrier((v, right, left))
    from_left, from_right = yhop(right, 1), yhop(left, -1)
    from_far = lax.ppermute(far2, "col", [(i, i ^ 2) for i in range(4)])
    v, from_left, from_right = together([("depth", 2)], v, from_left, from_right)
    (own,) = call(
        own_kernel,
        [own0, own1, own2, from_left, from_right, from_far],
        [((256, 1024), BF16)],
        1 << 20,
        name="own",
    )
    whole_rows, v = gather_far(*gather_near(own, v))

    far, whole, theirs, mine = call(
        far_kernel,
        [y, *whole_rows, joined0, joined1, joined2],
        [((TILE, TILE), BF16), ((1024, 1024), BF16)] + [((2, 1024, TILE), BF16)] * 2,
        1 << 29,
        name="far",
    )
    far = sib(far)
    rest = call(rest_kernel, [whole, theirs], [((TILE, TILE), BF16)] * 3, 3 << 29, name="rest")
    rest = [sib(t) for t in rest]
    upper, lower = call(
        far_sum_kernel, [whole, mine, far], [((256, TILE), BF16)] * 2, 1 << 29, name="far_sum"
    )
    v, upper, lower = lax.optimization_barrier((v, upper, lower))
    a1, b1 = inner(upper), outer(lower)
    t_own, t_in, t_out = call(
        rest_sum_kernel,
        [whole, mine, *rest],
        [((TILE, TILE), F32)] + [((TILE, TILE), BF16)] * 2,
        3 << 29,
        name="rest_sum",
    )
    v, a1, b1 = together([("row", 4)], v, a1, b1)
    to_out = jnp.concatenate([add(t_out[:256], a1).astype(BF16), t_out[256:]], 0)
    to_in = jnp.concatenate([t_in[:256], add(t_in[256:], b1).astype(BF16)], 0)
    v, to_in, to_out = lax.optimization_barrier((v, to_in, to_out))
    from_in, from_out = inner(to_in), outer(to_out)
    v, from_in, from_out = together([("row", 8)], v, from_in, from_out)
    prod = add(t_own, from_in, from_out)

    gain = math.sqrt(M) / (1.5 * (jnp.sqrt(jnp.sum(v)) + EPSILON))
    update = math.sqrt(M) * (
        (1.5 * gain) * tile.astype(F32) - (0.5 * gain * gain * gain) * prod
    )
    return (new_momentum, update)


def solution(mesh):
    placed = (P("depth", "row", "col"), P("depth", "row", "col"), P("row", ("col", "depth")))
    return jax.shard_map(
        body,
        mesh=mesh,
        in_specs=placed,
        out_specs=(P("row", ("col", "depth")), P("row", ("col", "depth"))),
        check_vma=False,
    )
```

```python
import functools
import math

import jax
import jax.numpy as jnp
from jax import lax
from jax.experimental import pallas as pl
from jax.experimental.pallas import tpu as pltpu
from jax.sharding import PartitionSpec as P

M = 8192
BETA = 0.95
EPSILON = 1e-07
F32 = jnp.float32
BF16 = jnp.bfloat16

NY = 4
TILE = 512
PIECE = 128
ZPERM = {s: [(r, (r + 2 * s) % 16) for r in range(16)] for s in (1, -1)}
YPERM = {s: [(y, (y + s) % 4) for y in range(4)] for s in (1, -1)}
SIB = [(d, d ^ 1) for d in range(4)]
INNER = [(d, d ^ 2) for d in range(4)]
OUTER = [(r * 4 + d, (r ^ 1) * 4 + (d ^ 2)) for r in range(16) for d in range(4)]


def sib(v):
    return lax.ppermute(v, "depth", SIB)


def inner(v):
    return lax.ppermute(v, "depth", INNER)


def outer(v):
    return lax.ppermute(v, ("row", "depth"), OUTER)


def across(v):
    return lax.ppermute(v, "row", [(r, r ^ 1) for r in range(16)])


def zhop(v, s):
    return lax.ppermute(v, "row", ZPERM[s])


def yhop(v, s):
    return lax.ppermute(v, "col", YPERM[s])


def in_hbm(v):
    return pltpu.with_memory_space_constraint(v, pltpu.HBM)


def swap_add(v, axis, bit):
    return v + lax.ppermute(v, axis, [(i, i ^ bit) for i in range(lax.axis_size(axis))])


def add(*vs):
    total = vs[0].astype(F32)
    for v in vs[1:]:
        total = total + v.astype(F32)
    return total


VMEM = pl.BlockSpec(memory_space=pltpu.VMEM)
SMEM = pl.BlockSpec(memory_space=pltpu.SMEM)
HBM = pl.BlockSpec(memory_space=pltpu.HBM)
ANY = pl.BlockSpec(memory_space=pl.ANY)


def gram_kernel(sources, with_panel, y_ref, *refs):
    n_tiles = 10 if with_panel else 1
    n_in = n_tiles + 1 + max(i for piece in sources for parts in piece for i, _, _ in parts)
    tiles, parts_in, outs = refs[:n_tiles], refs[n_tiles:n_in], list(refs[n_in:])
    held, sems = outs[-2:]
    joined, right, left, own, *far = outs[:-2]
    copies = []

    def copy(source, target):
        copies.append(pltpu.make_async_copy(source, target, sems.at[len(copies)]))
        copies[-1].start()

    for p, piece in enumerate(sources):
        for half, parts in enumerate(piece):
            row = p * PIECE
            for i, start, size in parts:
                copy(
                    parts_in[i].at[pl.ds(start, size)],
                    joined.at[pl.ds(row, size), pl.ds(half * 1024, 1024)],
                )
                row += size
    late = 0
    if with_panel:
        panel = far.pop()
        for i in range(4):
            copy(tiles[i], panel.at[pl.ds(0, TILE), pl.ds(i * TILE, TILE)])
        late = len(copies)
        for i in range(2):
            for part in range(2):
                copy(
                    tiles[4 + 2 * i + part],
                    panel.at[pl.ds(TILE + 256 * part, 256), pl.ds(i * TILE, TILE)],
                )
            copy(tiles[8 + i], panel.at[pl.ds(TILE, TILE), pl.ds((2 + i) * TILE, TILE)])
        late -= len(copies)
    else:
        panel = tiles[0]
    for c in copies[: late or None]:
        c.wait()
    y = y_ref[0]
    for block in range(4):
        if late and block == 2:
            for c in copies[late:]:
                c.wait()
        held[lax.rem(block + 4 - y, 4)] = lax.dot_general(
            panel[block * 256 : block * 256 + 256, :],
            joined[...],
            (((1,), (1,)), ((), ())),
            preferred_element_type=F32,
        ).astype(BF16)
    own[...] = held[0]
    right[...] = held[1]
    left[...] = held[3]
    rows = 256 // len(far)
    for i, out in enumerate(far):
        out[...] = held[2, i * rows : (i + 1) * rows]


def gram(y, tiles, arrays, sources, far_parts=2):
    n = len(sources) * PIECE
    with_panel = len(tiles) > 1
    shapes = [(n, 2048)] + [(256, n)] * 3 + [(256 // far_parts, n)] * far_parts
    n_copies = sum(len(parts) for piece in sources for parts in piece)
    if with_panel:
        shapes.append((1024, 2048))
        n_copies += 10
    return pl.pallas_call(
        functools.partial(gram_kernel, sources, with_panel),
        out_shape=[jax.ShapeDtypeStruct(s, BF16) for s in shapes],
        in_specs=[SMEM] + ([ANY] * 10 if with_panel else [VMEM]) + [ANY] * len(arrays),
        out_specs=[VMEM] * len(shapes),
        scratch_shapes=[
            pltpu.VMEM((4, 256, n), BF16),
            pltpu.SemaphoreType.DMA((n_copies,)),
        ],
        compiler_params=pltpu.CompilerParams(vmem_limit_bytes=8 << 20),
        cost_estimate=pl.CostEstimate(
            flops=2 * 1024 * 2048 * n, bytes_accessed=8 << 20, transcendentals=0
        ),
        name="gram",
    )(y, *tiles, *arrays)


def near_kernel(*refs):
    rights, lefts, from_left, from_right = refs[0:3], refs[3:6], refs[6:8], refs[8:10]
    to_right, to_left = refs[10:]
    at = 0
    for i in range(3):
        cols = slice(at, at + rights[i].shape[1])
        to_right[:, cols] = rights[i][...]
        to_left[:, cols] = lefts[i][...]
        if i < 2:
            to_right[:128, cols] = add(rights[i][:128, :], from_left[i][...]).astype(BF16)
            to_left[128:, cols] = add(lefts[i][128:, :], from_right[i][...]).astype(BF16)
        at = cols.stop


def own_kernel(own0, own1, own2, from_left, from_right, from_far, total):
    at = 0
    for i, own in enumerate((own0, own1, own2)):
        cols = slice(at, at + own.shape[1])
        value = add(own[...], from_left[:, cols], from_right[:, cols])
        if i == 2:
            value = value + from_far[...].astype(F32)
        total[:, cols] = value.astype(BF16)
        at = cols.stop


def far_kernel(y_ref, own, r3, l3, r4, l4, joined0, joined1, joined2, far, whole, theirs, mine):
    y = y_ref[0]

    def rows(k):
        return pl.multiple_of(lax.rem(y + k, 4) * 256, 256)

    for k, part in ((0, own), (1, l3), (3, r3)):
        whole[pl.ds(rows(k), 256), :] = part[...]
    whole[pl.ds(rows(2), 128), :] = r4[...]
    whole[pl.ds(rows(2) + 128, 128), :] = l4[...]
    at = 0
    for joined in (joined0, joined1, joined2):
        size = joined.shape[0]
        for half in range(2):
            start = half * 1024
            mine[half, at : at + size, :] = joined[:, start : start + TILE]
            theirs[half, at : at + size, :] = joined[:, start + TILE : start + 2 * TILE]
        at += size
    far[...] = jnp.dot(whole[512:], theirs[0], preferred_element_type=F32).astype(BF16)


def rest_kernel(whole, theirs, own, near, out):
    own[...] = jnp.dot(whole[:512], theirs[0], preferred_element_type=F32).astype(BF16)
    near[...] = jnp.dot(whole[:512], theirs[1], preferred_element_type=F32).astype(BF16)
    out[...] = jnp.dot(whole[512:], theirs[1], preferred_element_type=F32).astype(BF16)


def far_sum_kernel(whole, mine, arrived, upper, lower):
    total = jnp.dot(whole[512:], mine[0], preferred_element_type=F32) + arrived[...].astype(F32)
    upper[...] = total[:256].astype(BF16)
    lower[...] = total[256:].astype(BF16)


def rest_sum_kernel(whole, mine, a_own, a_near, a_out, own, near, out):
    def term(rows, half, arrived):
        return jnp.dot(whole[rows], mine[half], preferred_element_type=F32) + arrived[...].astype(F32)

    own[...] = term(slice(0, 512), 0, a_own)
    near[...] = term(slice(0, 512), 1, a_near).astype(BF16)
    out[...] = term(slice(512, 1024), 1, a_out).astype(BF16)


def call(kernel, operands, shapes, flops, limit=8, name=None):
    return pl.pallas_call(
        kernel,
        out_shape=[jax.ShapeDtypeStruct(*s) for s in shapes],
        in_specs=[SMEM if v.dtype == jnp.int32 else VMEM for v in operands],
        out_specs=[VMEM] * len(shapes),
        compiler_params=pltpu.CompilerParams(vmem_limit_bytes=limit << 20),
        cost_estimate=pl.CostEstimate(flops=flops, bytes_accessed=4 << 20, transcendentals=0),
        name=name,
    )(*operands)


def scaled_kernel(at_ref, q_ref, s_ref, send0, send1, keep, q_buf, s_buf, sems):
    c = at_ref[0]
    scales = pltpu.make_async_copy(s_ref.at[0], s_buf, sems.at[8])
    scales.start()
    copies = []
    for step in range(4):
        for side, core in enumerate((1 - c, c)):
            start = pl.multiple_of((step % 2 * 2 + core) * TILE, TILE)
            copies.append(
                pltpu.make_async_copy(
                    q_ref.at[0, pl.ds(step // 2 * 256, 256), pl.ds(start, TILE)],
                    q_buf.at[2 * step + side],
                    sems.at[2 * step + side],
                )
            )
            copies[-1].start()
    scales.wait()
    for step in range(4):
        for side, core in enumerate((1 - c, c)):
            copies[2 * step + side].wait()
            start = pl.multiple_of((step % 2 * 2 + core) * TILE, TILE)
            for r in range(2):
                rows = slice(r * 128, r * 128 + 128)
                row = step // 2 * 2 + r
                scale = s_buf[row : row + 1, pl.ds(start, TILE)]
                value = q_buf[2 * step + side, rows, :].astype(F32) * scale
                if side:
                    keep[step, rows, :] = value
                else:
                    (send0, send1)[step // 2][step % 2, rows, :] = value.astype(BF16)


def scaled_parts(at, quant, scale):
    return pl.pallas_call(
        scaled_kernel,
        in_specs=[SMEM, HBM, HBM],
        out_specs=[VMEM] * 3,
        out_shape=[
            jax.ShapeDtypeStruct((2, 256, TILE), BF16),
            jax.ShapeDtypeStruct((2, 256, TILE), BF16),
            jax.ShapeDtypeStruct((4, 256, TILE), F32),
        ],
        scratch_shapes=[
            pltpu.VMEM((8, 256, TILE), BF16),
            pltpu.VMEM((4, 4 * TILE), F32),
            pltpu.SemaphoreType.DMA((9,)),
        ],
        compiler_params=pltpu.CompilerParams(vmem_limit_bytes=8 << 20),
        name="scaled",
    )(at, in_hbm(quant), in_hbm(scale))


def pair_kernel(half, at_ref, keep, arrived, to_inner, kept):
    xl = at_ref[1]
    to_inner[...] = (keep[2 * half + 1 - xl] + arrived[1 - xl].astype(F32)).astype(BF16)
    kept[...] = keep[2 * half + xl] + arrived[xl].astype(F32)


def momentum_kernel(kept0, kept1, arrived0, arrived1, momentum, new_ref, tile_ref, squares_ref):
    total = jnp.zeros((8, TILE), F32)
    for half, (kept, arrived) in enumerate(((kept0, arrived0), (kept1, arrived1))):
        rows = slice(half * 256, half * 256 + 256)
        gradient = kept[...] + arrived[...].astype(F32)
        new = BETA * momentum[rows, :] + gradient
        nesterov = gradient + BETA * new
        new_ref[rows, :] = new
        tile_ref[rows, :] = nesterov.astype(BF16)
        total = total + jnp.sum((nesterov * nesterov).reshape(32, 8, TILE), axis=0)
    squares_ref[...] = total[:, :128] + total[:, 128:256] + total[:, 256:384] + total[:, 384:]


def together(steps, v, *arrays):
    for axis, bit in steps:
        v = swap_add(v, axis, bit)
    return lax.optimization_barrier((v, *arrays))


def start_sum(far0, far1):
    return yhop(far0, 1), yhop(far1, -1)


def gather_near(own, v=None):
    if v is not None:
        v, own = lax.optimization_barrier((v, own))
    r3, l3 = yhop(own, 1), yhop(own, -1)
    if v is not None:
        v, r3, l3 = together([("row", 1)], v, r3, l3)
    return own, r3, l3, v


def gather_far(own, r3, l3, v=None):
    r4, l4 = yhop(r3[:128], 1), yhop(l3[128:], -1)
    if v is not None:
        v, r4, l4 = together([("row", 2)], v, r4, l4)
    return (own, r3, l3, r4, l4), v


def body(grad_partial, grad_scale, momentum):
    y = lax.axis_index("col").astype(jnp.int32).reshape(1)
    depth = lax.axis_index("depth").astype(jnp.int32)
    xl, c = depth // 2, depth % 2
    at = jnp.stack([c, xl])
    send0, send1, keep = scaled_parts(at, grad_partial, grad_scale)
    arrived = [sib(send0), sib(send1)]
    pairs = [
        call(
            functools.partial(pair_kernel, h),
            [at, keep, arrived[h]],
            [((256, TILE), BF16), ((256, TILE), F32)],
            1 << 20,
            name="pair",
        )
        for h in range(2)
    ]
    arrived = [inner(p[0]) for p in pairs]
    new_momentum, tile, v = call(
        momentum_kernel,
        [pairs[0][1], pairs[1][1], *arrived, momentum],
        [((TILE, TILE), F32), ((TILE, TILE), BF16), ((8, 128), F32)],
        1 << 20,
        name="momentum",
    )

    tile_s = sib(tile)

    def rows_of(half):
        start = (half * 2 + c) * PIECE
        return jnp.concatenate(
            [lax.dynamic_slice_in_dim(t, start, PIECE, 0) for t in (tile, tile_s)], axis=1
        )

    a = rows_of(xl)
    b = inner(rows_of(1 - xl))
    ra, la = zhop(a, 1), zhop(a, -1)
    t_out = outer(tile)
    v, b = together([("depth", 1)], v, b)
    r2 = zhop(jnp.concatenate([b, ra], axis=0), 1)
    l2 = zhop(jnp.concatenate([la, b], axis=0), -1)
    t_in = inner(lax.optimization_barrier((tile, b))[0])
    v, r2, l2, t_out = together([("col", 1)], v, r2, l2, t_out)
    v, t_in, r2, l2 = lax.optimization_barrier((v, t_in, r2, l2))
    r3, l3 = zhop(r2, 1), zhop(l2, -1)
    v, t_in, t_out, t_in_s, t_out_s = lax.optimization_barrier(
        (v, t_in, t_out, sib(t_in), sib(t_out))
    )
    far_a, far_b = outer(t_in[:256]), inner(t_out[256:])
    v, far_a, far_b = together([("col", 2)], v, far_a, far_b)
    r4_b, l4_b = zhop(r3[:128], 1), zhop(l3[128:], -1)
    r4_a = zhop(r3[128:], 1)
    l5_b = zhop(l4_b, -1)
    t_in, t_in_s, t_out, t_out_s = (in_hbm(t) for t in (t_in, t_in_s, t_out, t_out_s))
    tiles = [tile, tile_s, t_in, t_in_s, far_a, far_b, sib(far_a), sib(far_b), t_out, t_out_s]
    joined0, right0, left0, own0, far0, far1, panel = gram(
        y,
        tiles,
        [in_hbm(t) for t in (a, b, ra, la, r2, l2)] + [r3, l3],
        [
            [[(0, 0, 128)], [(1, 0, 128)]],
            [[(2, 0, 128)], [(4, 0, 128)]],
            [[(3, 0, 128)], [(5, 128, 128)]],
            [[(4, 128, 128)], [(6, 0, 128)]],
            [[(5, 0, 128)], [(7, 128, 128)]],
        ],
    )
    from_left0, from_right0 = start_sum(far0, far1)
    r4_b, l4_b, panel, from_left0 = lax.optimization_barrier((r4_b, l4_b, panel, from_left0))
    joined1, right1, left1, own1, far0, far1 = gram(
        y,
        [panel],
        [r3, l3, r4_b, l4_b],
        [[[(0, 128, 128)], [(2, 0, 128)]], [[(1, 0, 128)], [(3, 0, 128)]]],
    )
    r4_a, l5_b, from_left0, from_right0, far0, far1 = lax.optimization_barrier(
        (r4_a, l5_b, from_left0, from_right0, far0, far1)
    )
    from_left1, from_right1 = start_sum(far0, far1)
    joined2, right2, left2, own2, far2 = gram(
        y, [panel], [r4_a, l5_b], [[[(0, 0, 128)], [(1, 0, 128)]]], far_parts=1
    )
    right, left = call(
        near_kernel,
        [right0, right1, right2, left0, left1, left2]
        + [from_left0, from_left1, from_right0, from_right1],
        [((256, 1024), BF16)] * 2,
        1 << 20,
        name="near",
    )
    v, right, left = lax.optimization_barrier((v, right, left))
    from_left, from_right = yhop(right, 1), yhop(left, -1)
    from_far = lax.ppermute(far2, "col", [(i, i ^ 2) for i in range(4)])
    v, from_left, from_right = together([("depth", 2)], v, from_left, from_right)
    (own,) = call(
        own_kernel,
        [own0, own1, own2, from_left, from_right, from_far],
        [((256, 1024), BF16)],
        1 << 20,
        name="own",
    )
    whole_rows, v = gather_far(*gather_near(own, v))

    far, whole, theirs, mine = call(
        far_kernel,
        [y, *whole_rows, joined0, joined1, joined2],
        [((TILE, TILE), BF16), ((1024, 1024), BF16)] + [((2, 1024, TILE), BF16)] * 2,
        1 << 29,
        name="far",
    )
    far = sib(far)
    rest = call(rest_kernel, [whole, theirs], [((TILE, TILE), BF16)] * 3, 3 << 29, name="rest")
    rest = [sib(t) for t in rest]
    upper, lower = call(
        far_sum_kernel, [whole, mine, far], [((256, TILE), BF16)] * 2, 1 << 29, name="far_sum"
    )
    v, upper, lower = lax.optimization_barrier((v, upper, lower))
    a1, b1 = inner(upper), outer(lower)
    t_own, t_in, t_out = call(
        rest_sum_kernel,
        [whole, mine, *rest],
        [((TILE, TILE), F32)] + [((TILE, TILE), BF16)] * 2,
        3 << 29,
        name="rest_sum",
    )
    v, a1, b1 = together([("row", 4)], v, a1, b1)
    to_out = jnp.concatenate([add(t_out[:256], a1).astype(BF16), t_out[256:]], 0)
    to_in = jnp.concatenate([t_in[:256], add(t_in[256:], b1).astype(BF16)], 0)
    v, to_in, to_out = lax.optimization_barrier((v, to_in, to_out))
    from_in, from_out = inner(to_in), outer(to_out)
    v, from_in, from_out = together([("row", 8)], v, from_in, from_out)
    prod = add(t_own, from_in, from_out)

    gain = math.sqrt(M) / (1.5 * (jnp.sqrt(jnp.sum(v)) + EPSILON))
    update = math.sqrt(M) * (
        (1.5 * gain) * tile.astype(F32) - (0.5 * gain * gain * gain) * prod
    )
    return (new_momentum, update)


def solution(mesh):
    placed = (P("depth", "row", "col"), P("depth", "row", "col"), P("row", ("col", "depth")))
    return jax.shard_map(
        body,
        mesh=mesh,
        in_specs=placed,
        out_specs=(P("row", ("col", "depth")), P("row", ("col", "depth"))),
        check_vma=False,
    )
```

```python
import functools
import math

import jax
import jax.numpy as jnp
from jax import lax
from jax.experimental import pallas as pl
from jax.experimental.pallas import tpu as pltpu
from jax.sharding import PartitionSpec as P

M = 8192
BETA = 0.95
EPSILON = 1e-07
F32 = jnp.float32
BF16 = jnp.bfloat16

NY = 4
TILE = 512
PIECE = 128
ZPERM = {s: [(r, (r + 2 * s) % 16) for r in range(16)] for s in (1, -1)}
YPERM = {s: [(y, (y + s) % 4) for y in range(4)] for s in (1, -1)}
SIB = [(d, d ^ 1) for d in range(4)]
INNER = [(d, d ^ 2) for d in range(4)]
OUTER = [(r * 4 + d, (r ^ 1) * 4 + (d ^ 2)) for r in range(16) for d in range(4)]


def sib(v):
    return lax.ppermute(v, "depth", SIB)


def inner(v):
    return lax.ppermute(v, "depth", INNER)


def outer(v):
    return lax.ppermute(v, ("row", "depth"), OUTER)


def aside(v, k):
    pairs = []
    for r in range(16):
        for y in range(4):
            for d in range(4):
                other = r ^ 1 if (y + k) % 4 >= 2 else r
                pairs.append(((r * 4 + y) * 4 + d, (other * 4 + y) * 4 + (d ^ 2)))
    return lax.ppermute(v, ("row", "col", "depth"), pairs)


def across(v):
    return lax.ppermute(v, "row", [(r, r ^ 1) for r in range(16)])


def zhop(v, s):
    return lax.ppermute(v, "row", ZPERM[s])


def yhop(v, s):
    return lax.ppermute(v, "col", YPERM[s])


def in_hbm(v):
    return pltpu.with_memory_space_constraint(v, pltpu.HBM)


def swap_add(v, axis, bit):
    return v + lax.ppermute(v, axis, [(i, i ^ bit) for i in range(lax.axis_size(axis))])


def add(*vs):
    total = vs[0].astype(F32)
    for v in vs[1:]:
        total = total + v.astype(F32)
    return total


VMEM = pl.BlockSpec(memory_space=pltpu.VMEM)
SMEM = pl.BlockSpec(memory_space=pltpu.SMEM)
HBM = pl.BlockSpec(memory_space=pltpu.HBM)
ANY = pl.BlockSpec(memory_space=pl.ANY)


def gram_kernel(sources, with_panel, y_ref, *refs):
    n_tiles = 8 if with_panel else 1
    n_in = n_tiles + 1 + max(i for piece in sources for parts in piece for i, _, _ in parts)
    tiles, parts_in, outs = refs[:n_tiles], refs[n_tiles:n_in], list(refs[n_in:])
    held, sems = outs[-2:]
    joined, right, left, own, *far = outs[:-2]
    copies = []

    def copy(source, target):
        copies.append(pltpu.make_async_copy(source, target, sems.at[len(copies)]))
        copies[-1].start()

    for p, piece in enumerate(sources):
        for half, parts in enumerate(piece):
            row = p * PIECE
            for i, start, size in parts:
                copy(
                    parts_in[i].at[pl.ds(start, size)],
                    joined.at[pl.ds(row, size), pl.ds(half * 1024, 1024)],
                )
                row += size
    late = 0
    if with_panel:
        panel = far.pop()
        for i in range(4):
            copy(tiles[i], panel.at[pl.ds(0, TILE), pl.ds(i * TILE, TILE)])
        for i in range(4):
            copy(tiles[4 + i], panel.at[pl.ds(TILE, TILE), pl.ds(i * TILE, TILE)])
        late = -4
    else:
        panel = tiles[0]
    for c in copies[: late or None]:
        c.wait()
    y = y_ref[0]
    for block in range(4):
        if late and block == 2:
            for c in copies[late:]:
                c.wait()
        held[lax.rem(block + 4 - y, 4)] = lax.dot_general(
            panel[block * 256 : block * 256 + 256, :],
            joined[...],
            (((1,), (1,)), ((), ())),
            preferred_element_type=F32,
        ).astype(BF16)
    own[...] = held[0]
    right[...] = held[1]
    left[...] = held[3]
    rows = 256 // len(far)
    for i, out in enumerate(far):
        out[...] = held[2, i * rows : (i + 1) * rows]


def gram(y, tiles, arrays, sources, far_parts=2):
    n = len(sources) * PIECE
    with_panel = len(tiles) > 1
    shapes = [(n, 2048)] + [(256, n)] * 3 + [(256 // far_parts, n)] * far_parts
    n_copies = sum(len(parts) for piece in sources for parts in piece)
    if with_panel:
        shapes.append((1024, 2048))
        n_copies += 8
    return pl.pallas_call(
        functools.partial(gram_kernel, sources, with_panel),
        out_shape=[jax.ShapeDtypeStruct(s, BF16) for s in shapes],
        in_specs=[SMEM] + ([ANY] * 8 if with_panel else [VMEM]) + [ANY] * len(arrays),
        out_specs=[VMEM] * len(shapes),
        scratch_shapes=[
            pltpu.VMEM((4, 256, n), BF16),
            pltpu.SemaphoreType.DMA((n_copies,)),
        ],
        compiler_params=pltpu.CompilerParams(vmem_limit_bytes=8 << 20),
        cost_estimate=pl.CostEstimate(
            flops=2 * 1024 * 2048 * n, bytes_accessed=8 << 20, transcendentals=0
        ),
        name="gram",
    )(y, *tiles, *arrays)


def near_kernel(*refs):
    rights, lefts, from_left, from_right = refs[0:3], refs[3:6], refs[6:8], refs[8:10]
    to_right, to_left = refs[10:]
    at = 0
    for i in range(3):
        cols = slice(at, at + rights[i].shape[1])
        to_right[:, cols] = rights[i][...]
        to_left[:, cols] = lefts[i][...]
        if i < 2:
            to_right[:128, cols] = add(rights[i][:128, :], from_left[i][...]).astype(BF16)
            to_left[128:, cols] = add(lefts[i][128:, :], from_right[i][...]).astype(BF16)
        at = cols.stop


def own_kernel(own0, own1, own2, from_left, from_right, from_far, total):
    at = 0
    for i, own in enumerate((own0, own1, own2)):
        cols = slice(at, at + own.shape[1])
        value = add(own[...], from_left[:, cols], from_right[:, cols])
        if i == 2:
            value = value + from_far[...].astype(F32)
        total[:, cols] = value.astype(BF16)
        at = cols.stop


def split_kernel(joined0, joined1, joined2, mine, theirs):
    at = 0
    for joined in (joined0, joined1, joined2):
        size = joined.shape[0]
        for half in range(2):
            start = half * 1024
            mine[half, at : at + size, :] = joined[:, start : start + TILE]
            theirs[half, at : at + size, :] = joined[:, start + TILE : start + 2 * TILE]
        at += size


def early_kernel(own, from_right, from_left, inner_rows, out):
    for i, gram_rows in enumerate((own, from_right, from_left)):
        for half in range(2):
            out[i, half] = jnp.dot(
                gram_rows[...], inner_rows[half], preferred_element_type=F32
            ).astype(out.dtype)


def early_sum_kernel(y_ref, mine, arrived, side0, side1, side3, kept0, kept13, across):
    for i, side in enumerate((side0, side1, side3)):
        side[...] = (mine[i, 1] + arrived[i, 1].astype(F32)).astype(BF16)
    kept0[...] = mine[0, 0] + arrived[0, 0].astype(F32)
    goes = jnp.where(lax.rem(y_ref[0] + 1, 4) >= 2, 1, 2)
    across[...] = (mine[goes, 0] + arrived[goes, 0].astype(F32)).astype(BF16)
    kept13[...] = mine[3 - goes, 0] + arrived[3 - goes, 0].astype(F32)


def late_kernel(upper, lower, inner_rows, out):
    for half in range(2):
        for i, rows in enumerate((upper, lower)):
            out[half, i * 128 : i * 128 + 128, :] = jnp.dot(
                rows[...], inner_rows[half], preferred_element_type=F32
            ).astype(out.dtype)


def late_sum_kernel(y_ref, upper, lower, inner_rows, arrived, kept0, side2, kept02, across):
    def block(half):
        value = jnp.concatenate(
            [
                jnp.dot(rows[...], inner_rows[half], preferred_element_type=F32)
                for rows in (upper, lower)
            ],
            axis=0,
        )
        return value + arrived[half].astype(F32)

    near = block(0)
    side2[...] = block(1).astype(BF16)
    first_goes = y_ref[0] >= 2
    across[...] = jnp.where(first_goes, kept0[...], near).astype(BF16)
    kept02[...] = jnp.where(first_goes, near, kept0[...])


def call(kernel, operands, shapes, flops, limit=8, name=None):
    return pl.pallas_call(
        kernel,
        out_shape=[jax.ShapeDtypeStruct(*s) for s in shapes],
        in_specs=[SMEM if v.dtype == jnp.int32 else VMEM for v in operands],
        out_specs=[VMEM] * len(shapes),
        compiler_params=pltpu.CompilerParams(vmem_limit_bytes=limit << 20),
        cost_estimate=pl.CostEstimate(flops=flops, bytes_accessed=4 << 20, transcendentals=0),
        name=name,
    )(*operands)


def scaled_kernel(at_ref, q_ref, s_ref, send0, send1, keep, q_buf, s_buf, sems):
    c = at_ref[0]
    scales = pltpu.make_async_copy(s_ref.at[0], s_buf, sems.at[8])
    scales.start()
    copies = []
    for step in range(4):
        for side, core in enumerate((1 - c, c)):
            start = pl.multiple_of((step % 2 * 2 + core) * TILE, TILE)
            copies.append(
                pltpu.make_async_copy(
                    q_ref.at[0, pl.ds(step // 2 * 256, 256), pl.ds(start, TILE)],
                    q_buf.at[2 * step + side],
                    sems.at[2 * step + side],
                )
            )
            copies[-1].start()
    scales.wait()
    for step in range(4):
        for side, core in enumerate((1 - c, c)):
            copies[2 * step + side].wait()
            start = pl.multiple_of((step % 2 * 2 + core) * TILE, TILE)
            for r in range(2):
                rows = slice(r * 128, r * 128 + 128)
                row = step // 2 * 2 + r
                scale = s_buf[row : row + 1, pl.ds(start, TILE)]
                value = q_buf[2 * step + side, rows, :].astype(F32) * scale
                if side:
                    keep[step, rows, :] = value
                else:
                    (send0, send1)[step // 2][step % 2, rows, :] = value.astype(BF16)


def scaled_parts(at, quant, scale):
    return pl.pallas_call(
        scaled_kernel,
        in_specs=[SMEM, HBM, HBM],
        out_specs=[VMEM] * 3,
        out_shape=[
            jax.ShapeDtypeStruct((2, 256, TILE), BF16),
            jax.ShapeDtypeStruct((2, 256, TILE), BF16),
            jax.ShapeDtypeStruct((4, 256, TILE), F32),
        ],
        scratch_shapes=[
            pltpu.VMEM((8, 256, TILE), BF16),
            pltpu.VMEM((4, 4 * TILE), F32),
            pltpu.SemaphoreType.DMA((9,)),
        ],
        compiler_params=pltpu.CompilerParams(vmem_limit_bytes=8 << 20),
        name="scaled",
    )(at, in_hbm(quant), in_hbm(scale))


def pair_kernel(half, at_ref, keep, arrived, to_inner, kept):
    xl = at_ref[1]
    to_inner[...] = (keep[2 * half + 1 - xl] + arrived[1 - xl].astype(F32)).astype(BF16)
    kept[...] = keep[2 * half + xl] + arrived[xl].astype(F32)


def momentum_kernel(kept0, kept1, arrived0, arrived1, momentum, new_ref, tile_ref, squares_ref):
    total = jnp.zeros((8, TILE), F32)
    for half, (kept, arrived) in enumerate(((kept0, arrived0), (kept1, arrived1))):
        rows = slice(half * 256, half * 256 + 256)
        gradient = kept[...] + arrived[...].astype(F32)
        new = BETA * momentum[rows, :] + gradient
        nesterov = gradient + BETA * new
        new_ref[rows, :] = new
        tile_ref[rows, :] = nesterov.astype(BF16)
        total = total + jnp.sum((nesterov * nesterov).reshape(32, 8, TILE), axis=0)
    squares_ref[...] = total[:, :128] + total[:, 128:256] + total[:, 256:384] + total[:, 384:]


def together(steps, v, *arrays):
    for axis, bit in steps:
        v = swap_add(v, axis, bit)
    return lax.optimization_barrier((v, *arrays))


def start_sum(far0, far1):
    return yhop(far0, 1), yhop(far1, -1)


def body(grad_partial, grad_scale, momentum):
    y = lax.axis_index("col").astype(jnp.int32).reshape(1)
    depth = lax.axis_index("depth").astype(jnp.int32)
    xl, c = depth // 2, depth % 2
    at = jnp.stack([c, xl])
    send0, send1, keep = scaled_parts(at, grad_partial, grad_scale)
    arrived = [sib(send0), sib(send1)]
    pairs = [
        call(
            functools.partial(pair_kernel, h),
            [at, keep, arrived[h]],
            [((256, TILE), BF16), ((256, TILE), F32)],
            1 << 20,
            name="pair",
        )
        for h in range(2)
    ]
    arrived = [inner(p[0]) for p in pairs]
    new_momentum, tile, v = call(
        momentum_kernel,
        [pairs[0][1], pairs[1][1], *arrived, momentum],
        [((TILE, TILE), F32), ((TILE, TILE), BF16), ((8, 128), F32)],
        1 << 20,
        name="momentum",
    )

    tile_s = sib(tile)

    def rows_of(half):
        start = (half * 2 + c) * PIECE
        return jnp.concatenate(
            [lax.dynamic_slice_in_dim(t, start, PIECE, 0) for t in (tile, tile_s)], axis=1
        )

    a = rows_of(xl)
    b = inner(rows_of(1 - xl))
    ra, la = zhop(a, 1), zhop(a, -1)
    t_out = outer(tile)
    v, b = together([("depth", 1)], v, b)
    r2 = zhop(jnp.concatenate([b, ra], axis=0), 1)
    l2 = zhop(jnp.concatenate([la, b], axis=0), -1)
    later, b = lax.optimization_barrier((tile, b))
    t_in, t_far = inner(later), across(later)
    v, r2, l2, t_out = together([("col", 1), ("depth", 2)], v, r2, l2, t_out)
    v, t_in, r2, l2 = lax.optimization_barrier((v, t_in, r2, l2))
    r3, l3 = zhop(r2, 1), zhop(l2, -1)
    v, t_in, t_out, t_in_s, t_out_s = lax.optimization_barrier(
        (v, t_in, t_out, sib(t_in), sib(t_out))
    )
    v, r3, l3, t_far = together([("col", 2)], v, r3, l3, t_far)
    r4_b, l4_b = zhop(r3[:128], 1), zhop(l3[128:], -1)
    r4_a = zhop(r3[128:], 1)
    l5_b = zhop(l4_b, -1)
    t_in, t_in_s, t_out, t_out_s = (in_hbm(t) for t in (t_in, t_in_s, t_out, t_out_s))
    tiles = [tile, tile_s, t_in, t_in_s, t_far, sib(t_far), t_out, t_out_s]
    joined0, right0, left0, own0, far0, far1, panel = gram(
        y,
        tiles,
        [in_hbm(t) for t in (a, b, ra, la, r2, l2)] + [r3, l3],
        [
            [[(0, 0, 128)], [(1, 0, 128)]],
            [[(2, 0, 128)], [(4, 0, 128)]],
            [[(3, 0, 128)], [(5, 128, 128)]],
            [[(4, 128, 128)], [(6, 0, 128)]],
            [[(5, 0, 128)], [(7, 128, 128)]],
        ],
    )
    from_left0, from_right0 = start_sum(far0, far1)
    r4_b, l4_b, panel, from_left0 = lax.optimization_barrier((r4_b, l4_b, panel, from_left0))
    joined1, right1, left1, own1, far0, far1 = gram(
        y,
        [panel],
        [r3, l3, r4_b, l4_b],
        [[[(0, 128, 128)], [(2, 0, 128)]], [[(1, 0, 128)], [(3, 0, 128)]]],
    )
    r4_a, l5_b, from_left0, from_right0, far0, far1 = lax.optimization_barrier(
        (r4_a, l5_b, from_left0, from_right0, far0, far1)
    )
    from_left1, from_right1 = start_sum(far0, far1)
    joined2, right2, left2, own2, far2 = gram(
        y, [panel], [r4_a, l5_b], [[[(0, 0, 128)], [(1, 0, 128)]]], far_parts=1
    )
    right, left = call(
        near_kernel,
        [right0, right1, right2, left0, left1, left2]
        + [from_left0, from_left1, from_right0, from_right1],
        [((256, 1024), BF16)] * 2,
        1 << 20,
        name="near",
    )
    v, right, left = lax.optimization_barrier((v, right, left))
    from_left, from_right = yhop(right, 1), yhop(left, -1)
    from_far = lax.ppermute(far2, "col", [(i, i ^ 2) for i in range(4)])
    v, from_left, from_right = together([("row", 1)], v, from_left, from_right)
    (own,) = call(
        own_kernel,
        [own0, own1, own2, from_left, from_right, from_far],
        [((256, 1024), BF16)],
        1 << 20,
        name="own",
    )
    mine, theirs = call(
        split_kernel,
        [joined0, joined1, joined2],
        [((2, 1024, TILE), BF16)] * 2,
        1 << 20,
        name="split",
    )
    v, own = lax.optimization_barrier((v, own))
    r3, l3 = yhop(own, 1), yhop(own, -1)
    v, r3, l3 = together([("row", 2)], v, r3, l3)
    r4, l4 = yhop(r3[:128], 1), yhop(l3[128:], -1)

    (early_theirs,) = call(
        early_kernel, [own, l3, r3, theirs], [((3, 2, 256, TILE), BF16)], 3 << 29, name="early"
    )
    arrived = sib(early_theirs)
    (early_mine,) = call(
        early_kernel, [own, l3, r3, mine], [((3, 2, 256, TILE), F32)], 3 << 29, name="early"
    )
    block = ((256, TILE), BF16)
    wide = ((256, TILE), F32)
    side0, side1, side3, kept0, kept13, cross13 = call(
        early_sum_kernel,
        [y, early_mine, arrived],
        [block] * 3 + [wide] * 2 + [block],
        1 << 20,
        name="early_sum",
    )
    r4, l4, side1 = lax.optimization_barrier((r4, l4, side1))
    (late_theirs,) = call(
        late_kernel, [r4, l4, theirs], [((2, 256, TILE), BF16)], 1 << 29, name="late"
    )
    late_arrived = sib(late_theirs)
    side0, side1, side3, cross13 = aside(side0, 0), aside(side1, 1), aside(side3, 3), across(cross13)
    side2, kept02, cross02 = call(
        late_sum_kernel,
        [y, r4, l4, mine, late_arrived, kept0],
        [block, wide, block],
        1 << 29,
        name="late_sum",
    )
    v, side1, side3, side2, cross02 = lax.optimization_barrier((v, side1, side3, side2, cross02))
    side2, cross02 = aside(side2, 2), across(cross02)
    v = swap_add(v, "row", 4)
    v, side0, cross13 = lax.optimization_barrier((v, side0, cross13))
    v = swap_add(v, "row", 8)
    gain = math.sqrt(M) / (1.5 * (jnp.sqrt(jnp.sum(v)) + EPSILON))
    linear, cubic = math.sqrt(M) * 1.5 * gain, math.sqrt(M) * 0.5 * gain * gain * gain
    linear, cubic, side2, cross02 = lax.optimization_barrier((linear, cubic, side2, cross02))
    part02 = kept02 + add(side0, side2, cross02)
    part13 = kept13 + add(side1, side3, cross13)
    even = y[0] % 2 == 0
    prod = jnp.concatenate(
        [jnp.where(even, part02, part13), jnp.where(even, part13, part02)], axis=0
    )
    update = linear * tile.astype(F32) - cubic * prod
    return (new_momentum, update)


def solution(mesh):
    placed = (P("depth", "row", "col"), P("depth", "row", "col"), P("row", ("col", "depth")))
    return jax.shard_map(
        body,
        mesh=mesh,
        in_specs=placed,
        out_specs=(P("row", ("col", "depth")), P("row", ("col", "depth"))),
        check_vma=False,
    )
```

```python
import functools
import math

import jax
import jax.numpy as jnp
from jax import lax
from jax.experimental import pallas as pl
from jax.experimental.pallas import tpu as pltpu
from jax.sharding import PartitionSpec as P

M = 8192
BETA = 0.95
EPSILON = 1e-07
F32 = jnp.float32
BF16 = jnp.bfloat16

NY = 4
TILE = 512
PIECE = 128
ZPERM = {s: [(r, (r + 2 * s) % 16) for r in range(16)] for s in (1, -1)}
YPERM = {s: [(y, (y + s) % 4) for y in range(4)] for s in (1, -1)}
SIB = [(d, d ^ 1) for d in range(4)]
INNER = [(d, d ^ 2) for d in range(4)]
OUTER = [(r * 4 + d, (r ^ 1) * 4 + (d ^ 2)) for r in range(16) for d in range(4)]


def sib(v):
    return lax.ppermute(v, "depth", SIB)


def inner(v):
    return lax.ppermute(v, "depth", INNER)


def outer(v):
    return lax.ppermute(v, ("row", "depth"), OUTER)


def across(v):
    return lax.ppermute(v, "row", [(r, r ^ 1) for r in range(16)])


def zhop(v, s):
    return lax.ppermute(v, "row", ZPERM[s])


def yhop(v, s):
    return lax.ppermute(v, "col", YPERM[s])


def in_hbm(v):
    return pltpu.with_memory_space_constraint(v, pltpu.HBM)


def mixed(v, first):
    step = {0: -1, 1: 1} if first else {0: 1, 1: -1}
    pairs = [(y * 4 + d, (y + step[d % 2]) % 4 * 4 + d) for y in range(4) for d in range(4)]
    return lax.ppermute(v, ("col", "depth"), pairs)


def opposite(v):
    return lax.ppermute(v, "col", [(y, y ^ 2) for y in range(4)])


def swap_add(v, axis, bit):
    return v + lax.ppermute(v, axis, [(i, i ^ bit) for i in range(lax.axis_size(axis))])


def add(*vs):
    total = vs[0].astype(F32)
    for v in vs[1:]:
        total = total + v.astype(F32)
    return total


VMEM = pl.BlockSpec(memory_space=pltpu.VMEM)
SMEM = pl.BlockSpec(memory_space=pltpu.SMEM)
HBM = pl.BlockSpec(memory_space=pltpu.HBM)
ANY = pl.BlockSpec(memory_space=pl.ANY)


def gram_kernel(sources, with_panel, at_ref, *refs):
    n_tiles = 10 if with_panel else 1
    n_in = n_tiles + 1 + max(i for piece in sources for parts in piece for i, _, _ in parts)
    tiles, parts_in, rest = refs[:n_tiles], refs[n_tiles:n_in], list(refs[n_in:])
    held, sems = rest[-2:]
    before = rest[: 4 if len(sources) == 1 else 0]
    joined, near, own, far, *panel_out = rest[len(before) : -2]
    copies = []

    def copy(source, target):
        copies.append(pltpu.make_async_copy(source, target, sems.at[len(copies)]))
        copies[-1].start()

    for p, piece in enumerate(sources):
        for half, parts in enumerate(piece):
            row = p * PIECE
            for i, start, size in parts:
                copy(
                    parts_in[i].at[pl.ds(start, size)],
                    joined.at[pl.ds(row, size), pl.ds(half * 1024, 1024)],
                )
                row += size
    late = 0
    if with_panel:
        panel = panel_out[0]
        for i in range(4):
            copy(tiles[i], panel.at[pl.ds(0, TILE), pl.ds(i * TILE, TILE)])
        late = len(copies)
        for i in range(2):
            for part in range(2):
                copy(
                    tiles[4 + 2 * i + part],
                    panel.at[pl.ds(TILE + 256 * part, 256), pl.ds(i * TILE, TILE)],
                )
            copy(tiles[8 + i], panel.at[pl.ds(TILE, TILE), pl.ds((2 + i) * TILE, TILE)])
        late -= len(copies)
    else:
        panel = tiles[0]
    for c in copies[: late or None]:
        c.wait()
    y, core = at_ref[0], at_ref[1]
    at = 0
    for near_before, own_before in zip(before[0::2], before[1::2]):
        cols = slice(at, at + own_before.shape[1])
        near[:, :, cols] = near_before[...]
        own[:, cols] = own_before[...]
        at = cols.stop
    for block in range(4):
        if late and block == 2:
            for c in copies[late:]:
                c.wait()
        held[lax.rem(block + 4 - y, 4)] = lax.dot_general(
            panel[block * 256 : block * 256 + 256, :],
            joined[...],
            (((1,), (1,)), ((), ())),
            preferred_element_type=F32,
        ).astype(BF16)
    own[:, at:] = held[0]
    far[...] = held[2]
    near[0, :, at:] = held[3 - 2 * core]
    near[1, :, at:] = held[1 + 2 * core]


def gram(at, tiles, arrays, sources, before=()):
    n = len(sources) * PIECE
    wide = n + sum(v.shape[1] for v in before[1::2])
    with_panel = len(tiles) > 1
    shapes = [(n, 2048), (2, 256, wide), (256, wide), (256, n)]
    n_copies = sum(len(parts) for piece in sources for parts in piece)
    if with_panel:
        shapes.append((1024, 2048))
        n_copies += 10
    return pl.pallas_call(
        functools.partial(gram_kernel, sources, with_panel),
        out_shape=[jax.ShapeDtypeStruct(s, BF16) for s in shapes],
        in_specs=[SMEM]
        + ([ANY] * 10 if with_panel else [VMEM])
        + [ANY] * len(arrays)
        + [VMEM] * len(before),
        out_specs=[VMEM] * len(shapes),
        scratch_shapes=[
            pltpu.VMEM((4, 256, n), BF16),
            pltpu.SemaphoreType.DMA((n_copies,)),
        ],
        compiler_params=pltpu.CompilerParams(vmem_limit_bytes=8 << 20),
        cost_estimate=pl.CostEstimate(
            flops=2 * 1024 * 2048 * n, bytes_accessed=8 << 20, transcendentals=0
        ),
        name="gram",
    )(at, *tiles, *arrays, *before)


def own_kernel(own, first, second, far0, far1, far2, total):
    at = 0
    for far in (far0, far1, far2):
        cols = slice(at, at + far.shape[1])
        total[:, cols] = add(own[:, cols], first[:, cols], second[:, cols], far[...]).astype(BF16)
        at = cols.stop


def far_kernel(at_ref, own, first, second, far_first, far_second, joined0, joined1, joined2, far, whole, theirs, mine):
    y, core = at_ref[0], at_ref[1]

    def rows(k):
        return pl.multiple_of(lax.rem(y + k, 4) * 256, 256)

    for k, part in ((0, own), (1 + 2 * core, first), (3 - 2 * core, second)):
        whole[pl.ds(rows(k), 256), :] = part[...]
    for offset, part in ((1 - core, far_first), (core, far_second)):
        whole[pl.ds(pl.multiple_of(rows(2) + 128 * offset, 128), 128), :] = part[...]
    at = 0
    for joined in (joined0, joined1, joined2):
        size = joined.shape[0]
        for half in range(2):
            start = half * 1024
            mine[half, at : at + size, :] = joined[:, start : start + TILE]
            theirs[half, at : at + size, :] = joined[:, start + TILE : start + 2 * TILE]
        at += size
    far[...] = jnp.dot(whole[512:], theirs[0], preferred_element_type=F32).astype(BF16)


def rest_kernel(whole, theirs, own, near, out):
    own[...] = jnp.dot(whole[:512], theirs[0], preferred_element_type=F32).astype(BF16)
    near[...] = jnp.dot(whole[:512], theirs[1], preferred_element_type=F32).astype(BF16)
    out[...] = jnp.dot(whole[512:], theirs[1], preferred_element_type=F32).astype(BF16)


def far_sum_kernel(whole, mine, arrived, upper, lower):
    total = jnp.dot(whole[512:], mine[0], preferred_element_type=F32) + arrived[...].astype(F32)
    upper[...] = total[:256].astype(BF16)
    lower[...] = total[256:].astype(BF16)


def rest_sum_kernel(whole, mine, a_own, a_near, a_out, own, near, out):
    def term(rows, half, arrived):
        return jnp.dot(whole[rows], mine[half], preferred_element_type=F32) + arrived[...].astype(F32)

    own[...] = term(slice(0, 512), 0, a_own)
    near[...] = term(slice(0, 512), 1, a_near).astype(BF16)
    out[...] = term(slice(512, 1024), 1, a_out).astype(BF16)


def call(kernel, operands, shapes, flops, limit=8, name=None):
    return pl.pallas_call(
        kernel,
        out_shape=[jax.ShapeDtypeStruct(*s) for s in shapes],
        in_specs=[SMEM if v.dtype == jnp.int32 else VMEM for v in operands],
        out_specs=[VMEM] * len(shapes),
        compiler_params=pltpu.CompilerParams(vmem_limit_bytes=limit << 20),
        cost_estimate=pl.CostEstimate(flops=flops, bytes_accessed=4 << 20, transcendentals=0),
        name=name,
    )(*operands)


def scaled_kernel(at_ref, q_ref, s_ref, send0, send1, keep, q_buf, s_buf, sems):
    c = at_ref[0]
    scales = pltpu.make_async_copy(s_ref.at[0], s_buf, sems.at[8])
    scales.start()
    copies = []
    for step in range(4):
        for side, core in enumerate((1 - c, c)):
            start = pl.multiple_of((step % 2 * 2 + core) * TILE, TILE)
            copies.append(
                pltpu.make_async_copy(
                    q_ref.at[0, pl.ds(step // 2 * 256, 256), pl.ds(start, TILE)],
                    q_buf.at[2 * step + side],
                    sems.at[2 * step + side],
                )
            )
            copies[-1].start()
    scales.wait()
    for step in range(4):
        for side, core in enumerate((1 - c, c)):
            copies[2 * step + side].wait()
            start = pl.multiple_of((step % 2 * 2 + core) * TILE, TILE)
            for r in range(2):
                rows = slice(r * 128, r * 128 + 128)
                row = step // 2 * 2 + r
                scale = s_buf[row : row + 1, pl.ds(start, TILE)]
                value = q_buf[2 * step + side, rows, :].astype(F32) * scale
                if side:
                    keep[step, rows, :] = value
                else:
                    (send0, send1)[step // 2][step % 2, rows, :] = value.astype(BF16)


def scaled_parts(at, quant, scale):
    return pl.pallas_call(
        scaled_kernel,
        in_specs=[SMEM, HBM, HBM],
        out_specs=[VMEM] * 3,
        out_shape=[
            jax.ShapeDtypeStruct((2, 256, TILE), BF16),
            jax.ShapeDtypeStruct((2, 256, TILE), BF16),
            jax.ShapeDtypeStruct((4, 256, TILE), F32),
        ],
        scratch_shapes=[
            pltpu.VMEM((8, 256, TILE), BF16),
            pltpu.VMEM((4, 4 * TILE), F32),
            pltpu.SemaphoreType.DMA((9,)),
        ],
        compiler_params=pltpu.CompilerParams(vmem_limit_bytes=8 << 20),
        name="scaled",
    )(at, in_hbm(quant), in_hbm(scale))


def pair_kernel(half, at_ref, keep, arrived, to_inner, kept):
    xl = at_ref[1]
    to_inner[...] = (keep[2 * half + 1 - xl] + arrived[1 - xl].astype(F32)).astype(BF16)
    kept[...] = keep[2 * half + xl] + arrived[xl].astype(F32)


def momentum_kernel(kept0, kept1, arrived0, arrived1, momentum, new_ref, tile_ref, squares_ref):
    total = jnp.zeros((8, TILE), F32)
    for half, (kept, arrived) in enumerate(((kept0, arrived0), (kept1, arrived1))):
        rows = slice(half * 256, half * 256 + 256)
        gradient = kept[...] + arrived[...].astype(F32)
        new = BETA * momentum[rows, :] + gradient
        nesterov = gradient + BETA * new
        new_ref[rows, :] = new
        tile_ref[rows, :] = nesterov.astype(BF16)
        total = total + jnp.sum((nesterov * nesterov).reshape(32, 8, TILE), axis=0)
    squares_ref[...] = total[:, :128] + total[:, 128:256] + total[:, 256:384] + total[:, 384:]


def together(steps, v, *arrays):
    for axis, bit in steps:
        v = swap_add(v, axis, bit)
    return lax.optimization_barrier((v, *arrays))


def body(grad_partial, grad_scale, momentum):
    y = lax.axis_index("col").astype(jnp.int32).reshape(1)
    depth = lax.axis_index("depth").astype(jnp.int32)
    xl, c = depth // 2, depth % 2
    at = jnp.stack([c, xl])
    place = jnp.stack([y[0], c])
    send0, send1, keep = scaled_parts(at, grad_partial, grad_scale)
    arrived = [sib(send0), sib(send1)]
    pairs = [
        call(
            functools.partial(pair_kernel, h),
            [at, keep, arrived[h]],
            [((256, TILE), BF16), ((256, TILE), F32)],
            1 << 20,
            name="pair",
        )
        for h in range(2)
    ]
    arrived = [inner(p[0]) for p in pairs]
    new_momentum, tile, v = call(
        momentum_kernel,
        [pairs[0][1], pairs[1][1], *arrived, momentum],
        [((TILE, TILE), F32), ((TILE, TILE), BF16), ((8, 128), F32)],
        1 << 20,
        name="momentum",
    )

    tile_s = sib(tile)

    def rows_of(half):
        start = (half * 2 + c) * PIECE
        return jnp.concatenate(
            [lax.dynamic_slice_in_dim(t, start, PIECE, 0) for t in (tile, tile_s)], axis=1
        )

    a = rows_of(xl)
    b = inner(rows_of(1 - xl))
    ra, la = zhop(a, 1), zhop(a, -1)
    t_out = outer(tile)
    v, b = together([("depth", 1)], v, b)
    r2 = zhop(jnp.concatenate([b, ra], axis=0), 1)
    l2 = zhop(jnp.concatenate([la, b], axis=0), -1)
    t_in = inner(lax.optimization_barrier((tile, b))[0])
    v, r2, l2, t_out = together([("col", 1)], v, r2, l2, t_out)
    v, t_in, r2, l2 = lax.optimization_barrier((v, t_in, r2, l2))
    r3, l3 = zhop(r2, 1), zhop(l2, -1)
    v, t_in, t_out, t_in_s, t_out_s = lax.optimization_barrier(
        (v, t_in, t_out, sib(t_in), sib(t_out))
    )
    far_a, far_b = outer(t_in[:256]), inner(t_out[256:])
    v, r3, l3 = together([("col", 2)], v, r3, l3)
    r4_b, l4_b = zhop(r3[:128], 1), zhop(l3[128:], -1)
    r4_a = zhop(r3[128:], 1)
    l5_b = zhop(l4_b, -1)
    t_in, t_in_s, t_out, t_out_s = (in_hbm(t) for t in (t_in, t_in_s, t_out, t_out_s))
    tiles = [tile, tile_s, t_in, t_in_s, far_a, far_b, sib(far_a), sib(far_b), t_out, t_out_s]
    joined0, near0, own0, far0, panel = gram(
        place,
        tiles,
        [in_hbm(t) for t in (a, b, ra, la, r2, l2)] + [r3, l3],
        [
            [[(0, 0, 128)], [(1, 0, 128)]],
            [[(2, 0, 128)], [(4, 0, 128)]],
            [[(3, 0, 128)], [(5, 128, 128)]],
            [[(4, 128, 128)], [(6, 0, 128)]],
            [[(5, 0, 128)], [(7, 128, 128)]],
        ],
    )
    far0 = opposite(far0)
    r4_b, l4_b, panel = lax.optimization_barrier((r4_b, l4_b, panel))
    joined1, near1, own1, far1 = gram(
        place,
        [panel],
        [r3, l3, r4_b, l4_b],
        [[[(0, 128, 128)], [(2, 0, 128)]], [[(1, 0, 128)], [(3, 0, 128)]]],
    )
    r4_a, l5_b, far0, far1 = lax.optimization_barrier((r4_a, l5_b, far0, far1))
    far1 = opposite(far1)
    joined2, near, own, far2 = gram(
        place,
        [panel],
        [r4_a, l5_b],
        [[[(0, 0, 128)], [(1, 0, 128)]]],
        [near0, own0, near1, own1],
    )
    v, near, far1 = lax.optimization_barrier((v, near, far1))
    first, second, far2 = mixed(near[0], True), mixed(near[1], False), opposite(far2)
    v, first, second = together([("depth", 2)], v, first, second)
    (own,) = call(
        own_kernel,
        [own, first, second, far0, far1, far2],
        [((256, 1024), BF16)],
        1 << 20,
        name="own",
    )
    v, own = lax.optimization_barrier((v, own))
    first, second = mixed(own, True), mixed(own, False)
    v, first, second = together([("row", 1)], v, first, second)
    far_first = mixed(lax.dynamic_slice_in_dim(first, 128 * (1 - c), 128, 0), True)
    far_second = mixed(lax.dynamic_slice_in_dim(second, 128 * c, 128, 0), False)
    v, far_first, far_second = together([("row", 2)], v, far_first, far_second)

    far, whole, theirs, mine = call(
        far_kernel,
        [place, own, first, second, far_first, far_second, joined0, joined1, joined2],
        [((TILE, TILE), BF16), ((1024, 1024), BF16)] + [((2, 1024, TILE), BF16)] * 2,
        1 << 29,
        name="far",
    )
    far = sib(far)
    rest = call(rest_kernel, [whole, theirs], [((TILE, TILE), BF16)] * 3, 3 << 29, name="rest")
    rest = [sib(t) for t in rest]
    upper, lower = call(
        far_sum_kernel, [whole, mine, far], [((256, TILE), BF16)] * 2, 1 << 29, name="far_sum"
    )
    v, upper, lower = lax.optimization_barrier((v, upper, lower))
    a1, b1 = inner(upper), outer(lower)
    t_own, t_in, t_out = call(
        rest_sum_kernel,
        [whole, mine, *rest],
        [((TILE, TILE), F32)] + [((TILE, TILE), BF16)] * 2,
        3 << 29,
        name="rest_sum",
    )
    v, a1, b1 = together([("row", 4)], v, a1, b1)
    to_out = jnp.concatenate([add(t_out[:256], a1).astype(BF16), t_out[256:]], 0)
    to_in = jnp.concatenate([t_in[:256], add(t_in[256:], b1).astype(BF16)], 0)
    v, to_in, to_out = lax.optimization_barrier((v, to_in, to_out))
    from_in, from_out = inner(to_in), outer(to_out)
    v = swap_add(v, "row", 8)
    gain = math.sqrt(M) / (1.5 * (jnp.sqrt(jnp.sum(v)) + EPSILON))
    linear, cubic = math.sqrt(M) * 1.5 * gain, math.sqrt(M) * 0.5 * gain * gain * gain
    linear, cubic, from_in, from_out = lax.optimization_barrier((linear, cubic, from_in, from_out))
    prod = add(t_own, from_in, from_out)
    update = linear * tile.astype(F32) - cubic * prod
    return (new_momentum, update)


def solution(mesh):
    placed = (P("depth", "row", "col"), P("depth", "row", "col"), P("row", ("col", "depth")))
    return jax.shard_map(
        body,
        mesh=mesh,
        in_specs=placed,
        out_specs=(P("row", ("col", "depth")), P("row", ("col", "depth"))),
        check_vma=False,
    )
```

```python
import functools
import math

import jax
import jax.numpy as jnp
from jax import lax
from jax.experimental import pallas as pl
from jax.experimental.pallas import tpu as pltpu
from jax.sharding import PartitionSpec as P

M = 8192
BETA = 0.95
EPSILON = 1e-07
F32 = jnp.float32
BF16 = jnp.bfloat16

NY = 4
TILE = 512
PIECE = 128
ZPERM = {s: [(r, (r + 2 * s) % 16) for r in range(16)] for s in (1, -1)}
YPERM = {s: [(y, (y + s) % 4) for y in range(4)] for s in (1, -1)}
SIB = [(d, d ^ 1) for d in range(4)]
INNER = [(d, d ^ 2) for d in range(4)]
OUTER = [(r * 4 + d, (r ^ 1) * 4 + (d ^ 2)) for r in range(16) for d in range(4)]


def sib(v):
    return lax.ppermute(v, "depth", SIB)


def inner(v):
    return lax.ppermute(v, "depth", INNER)


def outer(v):
    return lax.ppermute(v, ("row", "depth"), OUTER)


def across(v):
    return lax.ppermute(v, "row", [(r, r ^ 1) for r in range(16)])


def zhop(v, s):
    return lax.ppermute(v, "row", ZPERM[s])


def yhop(v, s):
    return lax.ppermute(v, "col", YPERM[s])


def in_hbm(v):
    return pltpu.with_memory_space_constraint(v, pltpu.HBM)


def mixed(v, first):
    step = {0: -1, 1: 1} if first else {0: 1, 1: -1}
    pairs = [(y * 4 + d, (y + step[d % 2]) % 4 * 4 + d) for y in range(4) for d in range(4)]
    return lax.ppermute(v, ("col", "depth"), pairs)


def opposite(v):
    return lax.ppermute(v, "col", [(y, y ^ 2) for y in range(4)])


def swap_add(v, axis, bit):
    return v + lax.ppermute(v, axis, [(i, i ^ bit) for i in range(lax.axis_size(axis))])


def add(*vs):
    total = vs[0].astype(F32)
    for v in vs[1:]:
        total = total + v.astype(F32)
    return total


VMEM = pl.BlockSpec(memory_space=pltpu.VMEM)
SMEM = pl.BlockSpec(memory_space=pltpu.SMEM)
HBM = pl.BlockSpec(memory_space=pltpu.HBM)
ANY = pl.BlockSpec(memory_space=pl.ANY)


def gram_kernel(sources, with_panel, at_ref, *refs):
    n_tiles = 10 if with_panel else 1
    n_in = n_tiles + 1 + max(i for piece in sources for parts in piece for i, _, _ in parts)
    tiles, parts_in, rest = refs[:n_tiles], refs[n_tiles:n_in], list(refs[n_in:])
    held, sems = rest[-2:]
    before = rest[: 4 if len(sources) == 1 else 0]
    joined, near, own, far, *panel_out = rest[len(before) : -2]
    copies = []

    def copy(source, target):
        copies.append(pltpu.make_async_copy(source, target, sems.at[len(copies)]))
        copies[-1].start()

    for p, piece in enumerate(sources):
        for half, parts in enumerate(piece):
            row = p * PIECE
            for i, start, size in parts:
                copy(
                    parts_in[i].at[pl.ds(start, size)],
                    joined.at[pl.ds(row, size), pl.ds(half * 1024, 1024)],
                )
                row += size
    late = 0
    if with_panel:
        panel = panel_out[0]
        for i in range(4):
            copy(tiles[i], panel.at[pl.ds(0, TILE), pl.ds(i * TILE, TILE)])
        late = len(copies)
        for i in range(2):
            for part in range(2):
                copy(
                    tiles[4 + 2 * i + part],
                    panel.at[pl.ds(TILE + 256 * part, 256), pl.ds(i * TILE, TILE)],
                )
            copy(tiles[8 + i], panel.at[pl.ds(TILE, TILE), pl.ds((2 + i) * TILE, TILE)])
        late -= len(copies)
    else:
        panel = tiles[0]
    for c in copies[: late or None]:
        c.wait()
    y, core = at_ref[2], at_ref[0]
    at = 0
    for near_before, own_before in zip(before[0::2], before[1::2]):
        cols = slice(at, at + own_before.shape[1])
        near[:, :, cols] = near_before[...]
        own[:, cols] = own_before[...]
        at = cols.stop
    for block in range(4):
        if late and block == 2:
            for c in copies[late:]:
                c.wait()
        held[lax.rem(block + 4 - y, 4)] = lax.dot_general(
            panel[block * 256 : block * 256 + 256, :],
            joined[...],
            (((1,), (1,)), ((), ())),
            preferred_element_type=F32,
        ).astype(BF16)
    own[:, at:] = held[0]
    far[...] = held[2]
    near[0, :, at:] = held[3 - 2 * core]
    near[1, :, at:] = held[1 + 2 * core]


def gram(at, tiles, arrays, sources, before=()):
    n = len(sources) * PIECE
    wide = n + sum(v.shape[1] for v in before[1::2])
    with_panel = len(tiles) > 1
    shapes = [(n, 2048), (2, 256, wide), (256, wide), (256, n)]
    n_copies = sum(len(parts) for piece in sources for parts in piece)
    if with_panel:
        shapes.append((1024, 2048))
        n_copies += 10
    return pl.pallas_call(
        functools.partial(gram_kernel, sources, with_panel),
        out_shape=[jax.ShapeDtypeStruct(s, BF16) for s in shapes],
        in_specs=[SMEM]
        + ([ANY] * 10 if with_panel else [VMEM])
        + [ANY] * len(arrays)
        + [VMEM] * len(before),
        out_specs=[VMEM] * len(shapes),
        scratch_shapes=[
            pltpu.VMEM((4, 256, n), BF16),
            pltpu.SemaphoreType.DMA((n_copies,)),
        ],
        compiler_params=pltpu.CompilerParams(vmem_limit_bytes=8 << 20),
        cost_estimate=pl.CostEstimate(
            flops=2 * 1024 * 2048 * n, bytes_accessed=8 << 20, transcendentals=0
        ),
        name="gram",
    )(at, *tiles, *arrays, *before)


def own_kernel(own, first, second, far0, far1, far2, total):
    at = 0
    for far in (far0, far1, far2):
        cols = slice(at, at + far.shape[1])
        total[:, cols] = add(own[:, cols], first[:, cols], second[:, cols], far[...]).astype(BF16)
        at = cols.stop


def far_kernel(at_ref, own, first, second, far_first, far_second, joined0, joined1, joined2, far, whole, theirs, mine):
    y, core = at_ref[2], at_ref[0]

    def rows(k):
        return pl.multiple_of(lax.rem(y + k, 4) * 256, 256)

    for k, part in ((0, own), (1 + 2 * core, first), (3 - 2 * core, second)):
        whole[pl.ds(rows(k), 256), :] = part[...]
    for offset, part in ((1 - core, far_first), (core, far_second)):
        whole[pl.ds(pl.multiple_of(rows(2) + 128 * offset, 128), 128), :] = part[...]
    at = 0
    for joined in (joined0, joined1, joined2):
        size = joined.shape[0]
        for half in range(2):
            start = half * 1024
            mine[half, at : at + size, :] = joined[:, start : start + TILE]
            theirs[half, at : at + size, :] = joined[:, start + TILE : start + 2 * TILE]
        at += size
    far[...] = jnp.dot(whole[512:], theirs[0], preferred_element_type=F32).astype(BF16)


def rest_kernel(whole, theirs, own, near, out):
    own[...] = jnp.dot(whole[:512], theirs[0], preferred_element_type=F32).astype(BF16)
    near[...] = jnp.dot(whole[:512], theirs[1], preferred_element_type=F32).astype(BF16)
    out[...] = jnp.dot(whole[512:], theirs[1], preferred_element_type=F32).astype(BF16)


def far_sum_kernel(whole, mine, arrived, upper, lower):
    total = jnp.dot(whole[512:], mine[0], preferred_element_type=F32) + arrived[...].astype(F32)
    upper[...] = total[:256].astype(BF16)
    lower[...] = total[256:].astype(BF16)


def rest_sum_kernel(whole, mine, a_own, a_near, a_out, own, near, out):
    def term(rows, half, arrived):
        return jnp.dot(whole[rows], mine[half], preferred_element_type=F32) + arrived[...].astype(F32)

    own[...] = term(slice(0, 512), 0, a_own)
    near[...] = term(slice(0, 512), 1, a_near).astype(BF16)
    out[...] = term(slice(512, 1024), 1, a_out).astype(BF16)


def call(kernel, operands, shapes, flops, limit=8, name=None):
    return pl.pallas_call(
        kernel,
        out_shape=[jax.ShapeDtypeStruct(*s) for s in shapes],
        in_specs=[SMEM if v.dtype == jnp.int32 else VMEM for v in operands],
        out_specs=[VMEM] * len(shapes),
        compiler_params=pltpu.CompilerParams(vmem_limit_bytes=limit << 20),
        cost_estimate=pl.CostEstimate(flops=flops, bytes_accessed=4 << 20, transcendentals=0),
        name=name,
    )(*operands)


def scaled_kernel(at_ref, q_ref, s_ref, send0, send1, keep, q_buf, s_buf, sems):
    c = at_ref[0]
    scales = pltpu.make_async_copy(s_ref.at[0], s_buf, sems.at[8])
    scales.start()
    copies = []
    for step in range(4):
        for side, core in enumerate((1 - c, c)):
            start = pl.multiple_of((step % 2 * 2 + core) * TILE, TILE)
            copies.append(
                pltpu.make_async_copy(
                    q_ref.at[0, pl.ds(step // 2 * 256, 256), pl.ds(start, TILE)],
                    q_buf.at[2 * step + side],
                    sems.at[2 * step + side],
                )
            )
            copies[-1].start()
    scales.wait()
    for step in range(4):
        for side, core in enumerate((1 - c, c)):
            copies[2 * step + side].wait()
            start = pl.multiple_of((step % 2 * 2 + core) * TILE, TILE)
            for r in range(2):
                rows = slice(r * 128, r * 128 + 128)
                row = step // 2 * 2 + r
                scale = s_buf[row : row + 1, pl.ds(start, TILE)]
                value = q_buf[2 * step + side, rows, :].astype(F32) * scale
                if side:
                    keep[step, rows, :] = value
                else:
                    (send0, send1)[step // 2][step % 2, rows, :] = value.astype(BF16)


def scaled_parts(at, quant, scale):
    return pl.pallas_call(
        scaled_kernel,
        in_specs=[SMEM, HBM, HBM],
        out_specs=[VMEM] * 3,
        out_shape=[
            jax.ShapeDtypeStruct((2, 256, TILE), BF16),
            jax.ShapeDtypeStruct((2, 256, TILE), BF16),
            jax.ShapeDtypeStruct((4, 256, TILE), F32),
        ],
        scratch_shapes=[
            pltpu.VMEM((8, 256, TILE), BF16),
            pltpu.VMEM((4, 4 * TILE), F32),
            pltpu.SemaphoreType.DMA((9,)),
        ],
        compiler_params=pltpu.CompilerParams(vmem_limit_bytes=8 << 20),
        name="scaled",
    )(at, in_hbm(quant), in_hbm(scale))


def pair_kernel(half, at_ref, keep, arrived, to_inner, kept):
    xl = at_ref[1]
    to_inner[...] = (keep[2 * half + 1 - xl] + arrived[1 - xl].astype(F32)).astype(BF16)
    kept[...] = keep[2 * half + xl] + arrived[xl].astype(F32)


def pieces_kernel(at_ref, tile, tile_s, kept, sent):
    core, xl = at_ref[0], at_ref[1]
    for out, half in ((kept, xl), (sent, 1 - xl)):
        rows = pl.ds(pl.multiple_of((2 * half + core) * PIECE, PIECE), PIECE)
        out[:, :TILE] = tile[rows, :]
        out[:, TILE:] = tile_s[rows, :]


def halves_kernel(at_ref, first, second, far_first, far_second):
    core = at_ref[0]
    far_first[...] = first[pl.ds(pl.multiple_of(128 * (1 - core), 128), 128), :]
    far_second[...] = second[pl.ds(pl.multiple_of(128 * core, 128), 128), :]


def update_kernel(squares, tile, own, from_in, from_out, update):
    total = jnp.sum(jnp.sum(squares[...], axis=1, keepdims=True), axis=0, keepdims=True)
    gain = math.sqrt(M) / (1.5 * (jnp.sqrt(total) + EPSILON))
    linear, cubic = (math.sqrt(M) * 1.5) * gain, (math.sqrt(M) * 0.5) * gain * gain * gain
    product = add(own[...], from_in[...], from_out[...])
    update[...] = linear * tile[...].astype(F32) - cubic * product


def momentum_kernel(kept0, kept1, arrived0, arrived1, momentum, new_ref, tile_ref, squares_ref):
    total = jnp.zeros((8, TILE), F32)
    for half, (kept, arrived) in enumerate(((kept0, arrived0), (kept1, arrived1))):
        rows = slice(half * 256, half * 256 + 256)
        gradient = kept[...] + arrived[...].astype(F32)
        new = BETA * momentum[rows, :] + gradient
        nesterov = gradient + BETA * new
        new_ref[rows, :] = new
        tile_ref[rows, :] = nesterov.astype(BF16)
        total = total + jnp.sum((nesterov * nesterov).reshape(32, 8, TILE), axis=0)
    squares_ref[...] = total[:, :128] + total[:, 128:256] + total[:, 256:384] + total[:, 384:]


def together(steps, v, *arrays):
    for axis, bit in steps:
        v = swap_add(v, axis, bit)
    return lax.optimization_barrier((v, *arrays))


def body(grad_partial, grad_scale, momentum):
    depth = lax.axis_index("depth").astype(jnp.int32)
    at = jnp.stack([depth & 1, depth >> 1, lax.axis_index("col").astype(jnp.int32)])
    send0, send1, keep = scaled_parts(at, grad_partial, grad_scale)
    arrived = [sib(send0), sib(send1)]
    pairs = [
        call(
            functools.partial(pair_kernel, h),
            [at, keep, arrived[h]],
            [((256, TILE), BF16), ((256, TILE), F32)],
            1 << 20,
            name="pair",
        )
        for h in range(2)
    ]
    arrived = [inner(p[0]) for p in pairs]
    new_momentum, tile, v = call(
        momentum_kernel,
        [pairs[0][1], pairs[1][1], *arrived, momentum],
        [((TILE, TILE), F32), ((TILE, TILE), BF16), ((8, 128), F32)],
        1 << 20,
        name="momentum",
    )

    tile_s = sib(tile)

    a, b = call(
        pieces_kernel, [at, tile, tile_s], [((PIECE, 1024), BF16)] * 2, 1 << 16, name="pieces"
    )

    b = inner(b)
    ra, la = zhop(a, 1), zhop(a, -1)
    t_out = outer(tile)
    v, b = together([("depth", 1)], v, b)
    r2 = zhop(jnp.concatenate([b, ra], axis=0), 1)
    l2 = zhop(jnp.concatenate([la, b], axis=0), -1)
    t_in = inner(lax.optimization_barrier((tile, b))[0])
    v, r2, l2, t_out = together([("col", 1)], v, r2, l2, t_out)
    v, t_in, r2, l2 = lax.optimization_barrier((v, t_in, r2, l2))
    r3, l3 = zhop(r2, 1), zhop(l2, -1)
    v, t_in, t_out, t_in_s, t_out_s = lax.optimization_barrier(
        (v, t_in, t_out, sib(t_in), sib(t_out))
    )
    far_a, far_b = outer(t_in[:256]), inner(t_out[256:])
    v, r3, l3 = together([("col", 2)], v, r3, l3)
    r4_b, l4_b = zhop(r3[:128], 1), zhop(l3[128:], -1)
    r4_a = zhop(r3[128:], 1)
    l5_b = zhop(l4_b, -1)
    t_in, t_in_s, t_out, t_out_s = (in_hbm(t) for t in (t_in, t_in_s, t_out, t_out_s))
    tiles = [tile, tile_s, t_in, t_in_s, far_a, far_b, sib(far_a), sib(far_b), t_out, t_out_s]
    joined0, near0, own0, far0, panel = gram(
        at,
        tiles,
        [in_hbm(t) for t in (a, b, ra, la, r2, l2)] + [r3, l3],
        [
            [[(0, 0, 128)], [(1, 0, 128)]],
            [[(2, 0, 128)], [(4, 0, 128)]],
            [[(3, 0, 128)], [(5, 128, 128)]],
            [[(4, 128, 128)], [(6, 0, 128)]],
            [[(5, 0, 128)], [(7, 128, 128)]],
        ],
    )
    far0 = opposite(far0)
    r4_b, l4_b, panel = lax.optimization_barrier((r4_b, l4_b, panel))
    joined1, near1, own1, far1 = gram(
        at,
        [panel],
        [r3, l3, r4_b, l4_b],
        [[[(0, 128, 128)], [(2, 0, 128)]], [[(1, 0, 128)], [(3, 0, 128)]]],
    )
    r4_a, l5_b, far0, far1 = lax.optimization_barrier((r4_a, l5_b, far0, far1))
    far1 = opposite(far1)
    joined2, near, own, far2 = gram(
        at,
        [panel],
        [r4_a, l5_b],
        [[[(0, 0, 128)], [(1, 0, 128)]]],
        [near0, own0, near1, own1],
    )
    v, near, far1 = lax.optimization_barrier((v, near, far1))
    first, second, far2 = mixed(near[0], True), mixed(near[1], False), opposite(far2)
    v, first, second = together([("depth", 2)], v, first, second)
    (own,) = call(
        own_kernel,
        [own, first, second, far0, far1, far2],
        [((256, 1024), BF16)],
        1 << 20,
        name="own",
    )
    v, own = lax.optimization_barrier((v, own))
    first, second = mixed(own, True), mixed(own, False)
    v, first, second = together([("row", 1)], v, first, second)
    far_first, far_second = call(
        halves_kernel, [at, first, second], [((128, 1024), BF16)] * 2, 1 << 16, name="halves"
    )
    far_first, far_second = mixed(far_first, True), mixed(far_second, False)
    v, far_first, far_second = together([("row", 2)], v, far_first, far_second)

    far, whole, theirs, mine = call(
        far_kernel,
        [at, own, first, second, far_first, far_second, joined0, joined1, joined2],
        [((TILE, TILE), BF16), ((1024, 1024), BF16)] + [((2, 1024, TILE), BF16)] * 2,
        1 << 29,
        name="far",
    )
    far = sib(far)
    rest = call(rest_kernel, [whole, theirs], [((TILE, TILE), BF16)] * 3, 3 << 29, name="rest")
    rest = [sib(t) for t in rest]
    upper, lower = call(
        far_sum_kernel, [whole, mine, far], [((256, TILE), BF16)] * 2, 1 << 29, name="far_sum"
    )
    v, upper, lower = lax.optimization_barrier((v, upper, lower))
    a1, b1 = inner(upper), outer(lower)
    t_own, t_in, t_out = call(
        rest_sum_kernel,
        [whole, mine, *rest],
        [((TILE, TILE), F32)] + [((TILE, TILE), BF16)] * 2,
        3 << 29,
        name="rest_sum",
    )
    v, a1, b1 = together([("row", 4)], v, a1, b1)
    to_out = jnp.concatenate([add(t_out[:256], a1).astype(BF16), t_out[256:]], 0)
    to_in = jnp.concatenate([t_in[:256], add(t_in[256:], b1).astype(BF16)], 0)
    v, to_in, to_out = lax.optimization_barrier((v, to_in, to_out))
    from_in, from_out = inner(to_in), outer(to_out)
    v = swap_add(v, "row", 8)
    (update,) = call(
        update_kernel,
        [v, tile, t_own, from_in, from_out],
        [((TILE, TILE), F32)],
        1 << 20,
        name="update",
    )
    return (new_momentum, update)


def solution(mesh):
    placed = (P("depth", "row", "col"), P("depth", "row", "col"), P("row", ("col", "depth")))
    return jax.shard_map(
        body,
        mesh=mesh,
        in_specs=placed,
        out_specs=(P("row", ("col", "depth")), P("row", ("col", "depth"))),
        check_vma=False,
    )
```

```python
import functools
import math

import jax
import jax.numpy as jnp
from jax import lax
from jax.experimental import pallas as pl
from jax.experimental.pallas import tpu as pltpu
from jax.sharding import PartitionSpec as P

M = 8192
BETA = 0.95
EPSILON = 1e-07
F32 = jnp.float32
BF16 = jnp.bfloat16

NY = 4
TILE = 512
PIECE = 128
ZPERM = {s: [(r, (r + 2 * s) % 16) for r in range(16)] for s in (1, -1)}
YPERM = {s: [(y, (y + s) % 4) for y in range(4)] for s in (1, -1)}
SIB = [(d, d ^ 1) for d in range(4)]
INNER = [(d, d ^ 2) for d in range(4)]
OUTER = [(r * 4 + d, (r ^ 1) * 4 + (d ^ 2)) for r in range(16) for d in range(4)]


def sib(v):
    return lax.ppermute(v, "depth", SIB)


def inner(v):
    return lax.ppermute(v, "depth", INNER)


def outer(v):
    return lax.ppermute(v, ("row", "depth"), OUTER)


def across(v):
    return lax.ppermute(v, "row", [(r, r ^ 1) for r in range(16)])


def zhop(v, s):
    return lax.ppermute(v, "row", ZPERM[s])


def yhop(v, s):
    return lax.ppermute(v, "col", YPERM[s])


def in_hbm(v):
    return pltpu.with_memory_space_constraint(v, pltpu.HBM)


def mixed(v, first):
    step = {0: -1, 1: 1} if first else {0: 1, 1: -1}
    pairs = [(y * 4 + d, (y + step[d % 2]) % 4 * 4 + d) for y in range(4) for d in range(4)]
    return lax.ppermute(v, ("col", "depth"), pairs)


def swap_add(v, axis, bit):
    return v + lax.ppermute(v, axis, [(i, i ^ bit) for i in range(lax.axis_size(axis))])


def add(*vs):
    total = vs[0].astype(F32)
    for v in vs[1:]:
        total = total + v.astype(F32)
    return total


VMEM = pl.BlockSpec(memory_space=pltpu.VMEM)
SMEM = pl.BlockSpec(memory_space=pltpu.SMEM)
HBM = pl.BlockSpec(memory_space=pltpu.HBM)
ANY = pl.BlockSpec(memory_space=pl.ANY)


def gram_kernel(sources, with_panel, at_ref, *refs):
    n_tiles = 10 if with_panel else 1
    n_in = n_tiles + 1 + max(i for piece in sources for parts in piece for i, _, _ in parts)
    tiles, parts_in, outs = refs[:n_tiles], refs[n_tiles:n_in], list(refs[n_in:])
    held, sems = outs[-2:]
    joined, right, left, own, *far = outs[:-2]
    copies = []

    def copy(source, target):
        copies.append(pltpu.make_async_copy(source, target, sems.at[len(copies)]))
        copies[-1].start()

    for p, piece in enumerate(sources):
        for half, parts in enumerate(piece):
            row = p * PIECE
            for i, start, size in parts:
                copy(
                    parts_in[i].at[pl.ds(start, size)],
                    joined.at[pl.ds(row, size), pl.ds(half * 1024, 1024)],
                )
                row += size
    late = 0
    if with_panel:
        panel = far.pop()
        for i in range(4):
            copy(tiles[i], panel.at[pl.ds(0, TILE), pl.ds(i * TILE, TILE)])
        late = len(copies)
        for i in range(2):
            for part in range(2):
                copy(
                    tiles[4 + 2 * i + part],
                    panel.at[pl.ds(TILE + 256 * part, 256), pl.ds(i * TILE, TILE)],
                )
            copy(tiles[8 + i], panel.at[pl.ds(TILE, TILE), pl.ds((2 + i) * TILE, TILE)])
        late -= len(copies)
    else:
        panel = tiles[0]
    for c in copies[: late or None]:
        c.wait()
    y = at_ref[2]
    for block in range(4):
        if late and block == 2:
            for c in copies[late:]:
                c.wait()
        held[lax.rem(block + 4 - y, 4)] = lax.dot_general(
            panel[block * 256 : block * 256 + 256, :],
            joined[...],
            (((1,), (1,)), ((), ())),
            preferred_element_type=F32,
        ).astype(BF16)
    own[...] = held[0]
    right[...] = held[1]
    left[...] = held[3]
    rows = 256 // len(far)
    for i, out in enumerate(far):
        out[...] = held[2, i * rows : (i + 1) * rows]


def gram(at, tiles, arrays, sources, far_parts=2):
    n = len(sources) * PIECE
    with_panel = len(tiles) > 1
    shapes = [(n, 2048)] + [(256, n)] * 3 + [(256 // far_parts, n)] * far_parts
    n_copies = sum(len(parts) for piece in sources for parts in piece)
    if with_panel:
        shapes.append((1024, 2048))
        n_copies += 10
    return pl.pallas_call(
        functools.partial(gram_kernel, sources, with_panel),
        out_shape=[jax.ShapeDtypeStruct(s, BF16) for s in shapes],
        in_specs=[SMEM] + ([ANY] * 10 if with_panel else [VMEM]) + [ANY] * len(arrays),
        out_specs=[VMEM] * len(shapes),
        scratch_shapes=[
            pltpu.VMEM((4, 256, n), BF16),
            pltpu.SemaphoreType.DMA((n_copies,)),
        ],
        compiler_params=pltpu.CompilerParams(vmem_limit_bytes=8 << 20),
        cost_estimate=pl.CostEstimate(
            flops=2 * 1024 * 2048 * n, bytes_accessed=8 << 20, transcendentals=0
        ),
        name="gram",
    )(at, *tiles, *arrays)


def near_kernel(at_ref, *refs):
    rights, lefts, from_left, from_right = refs[0:3], refs[3:6], refs[6:8], refs[8:10]
    first, second = refs[10:]
    left_first = at_ref[0] == 0
    at = 0
    for i in range(3):
        cols = slice(at, at + rights[i].shape[1])
        for rows in (slice(0, 128), slice(128, 256)):
            to_right, to_left = rights[i][rows, :], lefts[i][rows, :]
            if i < 2 and rows.start == 0:
                to_right = add(to_right, from_left[i][...]).astype(BF16)
            if i < 2 and rows.start == 128:
                to_left = add(to_left, from_right[i][...]).astype(BF16)
            first[rows, cols] = jnp.where(left_first, to_left, to_right)
            second[rows, cols] = jnp.where(left_first, to_right, to_left)
        at = cols.stop


def own_kernel(own0, own1, own2, from_left, from_right, from_far, total):
    at = 0
    for i, own in enumerate((own0, own1, own2)):
        cols = slice(at, at + own.shape[1])
        value = add(own[...], from_left[:, cols], from_right[:, cols])
        if i == 2:
            value = value + from_far[...].astype(F32)
        total[:, cols] = value.astype(BF16)
        at = cols.stop


def far_kernel(at_ref, own, first, second, far_first, far_second, joined0, joined1, joined2, far, whole, theirs, mine):
    y, core = at_ref[2], at_ref[0]

    def rows(k):
        return pl.multiple_of(lax.rem(y + k, 4) * 256, 256)

    for k, part in ((0, own), (1 + 2 * core, first), (3 - 2 * core, second)):
        whole[pl.ds(rows(k), 256), :] = part[...]
    for offset, part in ((1 - core, far_first), (core, far_second)):
        whole[pl.ds(pl.multiple_of(rows(2) + 128 * offset, 128), 128), :] = part[...]
    at = 0
    for joined in (joined0, joined1, joined2):
        size = joined.shape[0]
        for half in range(2):
            start = half * 1024
            mine[half, at : at + size, :] = joined[:, start : start + TILE]
            theirs[half, at : at + size, :] = joined[:, start + TILE : start + 2 * TILE]
        at += size
    far[...] = jnp.dot(whole[512:], theirs[0], preferred_element_type=F32).astype(BF16)


def rest_kernel(whole, theirs, own, near, out):
    own[...] = jnp.dot(whole[:512], theirs[0], preferred_element_type=F32).astype(BF16)
    near[...] = jnp.dot(whole[:512], theirs[1], preferred_element_type=F32).astype(BF16)
    out[...] = jnp.dot(whole[512:], theirs[1], preferred_element_type=F32).astype(BF16)


def far_sum_kernel(whole, mine, arrived, upper, lower):
    total = jnp.dot(whole[512:], mine[0], preferred_element_type=F32) + arrived[...].astype(F32)
    upper[...] = total[:256].astype(BF16)
    lower[...] = total[256:].astype(BF16)


def rest_sum_kernel(whole, mine, a_own, a_near, a_out, own, near, out):
    def term(rows, half, arrived):
        return jnp.dot(whole[rows], mine[half], preferred_element_type=F32) + arrived[...].astype(F32)

    own[...] = term(slice(0, 512), 0, a_own)
    near[...] = term(slice(0, 512), 1, a_near).astype(BF16)
    out[...] = term(slice(512, 1024), 1, a_out).astype(BF16)


def call(kernel, operands, shapes, flops, limit=8, name=None):
    return pl.pallas_call(
        kernel,
        out_shape=[jax.ShapeDtypeStruct(*s) for s in shapes],
        in_specs=[SMEM if v.dtype == jnp.int32 else VMEM for v in operands],
        out_specs=[VMEM] * len(shapes),
        compiler_params=pltpu.CompilerParams(vmem_limit_bytes=limit << 20),
        cost_estimate=pl.CostEstimate(flops=flops, bytes_accessed=4 << 20, transcendentals=0),
        name=name,
    )(*operands)


def scaled_kernel(at_ref, q_ref, s_ref, send0, send1, keep, q_buf, s_buf, sems):
    c = at_ref[0]
    scales = pltpu.make_async_copy(s_ref.at[0], s_buf, sems.at[8])
    scales.start()
    copies = []
    for step in range(4):
        for side, core in enumerate((1 - c, c)):
            start = pl.multiple_of((step % 2 * 2 + core) * TILE, TILE)
            copies.append(
                pltpu.make_async_copy(
                    q_ref.at[0, pl.ds(step // 2 * 256, 256), pl.ds(start, TILE)],
                    q_buf.at[2 * step + side],
                    sems.at[2 * step + side],
                )
            )
            copies[-1].start()
    scales.wait()
    for step in range(4):
        for side, core in enumerate((1 - c, c)):
            copies[2 * step + side].wait()
            start = pl.multiple_of((step % 2 * 2 + core) * TILE, TILE)
            for r in range(2):
                rows = slice(r * 128, r * 128 + 128)
                row = step // 2 * 2 + r
                scale = s_buf[row : row + 1, pl.ds(start, TILE)]
                value = q_buf[2 * step + side, rows, :].astype(F32) * scale
                if side:
                    keep[step, rows, :] = value
                else:
                    (send0, send1)[step // 2][step % 2, rows, :] = value.astype(BF16)


def scaled_parts(at, quant, scale):
    return pl.pallas_call(
        scaled_kernel,
        in_specs=[SMEM, HBM, HBM],
        out_specs=[VMEM] * 3,
        out_shape=[
            jax.ShapeDtypeStruct((2, 256, TILE), BF16),
            jax.ShapeDtypeStruct((2, 256, TILE), BF16),
            jax.ShapeDtypeStruct((4, 256, TILE), F32),
        ],
        scratch_shapes=[
            pltpu.VMEM((8, 256, TILE), BF16),
            pltpu.VMEM((4, 4 * TILE), F32),
            pltpu.SemaphoreType.DMA((9,)),
        ],
        compiler_params=pltpu.CompilerParams(vmem_limit_bytes=8 << 20),
        name="scaled",
    )(at, in_hbm(quant), in_hbm(scale))


def pair_kernel(half, at_ref, keep, arrived, to_inner, kept):
    xl = at_ref[1]
    to_inner[...] = (keep[2 * half + 1 - xl] + arrived[1 - xl].astype(F32)).astype(BF16)
    kept[...] = keep[2 * half + xl] + arrived[xl].astype(F32)


def pieces_kernel(at_ref, tile, tile_s, kept, sent):
    core, xl = at_ref[0], at_ref[1]
    for out, half in ((kept, xl), (sent, 1 - xl)):
        rows = pl.ds(pl.multiple_of((2 * half + core) * PIECE, PIECE), PIECE)
        out[:, :TILE] = tile[rows, :]
        out[:, TILE:] = tile_s[rows, :]


def halves_kernel(at_ref, first, second, far_first, far_second):
    core = at_ref[0]
    far_first[...] = first[pl.ds(pl.multiple_of(128 * (1 - core), 128), 128), :]
    far_second[...] = second[pl.ds(pl.multiple_of(128 * core, 128), 128), :]


def update_kernel(squares, tile, own, from_in, from_out, update):
    total = jnp.sum(jnp.sum(squares[...], axis=1, keepdims=True), axis=0, keepdims=True)
    gain = math.sqrt(M) / (1.5 * (jnp.sqrt(total) + EPSILON))
    linear, cubic = (math.sqrt(M) * 1.5) * gain, (math.sqrt(M) * 0.5) * gain * gain * gain
    product = add(own[...], from_in[...], from_out[...])
    update[...] = linear * tile[...].astype(F32) - cubic * product


def momentum_kernel(kept0, kept1, arrived0, arrived1, momentum, new_ref, tile_ref, squares_ref):
    total = jnp.zeros((8, TILE), F32)
    for half, (kept, arrived) in enumerate(((kept0, arrived0), (kept1, arrived1))):
        rows = slice(half * 256, half * 256 + 256)
        gradient = kept[...] + arrived[...].astype(F32)
        new = BETA * momentum[rows, :] + gradient
        nesterov = gradient + BETA * new
        new_ref[rows, :] = new
        tile_ref[rows, :] = nesterov.astype(BF16)
        total = total + jnp.sum((nesterov * nesterov).reshape(32, 8, TILE), axis=0)
    squares_ref[...] = total[:, :128] + total[:, 128:256] + total[:, 256:384] + total[:, 384:]


def together(steps, v, *arrays):
    for axis, bit in steps:
        v = swap_add(v, axis, bit)
    return lax.optimization_barrier((v, *arrays))


def start_sum(far0, far1):
    return yhop(far0, 1), yhop(far1, -1)


def body(grad_partial, grad_scale, momentum):
    depth = lax.axis_index("depth").astype(jnp.int32)
    at = jnp.stack([depth & 1, depth >> 1, lax.axis_index("col").astype(jnp.int32)])
    send0, send1, keep = scaled_parts(at, grad_partial, grad_scale)
    arrived = [sib(send0), sib(send1)]
    pairs = [
        call(
            functools.partial(pair_kernel, h),
            [at, keep, arrived[h]],
            [((256, TILE), BF16), ((256, TILE), F32)],
            1 << 20,
            name="pair",
        )
        for h in range(2)
    ]
    arrived = [inner(p[0]) for p in pairs]
    new_momentum, tile, v = call(
        momentum_kernel,
        [pairs[0][1], pairs[1][1], *arrived, momentum],
        [((TILE, TILE), F32), ((TILE, TILE), BF16), ((8, 128), F32)],
        1 << 20,
        name="momentum",
    )

    tile_s = sib(tile)

    a, b = call(
        pieces_kernel, [at, tile, tile_s], [((PIECE, 1024), BF16)] * 2, 1 << 16, name="pieces"
    )

    b = inner(b)
    ra, la = zhop(a, 1), zhop(a, -1)
    t_out = outer(tile)
    v, b = together([("depth", 1)], v, b)
    r2 = zhop(jnp.concatenate([b, ra], axis=0), 1)
    l2 = zhop(jnp.concatenate([la, b], axis=0), -1)
    t_in = inner(lax.optimization_barrier((tile, b))[0])
    v, r2, l2, t_out = together([("col", 1)], v, r2, l2, t_out)
    v, t_in, r2, l2 = lax.optimization_barrier((v, t_in, r2, l2))
    r3, l3 = zhop(r2, 1), zhop(l2, -1)
    v, t_in, t_out, t_in_s, t_out_s = lax.optimization_barrier(
        (v, t_in, t_out, sib(t_in), sib(t_out))
    )
    far_a, far_b = outer(t_in[:256]), inner(t_out[256:])
    v, far_a, far_b = together([("col", 2)], v, far_a, far_b)
    r4_b, l4_b = zhop(r3[:128], 1), zhop(l3[128:], -1)
    r4_a = zhop(r3[128:], 1)
    l5_b = zhop(l4_b, -1)
    t_in, t_in_s, t_out, t_out_s = (in_hbm(t) for t in (t_in, t_in_s, t_out, t_out_s))
    tiles = [tile, tile_s, t_in, t_in_s, far_a, far_b, sib(far_a), sib(far_b), t_out, t_out_s]
    joined0, right0, left0, own0, far0, far1, panel = gram(
        at,
        tiles,
        [in_hbm(t) for t in (a, b, ra, la, r2, l2)] + [r3, l3],
        [
            [[(0, 0, 128)], [(1, 0, 128)]],
            [[(2, 0, 128)], [(4, 0, 128)]],
            [[(3, 0, 128)], [(5, 128, 128)]],
            [[(4, 128, 128)], [(6, 0, 128)]],
            [[(5, 0, 128)], [(7, 128, 128)]],
        ],
    )
    from_left0, from_right0 = start_sum(far0, far1)
    r4_b, l4_b, panel, from_left0 = lax.optimization_barrier((r4_b, l4_b, panel, from_left0))
    joined1, right1, left1, own1, far0, far1 = gram(
        at,
        [panel],
        [r3, l3, r4_b, l4_b],
        [[[(0, 128, 128)], [(2, 0, 128)]], [[(1, 0, 128)], [(3, 0, 128)]]],
    )
    r4_a, l5_b, from_left0, from_right0, far0, far1 = lax.optimization_barrier(
        (r4_a, l5_b, from_left0, from_right0, far0, far1)
    )
    from_left1, from_right1 = start_sum(far0, far1)
    joined2, right2, left2, own2, far2 = gram(
        at, [panel], [r4_a, l5_b], [[[(0, 0, 128)], [(1, 0, 128)]]], far_parts=1
    )
    first, second = call(
        near_kernel,
        [at, right0, right1, right2, left0, left1, left2]
        + [from_left0, from_left1, from_right0, from_right1],
        [((256, 1024), BF16)] * 2,
        1 << 20,
        name="near",
    )
    v, first, second = lax.optimization_barrier((v, first, second))
    first, second = mixed(first, True), mixed(second, False)
    from_far = lax.ppermute(far2, "col", [(i, i ^ 2) for i in range(4)])
    v, first, second = together([("depth", 2)], v, first, second)
    (own,) = call(
        own_kernel,
        [own0, own1, own2, first, second, from_far],
        [((256, 1024), BF16)],
        1 << 20,
        name="own",
    )
    v, own = lax.optimization_barrier((v, own))
    first, second = mixed(own, True), mixed(own, False)
    v, first, second = together([("row", 1)], v, first, second)
    far_first, far_second = call(
        halves_kernel, [at, first, second], [((128, 1024), BF16)] * 2, 1 << 16, name="halves"
    )
    far_first, far_second = mixed(far_first, True), mixed(far_second, False)
    v, far_first, far_second = together([("row", 2)], v, far_first, far_second)

    far, whole, theirs, mine = call(
        far_kernel,
        [at, own, first, second, far_first, far_second, joined0, joined1, joined2],
        [((TILE, TILE), BF16), ((1024, 1024), BF16)] + [((2, 1024, TILE), BF16)] * 2,
        1 << 29,
        name="far",
    )
    far = sib(far)
    rest = call(rest_kernel, [whole, theirs], [((TILE, TILE), BF16)] * 3, 3 << 29, name="rest")
    rest = [sib(t) for t in rest]
    upper, lower = call(
        far_sum_kernel, [whole, mine, far], [((256, TILE), BF16)] * 2, 1 << 29, name="far_sum"
    )
    v, upper, lower = lax.optimization_barrier((v, upper, lower))
    a1, b1 = inner(upper), outer(lower)
    t_own, t_in, t_out = call(
        rest_sum_kernel,
        [whole, mine, *rest],
        [((TILE, TILE), F32)] + [((TILE, TILE), BF16)] * 2,
        3 << 29,
        name="rest_sum",
    )
    v, a1, b1 = together([("row", 4)], v, a1, b1)
    to_out = jnp.concatenate([add(t_out[:256], a1).astype(BF16), t_out[256:]], 0)
    to_in = jnp.concatenate([t_in[:256], add(t_in[256:], b1).astype(BF16)], 0)
    v, to_in, to_out = lax.optimization_barrier((v, to_in, to_out))
    from_in, from_out = inner(to_in), outer(to_out)
    v = swap_add(v, "row", 8)
    (update,) = call(
        update_kernel,
        [v, tile, t_own, from_in, from_out],
        [((TILE, TILE), F32)],
        1 << 20,
        name="update",
    )
    return (new_momentum, update)


def solution(mesh):
    placed = (P("depth", "row", "col"), P("depth", "row", "col"), P("row", ("col", "depth")))
    return jax.shard_map(
        body,
        mesh=mesh,
        in_specs=placed,
        out_specs=(P("row", ("col", "depth")), P("row", ("col", "depth"))),
        check_vma=False,
    )
```

```python
import functools
import math

import jax
import jax.numpy as jnp
from jax import lax
from jax.experimental import pallas as pl
from jax.experimental.pallas import tpu as pltpu
from jax.sharding import PartitionSpec as P

M = 8192
BETA = 0.95
EPSILON = 1e-07
F32 = jnp.float32
BF16 = jnp.bfloat16

NY = 4
TILE = 512
PIECE = 128
ZPERM = {s: [(r, (r + 2 * s) % 16) for r in range(16)] for s in (1, -1)}
YPERM = {s: [(y, (y + s) % 4) for y in range(4)] for s in (1, -1)}
SIB = [(d, d ^ 1) for d in range(4)]
INNER = [(d, d ^ 2) for d in range(4)]
OUTER = [(r * 4 + d, (r ^ 1) * 4 + (d ^ 2)) for r in range(16) for d in range(4)]


def sib(v):
    return lax.ppermute(v, "depth", SIB)


def inner(v):
    return lax.ppermute(v, "depth", INNER)


def outer(v):
    return lax.ppermute(v, ("row", "depth"), OUTER)


def across(v):
    return lax.ppermute(v, "row", [(r, r ^ 1) for r in range(16)])


def zhop(v, s):
    return lax.ppermute(v, "row", ZPERM[s])


def yhop(v, s):
    return lax.ppermute(v, "col", YPERM[s])


def in_hbm(v):
    return pltpu.with_memory_space_constraint(v, pltpu.HBM)


def mixed(v, first):
    step = {0: -1, 1: 1} if first else {0: 1, 1: -1}
    pairs = [(y * 4 + d, (y + step[d % 2]) % 4 * 4 + d) for y in range(4) for d in range(4)]
    return lax.ppermute(v, ("col", "depth"), pairs)


def swap_add(v, axis, bit):
    return v + lax.ppermute(v, axis, [(i, i ^ bit) for i in range(lax.axis_size(axis))])


def add(*vs):
    total = vs[0].astype(F32)
    for v in vs[1:]:
        total = total + v.astype(F32)
    return total


VMEM = pl.BlockSpec(memory_space=pltpu.VMEM)
SMEM = pl.BlockSpec(memory_space=pltpu.SMEM)
HBM = pl.BlockSpec(memory_space=pltpu.HBM)
ANY = pl.BlockSpec(memory_space=pl.ANY)


def gram_kernel(sources, with_panel, y_ref, *refs):
    n_tiles = 10 if with_panel else 1
    n_in = n_tiles + 1 + max(i for piece in sources for parts in piece for i, _, _ in parts)
    tiles, parts_in, outs = refs[:n_tiles], refs[n_tiles:n_in], list(refs[n_in:])
    held, sems = outs[-2:]
    joined, right, left, own, *far = outs[:-2]
    copies = []

    def copy(source, target):
        copies.append(pltpu.make_async_copy(source, target, sems.at[len(copies)]))
        copies[-1].start()

    for p, piece in enumerate(sources):
        for half, parts in enumerate(piece):
            row = p * PIECE
            for i, start, size in parts:
                copy(
                    parts_in[i].at[pl.ds(start, size)],
                    joined.at[pl.ds(row, size), pl.ds(half * 1024, 1024)],
                )
                row += size
    late = 0
    if with_panel:
        panel = far.pop()
        for i in range(4):
            copy(tiles[i], panel.at[pl.ds(0, TILE), pl.ds(i * TILE, TILE)])
        late = len(copies)
        for i in range(2):
            for part in range(2):
                copy(
                    tiles[4 + 2 * i + part],
                    panel.at[pl.ds(TILE + 256 * part, 256), pl.ds(i * TILE, TILE)],
                )
            copy(tiles[8 + i], panel.at[pl.ds(TILE, TILE), pl.ds((2 + i) * TILE, TILE)])
        late -= len(copies)
    else:
        panel = tiles[0]
    for c in copies[: late or None]:
        c.wait()
    y = y_ref[0]
    for block in range(4):
        if late and block == 2:
            for c in copies[late:]:
                c.wait()
        held[lax.rem(block + 4 - y, 4)] = lax.dot_general(
            panel[block * 256 : block * 256 + 256, :],
            joined[...],
            (((1,), (1,)), ((), ())),
            preferred_element_type=F32,
        ).astype(BF16)
    own[...] = held[0]
    right[...] = held[1]
    left[...] = held[3]
    rows = 256 // len(far)
    for i, out in enumerate(far):
        out[...] = held[2, i * rows : (i + 1) * rows]


def gram(y, tiles, arrays, sources, far_parts=2):
    n = len(sources) * PIECE
    with_panel = len(tiles) > 1
    shapes = [(n, 2048)] + [(256, n)] * 3 + [(256 // far_parts, n)] * far_parts
    n_copies = sum(len(parts) for piece in sources for parts in piece)
    if with_panel:
        shapes.append((1024, 2048))
        n_copies += 10
    return pl.pallas_call(
        functools.partial(gram_kernel, sources, with_panel),
        out_shape=[jax.ShapeDtypeStruct(s, BF16) for s in shapes],
        in_specs=[SMEM] + ([ANY] * 10 if with_panel else [VMEM]) + [ANY] * len(arrays),
        out_specs=[VMEM] * len(shapes),
        scratch_shapes=[
            pltpu.VMEM((4, 256, n), BF16),
            pltpu.SemaphoreType.DMA((n_copies,)),
        ],
        compiler_params=pltpu.CompilerParams(vmem_limit_bytes=8 << 20),
        cost_estimate=pl.CostEstimate(
            flops=2 * 1024 * 2048 * n, bytes_accessed=8 << 20, transcendentals=0
        ),
        name="gram",
    )(y, *tiles, *arrays)


def near_kernel(c_ref, *refs):
    rights, lefts, from_left, from_right = refs[0:3], refs[3:6], refs[6:8], refs[8:10]
    first, second = refs[10:]
    left_first = c_ref[0] == 0
    at = 0
    for i in range(3):
        cols = slice(at, at + rights[i].shape[1])
        for rows in (slice(0, 128), slice(128, 256)):
            to_right, to_left = rights[i][rows, :], lefts[i][rows, :]
            if i < 2 and rows.start == 0:
                to_right = add(to_right, from_left[i][...]).astype(BF16)
            if i < 2 and rows.start == 128:
                to_left = add(to_left, from_right[i][...]).astype(BF16)
            first[rows, cols] = jnp.where(left_first, to_left, to_right)
            second[rows, cols] = jnp.where(left_first, to_right, to_left)
        at = cols.stop


def own_kernel(own0, own1, own2, from_left, from_right, from_far, total):
    at = 0
    for i, own in enumerate((own0, own1, own2)):
        cols = slice(at, at + own.shape[1])
        value = add(own[...], from_left[:, cols], from_right[:, cols])
        if i == 2:
            value = value + from_far[...].astype(F32)
        total[:, cols] = value.astype(BF16)
        at = cols.stop


def far_kernel(c_ref, y_ref, own, first, second, far_first, far_second, joined0, joined1, joined2, far, whole, theirs, mine):
    y, core = y_ref[0], c_ref[0]

    def rows(k):
        return pl.multiple_of(lax.rem(y + k, 4) * 256, 256)

    for k, part in ((0, own), (1 + 2 * core, first), (3 - 2 * core, second)):
        whole[pl.ds(rows(k), 256), :] = part[...]
    for offset, part in ((1 - core, far_first), (core, far_second)):
        whole[pl.ds(pl.multiple_of(rows(2) + 128 * offset, 128), 128), :] = part[...]
    at = 0
    for joined in (joined0, joined1, joined2):
        size = joined.shape[0]
        for half in range(2):
            start = half * 1024
            mine[half, at : at + size, :] = joined[:, start : start + TILE]
            theirs[half, at : at + size, :] = joined[:, start + TILE : start + 2 * TILE]
        at += size
    far[...] = jnp.dot(whole[512:], theirs[0], preferred_element_type=F32).astype(BF16)


def rest_kernel(whole, theirs, own, near, out):
    own[...] = jnp.dot(whole[:512], theirs[0], preferred_element_type=F32).astype(BF16)
    near[...] = jnp.dot(whole[:512], theirs[1], preferred_element_type=F32).astype(BF16)
    out[...] = jnp.dot(whole[512:], theirs[1], preferred_element_type=F32).astype(BF16)


def far_sum_kernel(whole, mine, arrived, upper, lower):
    total = jnp.dot(whole[512:], mine[0], preferred_element_type=F32) + arrived[...].astype(F32)
    upper[...] = total[:256].astype(BF16)
    lower[...] = total[256:].astype(BF16)


def rest_sum_kernel(whole, mine, a_own, a_near, a_out, own, near, out):
    def term(rows, half, arrived):
        return jnp.dot(whole[rows], mine[half], preferred_element_type=F32) + arrived[...].astype(F32)

    own[...] = term(slice(0, 512), 0, a_own)
    near[...] = term(slice(0, 512), 1, a_near).astype(BF16)
    out[...] = term(slice(512, 1024), 1, a_out).astype(BF16)


def call(kernel, operands, shapes, flops, limit=8, name=None):
    return pl.pallas_call(
        kernel,
        out_shape=[jax.ShapeDtypeStruct(*s) for s in shapes],
        in_specs=[SMEM if v.dtype == jnp.int32 else VMEM for v in operands],
        out_specs=[VMEM] * len(shapes),
        compiler_params=pltpu.CompilerParams(vmem_limit_bytes=limit << 20),
        cost_estimate=pl.CostEstimate(flops=flops, bytes_accessed=4 << 20, transcendentals=0),
        name=name,
    )(*operands)


def scaled_kernel(c_ref, xl_ref, y_ref, q_ref, s_ref, send0, send1, keep, q_buf, s_buf, sems):
    c = c_ref[0]
    scales = pltpu.make_async_copy(s_ref.at[0], s_buf, sems.at[8])
    scales.start()
    copies = []
    for step in range(4):
        for side, core in enumerate((1 - c, c)):
            start = pl.multiple_of((step % 2 * 2 + core) * TILE, TILE)
            copies.append(
                pltpu.make_async_copy(
                    q_ref.at[0, pl.ds(step // 2 * 256, 256), pl.ds(start, TILE)],
                    q_buf.at[2 * step + side],
                    sems.at[2 * step + side],
                )
            )
            copies[-1].start()
    scales.wait()
    for step in range(4):
        for side, core in enumerate((1 - c, c)):
            copies[2 * step + side].wait()
            start = pl.multiple_of((step % 2 * 2 + core) * TILE, TILE)
            for r in range(2):
                rows = slice(r * 128, r * 128 + 128)
                row = step // 2 * 2 + r
                scale = s_buf[row : row + 1, pl.ds(start, TILE)]
                value = q_buf[2 * step + side, rows, :].astype(F32) * scale
                if side:
                    keep[step, rows, :] = value
                else:
                    (send0, send1)[step // 2][step % 2, rows, :] = value.astype(BF16)


def scaled_parts(at, quant, scale):
    return pl.pallas_call(
        scaled_kernel,
        in_specs=[SMEM] * 3 + [HBM] * 2,
        out_specs=[VMEM] * 3,
        out_shape=[
            jax.ShapeDtypeStruct((2, 256, TILE), BF16),
            jax.ShapeDtypeStruct((2, 256, TILE), BF16),
            jax.ShapeDtypeStruct((4, 256, TILE), F32),
        ],
        scratch_shapes=[
            pltpu.VMEM((8, 256, TILE), BF16),
            pltpu.VMEM((4, 4 * TILE), F32),
            pltpu.SemaphoreType.DMA((9,)),
        ],
        compiler_params=pltpu.CompilerParams(vmem_limit_bytes=8 << 20),
        name="scaled",
    )(*at, in_hbm(quant), in_hbm(scale))


def pair_kernel(half, xl_ref, keep, arrived, to_inner, kept):
    xl = xl_ref[0]
    to_inner[...] = (keep[2 * half + 1 - xl] + arrived[1 - xl].astype(F32)).astype(BF16)
    kept[...] = keep[2 * half + xl] + arrived[xl].astype(F32)


def pieces_kernel(c_ref, xl_ref, tile, tile_s, kept, sent):
    core, xl = c_ref[0], xl_ref[0]
    for out, half in ((kept, xl), (sent, 1 - xl)):
        rows = pl.ds(pl.multiple_of((2 * half + core) * PIECE, PIECE), PIECE)
        out[:, :TILE] = tile[rows, :]
        out[:, TILE:] = tile_s[rows, :]


def halves_kernel(c_ref, first, second, far_first, far_second):
    core = c_ref[0]
    far_first[...] = first[pl.ds(pl.multiple_of(128 * (1 - core), 128), 128), :]
    far_second[...] = second[pl.ds(pl.multiple_of(128 * core, 128), 128), :]


def update_kernel(squares, tile, own, from_in, from_out, update):
    total = jnp.sum(jnp.sum(squares[...], axis=1, keepdims=True), axis=0, keepdims=True)
    gain = math.sqrt(M) / (1.5 * (jnp.sqrt(total) + EPSILON))
    linear, cubic = (math.sqrt(M) * 1.5) * gain, (math.sqrt(M) * 0.5) * gain * gain * gain
    product = add(own[...], from_in[...], from_out[...])
    update[...] = linear * tile[...].astype(F32) - cubic * product


def momentum_kernel(kept0, kept1, arrived0, arrived1, momentum, new_ref, tile_ref, squares_ref):
    total = jnp.zeros((8, TILE), F32)
    for half, (kept, arrived) in enumerate(((kept0, arrived0), (kept1, arrived1))):
        rows = slice(half * 256, half * 256 + 256)
        gradient = kept[...] + arrived[...].astype(F32)
        new = BETA * momentum[rows, :] + gradient
        nesterov = gradient + BETA * new
        new_ref[rows, :] = new
        tile_ref[rows, :] = nesterov.astype(BF16)
        total = total + jnp.sum((nesterov * nesterov).reshape(32, 8, TILE), axis=0)
    squares_ref[...] = total[:, :128] + total[:, 128:256] + total[:, 256:384] + total[:, 384:]


def together(steps, v, *arrays):
    for axis, bit in steps:
        v = swap_add(v, axis, bit)
    return lax.optimization_barrier((v, *arrays))


def start_sum(far0, far1):
    return yhop(far0, 1), yhop(far1, -1)


def body(grad_partial, grad_scale, momentum):
    depth = lax.axis_index("depth").astype(jnp.int32)
    at = [v.reshape(1) for v in (depth & 1, depth >> 1, lax.axis_index("col").astype(jnp.int32))]
    c, xl, y = at
    send0, send1, keep = scaled_parts(at, grad_partial, grad_scale)
    arrived = [sib(send0), sib(send1)]
    pairs = [
        call(
            functools.partial(pair_kernel, h),
            [xl, keep, arrived[h]],
            [((256, TILE), BF16), ((256, TILE), F32)],
            1 << 20,
            name="pair",
        )
        for h in range(2)
    ]
    arrived = [inner(p[0]) for p in pairs]
    new_momentum, tile, v = call(
        momentum_kernel,
        [pairs[0][1], pairs[1][1], *arrived, momentum],
        [((TILE, TILE), F32), ((TILE, TILE), BF16), ((8, 128), F32)],
        1 << 20,
        name="momentum",
    )

    tile_s = sib(tile)

    a, b = call(
        pieces_kernel, [c, xl, tile, tile_s], [((PIECE, 1024), BF16)] * 2, 1 << 16, name="pieces"
    )

    b = inner(b)
    ra, la = zhop(a, 1), zhop(a, -1)
    t_out = outer(tile)
    v, b = together([("depth", 1)], v, b)
    r2 = zhop(jnp.concatenate([b, ra], axis=0), 1)
    l2 = zhop(jnp.concatenate([la, b], axis=0), -1)
    t_in = inner(lax.optimization_barrier((tile, b))[0])
    v, r2, l2, t_out = together([("col", 1)], v, r2, l2, t_out)
    v, t_in, r2, l2 = lax.optimization_barrier((v, t_in, r2, l2))
    r3, l3 = zhop(r2, 1), zhop(l2, -1)
    v, t_in, t_out, t_in_s, t_out_s = lax.optimization_barrier(
        (v, t_in, t_out, sib(t_in), sib(t_out))
    )
    far_a, far_b = outer(t_in[:256]), inner(t_out[256:])
    v, far_a, far_b = together([("col", 2)], v, far_a, far_b)
    r4_b, l4_b = zhop(r3[:128], 1), zhop(l3[128:], -1)
    r4_a = zhop(r3[128:], 1)
    l5_b = zhop(l4_b, -1)
    t_in, t_in_s, t_out, t_out_s = (in_hbm(t) for t in (t_in, t_in_s, t_out, t_out_s))
    tiles = [tile, tile_s, t_in, t_in_s, far_a, far_b, sib(far_a), sib(far_b), t_out, t_out_s]
    joined0, right0, left0, own0, far0, far1, panel = gram(
        y,
        tiles,
        [in_hbm(t) for t in (a, b, ra, la, r2, l2)] + [r3, l3],
        [
            [[(0, 0, 128)], [(1, 0, 128)]],
            [[(2, 0, 128)], [(4, 0, 128)]],
            [[(3, 0, 128)], [(5, 128, 128)]],
            [[(4, 128, 128)], [(6, 0, 128)]],
            [[(5, 0, 128)], [(7, 128, 128)]],
        ],
    )
    from_left0, from_right0 = start_sum(far0, far1)
    r4_b, l4_b, panel, from_left0 = lax.optimization_barrier((r4_b, l4_b, panel, from_left0))
    joined1, right1, left1, own1, far0, far1 = gram(
        y,
        [panel],
        [r3, l3, r4_b, l4_b],
        [[[(0, 128, 128)], [(2, 0, 128)]], [[(1, 0, 128)], [(3, 0, 128)]]],
    )
    r4_a, l5_b, from_left0, from_right0, far0, far1 = lax.optimization_barrier(
        (r4_a, l5_b, from_left0, from_right0, far0, far1)
    )
    from_left1, from_right1 = start_sum(far0, far1)
    joined2, right2, left2, own2, far2 = gram(
        y, [panel], [r4_a, l5_b], [[[(0, 0, 128)], [(1, 0, 128)]]], far_parts=1
    )
    first, second = call(
        near_kernel,
        [c, right0, right1, right2, left0, left1, left2]
        + [from_left0, from_left1, from_right0, from_right1],
        [((256, 1024), BF16)] * 2,
        1 << 20,
        name="near",
    )
    v, first, second = lax.optimization_barrier((v, first, second))
    first, second = mixed(first, True), mixed(second, False)
    from_far = lax.ppermute(far2, "col", [(i, i ^ 2) for i in range(4)])
    v, first, second = together([("depth", 2)], v, first, second)
    (own,) = call(
        own_kernel,
        [own0, own1, own2, first, second, from_far],
        [((256, 1024), BF16)],
        1 << 20,
        name="own",
    )
    v, own = lax.optimization_barrier((v, own))
    first, second = mixed(own, True), mixed(own, False)
    v, first, second = together([("row", 1)], v, first, second)
    far_first, far_second = call(
        halves_kernel, [c, first, second], [((128, 1024), BF16)] * 2, 1 << 16, name="halves"
    )
    far_first, far_second = mixed(far_first, True), mixed(far_second, False)
    v, far_first, far_second = together([("row", 2)], v, far_first, far_second)

    far, whole, theirs, mine = call(
        far_kernel,
        [c, y, own, first, second, far_first, far_second, joined0, joined1, joined2],
        [((TILE, TILE), BF16), ((1024, 1024), BF16)] + [((2, 1024, TILE), BF16)] * 2,
        1 << 29,
        name="far",
    )
    far = sib(far)
    rest = call(rest_kernel, [whole, theirs], [((TILE, TILE), BF16)] * 3, 3 << 29, name="rest")
    rest = [sib(t) for t in rest]
    upper, lower = call(
        far_sum_kernel, [whole, mine, far], [((256, TILE), BF16)] * 2, 1 << 29, name="far_sum"
    )
    v, upper, lower = lax.optimization_barrier((v, upper, lower))
    a1, b1 = inner(upper), outer(lower)
    t_own, t_in, t_out = call(
        rest_sum_kernel,
        [whole, mine, *rest],
        [((TILE, TILE), F32)] + [((TILE, TILE), BF16)] * 2,
        3 << 29,
        name="rest_sum",
    )
    v, a1, b1 = together([("row", 4)], v, a1, b1)
    to_out = jnp.concatenate([add(t_out[:256], a1).astype(BF16), t_out[256:]], 0)
    to_in = jnp.concatenate([t_in[:256], add(t_in[256:], b1).astype(BF16)], 0)
    v, to_in, to_out = lax.optimization_barrier((v, to_in, to_out))
    from_in, from_out = inner(to_in), outer(to_out)
    v = swap_add(v, "row", 8)
    (update,) = call(
        update_kernel,
        [v, tile, t_own, from_in, from_out],
        [((TILE, TILE), F32)],
        1 << 20,
        name="update",
    )
    return (new_momentum, update)


def solution(mesh):
    placed = (P("depth", "row", "col"), P("depth", "row", "col"), P("row", ("col", "depth")))
    return jax.shard_map(
        body,
        mesh=mesh,
        in_specs=placed,
        out_specs=(P("row", ("col", "depth")), P("row", ("col", "depth"))),
        check_vma=False,
    )
```

```python
import functools
import math

import jax
import jax.numpy as jnp
from jax import lax
from jax.experimental import pallas as pl
from jax.experimental.pallas import tpu as pltpu
from jax.sharding import PartitionSpec as P

M = 8192
BETA = 0.95
EPSILON = 1e-07
F32 = jnp.float32
BF16 = jnp.bfloat16

NY = 4
TILE = 512
PIECE = 128
ZPERM = {s: [(r, (r + 2 * s) % 16) for r in range(16)] for s in (1, -1)}
YPERM = {s: [(y, (y + s) % 4) for y in range(4)] for s in (1, -1)}
SIB = [(d, d ^ 1) for d in range(4)]
INNER = [(d, d ^ 2) for d in range(4)]
OUTER = [(r * 4 + d, (r ^ 1) * 4 + (d ^ 2)) for r in range(16) for d in range(4)]


def sib(v):
    return lax.ppermute(v, "depth", SIB)


def inner(v):
    return lax.ppermute(v, "depth", INNER)


def outer(v):
    return lax.ppermute(v, ("row", "depth"), OUTER)


def across(v):
    return lax.ppermute(v, "row", [(r, r ^ 1) for r in range(16)])


def zhop(v, s):
    return lax.ppermute(v, "row", ZPERM[s])


def yhop(v, s):
    return lax.ppermute(v, "col", YPERM[s])


def in_hbm(v):
    return pltpu.with_memory_space_constraint(v, pltpu.HBM)


def mixed(v, first):
    step = {0: -1, 1: 1} if first else {0: 1, 1: -1}
    pairs = [(y * 4 + d, (y + step[d % 2]) % 4 * 4 + d) for y in range(4) for d in range(4)]
    return lax.ppermute(v, ("col", "depth"), pairs)


def swap_add(v, axis, bit):
    return v + lax.ppermute(v, axis, [(i, i ^ bit) for i in range(lax.axis_size(axis))])


def add(*vs):
    total = vs[0].astype(F32)
    for v in vs[1:]:
        total = total + v.astype(F32)
    return total


VMEM = pl.BlockSpec(memory_space=pltpu.VMEM)
SMEM = pl.BlockSpec(memory_space=pltpu.SMEM)
HBM = pl.BlockSpec(memory_space=pltpu.HBM)
ANY = pl.BlockSpec(memory_space=pl.ANY)


def gram_kernel(sources, with_panel, y_ref, *refs):
    n_tiles = 10 if with_panel else 1
    n_in = n_tiles + 1 + max(i for piece in sources for parts in piece for i, _, _ in parts)
    tiles, parts_in, outs = refs[:n_tiles], refs[n_tiles:n_in], list(refs[n_in:])
    held, sems = outs[-2:]
    joined, right, left, own, *far = outs[:-2]
    copies = []

    def copy(source, target):
        copies.append(pltpu.make_async_copy(source, target, sems.at[len(copies)]))
        copies[-1].start()

    for p, piece in enumerate(sources):
        for half, parts in enumerate(piece):
            row = p * PIECE
            for i, start, size in parts:
                copy(
                    parts_in[i].at[pl.ds(start, size)],
                    joined.at[pl.ds(row, size), pl.ds(half * 1024, 1024)],
                )
                row += size
    late = 0
    if with_panel:
        panel = far.pop()
        for i in range(4):
            copy(tiles[i], panel.at[pl.ds(0, TILE), pl.ds(i * TILE, TILE)])
        late = len(copies)
        for i in range(2):
            for part in range(2):
                copy(
                    tiles[4 + 2 * i + part],
                    panel.at[pl.ds(TILE + 256 * part, 256), pl.ds(i * TILE, TILE)],
                )
            copy(tiles[8 + i], panel.at[pl.ds(TILE, TILE), pl.ds((2 + i) * TILE, TILE)])
        late -= len(copies)
    else:
        panel = tiles[0]
    for c in copies[: late or None]:
        c.wait()
    y = y_ref[0]
    for block in range(4):
        if late and block == 2:
            for c in copies[late:]:
                c.wait()
        held[lax.rem(block + 4 - y, 4)] = lax.dot_general(
            panel[block * 256 : block * 256 + 256, :],
            joined[...],
            (((1,), (1,)), ((), ())),
            preferred_element_type=F32,
        ).astype(BF16)
    own[...] = held[0]
    right[...] = held[1]
    left[...] = held[3]
    rows = 256 // len(far)
    for i, out in enumerate(far):
        out[...] = held[2, i * rows : (i + 1) * rows]


def gram(y, tiles, arrays, sources, far_parts=2):
    n = len(sources) * PIECE
    with_panel = len(tiles) > 1
    shapes = [(n, 2048)] + [(256, n)] * 3 + [(256 // far_parts, n)] * far_parts
    n_copies = sum(len(parts) for piece in sources for parts in piece)
    if with_panel:
        shapes.append((1024, 2048))
        n_copies += 10
    return pl.pallas_call(
        functools.partial(gram_kernel, sources, with_panel),
        out_shape=[jax.ShapeDtypeStruct(s, BF16) for s in shapes],
        in_specs=[SMEM] + ([ANY] * 10 if with_panel else [VMEM]) + [ANY] * len(arrays),
        out_specs=[VMEM] * len(shapes),
        scratch_shapes=[
            pltpu.VMEM((4, 256, n), BF16),
            pltpu.SemaphoreType.DMA((n_copies,)),
        ],
        compiler_params=pltpu.CompilerParams(vmem_limit_bytes=8 << 20),
        cost_estimate=pl.CostEstimate(
            flops=2 * 1024 * 2048 * n, bytes_accessed=8 << 20, transcendentals=0
        ),
        name="gram",
    )(y, *tiles, *arrays)


def near_kernel(c_ref, *refs):
    rights, lefts, from_left, from_right = refs[0:3], refs[3:6], refs[6:8], refs[8:10]
    first, second = refs[10:]
    left_first = c_ref[0] == 0
    at = 0
    for i in range(3):
        cols = slice(at, at + rights[i].shape[1])
        for rows in (slice(0, 128), slice(128, 256)):
            to_right, to_left = rights[i][rows, :], lefts[i][rows, :]
            if i < 2 and rows.start == 0:
                to_right = add(to_right, from_left[i][...]).astype(BF16)
            if i < 2 and rows.start == 128:
                to_left = add(to_left, from_right[i][...]).astype(BF16)
            first[rows, cols] = jnp.where(left_first, to_left, to_right)
            second[rows, cols] = jnp.where(left_first, to_right, to_left)
        at = cols.stop


def own_kernel(own0, own1, own2, from_left, from_right, from_far, total):
    at = 0
    for i, own in enumerate((own0, own1, own2)):
        cols = slice(at, at + own.shape[1])
        value = add(own[...], from_left[:, cols], from_right[:, cols])
        if i == 2:
            value = value + from_far[...].astype(F32)
        total[:, cols] = value.astype(BF16)
        at = cols.stop


def far_kernel(c_ref, y_ref, own, first, second, far_first, far_second, joined0, joined1, joined2, far, whole, theirs, mine):
    y, core = y_ref[0], c_ref[0]

    def rows(k):
        return pl.multiple_of(lax.rem(y + k, 4) * 256, 256)

    for k, part in ((0, own), (1 + 2 * core, first), (3 - 2 * core, second)):
        whole[pl.ds(rows(k), 256), :] = part[...]
    for offset, part in ((1 - core, far_first), (core, far_second)):
        whole[pl.ds(pl.multiple_of(rows(2) + 128 * offset, 128), 128), :] = part[...]
    at = 0
    for joined in (joined0, joined1, joined2):
        size = joined.shape[0]
        for half in range(2):
            start = half * 1024
            mine[half, at : at + size, :] = joined[:, start : start + TILE]
            theirs[half, at : at + size, :] = joined[:, start + TILE : start + 2 * TILE]
        at += size
    far[...] = jnp.dot(whole[512:], theirs[0], preferred_element_type=F32).astype(BF16)


def rest_kernel(whole, theirs, own, near, out):
    own[...] = jnp.dot(whole[:512], theirs[0], preferred_element_type=F32).astype(BF16)
    near[...] = jnp.dot(whole[:512], theirs[1], preferred_element_type=F32).astype(BF16)
    out[...] = jnp.dot(whole[512:], theirs[1], preferred_element_type=F32).astype(BF16)


def far_sum_kernel(whole, mine, arrived, upper, lower):
    total = jnp.dot(whole[512:], mine[0], preferred_element_type=F32) + arrived[...].astype(F32)
    upper[...] = total[:256].astype(BF16)
    lower[...] = total[256:].astype(BF16)


def rest_sum_kernel(whole, mine, a_own, a_near, a_out, own, near, out):
    def term(rows, half, arrived):
        return jnp.dot(whole[rows], mine[half], preferred_element_type=F32) + arrived[...].astype(F32)

    own[...] = term(slice(0, 512), 0, a_own)
    near[...] = term(slice(0, 512), 1, a_near).astype(BF16)
    out[...] = term(slice(512, 1024), 1, a_out).astype(BF16)


def call(kernel, operands, shapes, flops, limit=8, name=None):
    return pl.pallas_call(
        kernel,
        out_shape=[jax.ShapeDtypeStruct(*s) for s in shapes],
        in_specs=[SMEM if v.dtype == jnp.int32 else VMEM for v in operands],
        out_specs=[VMEM] * len(shapes),
        compiler_params=pltpu.CompilerParams(vmem_limit_bytes=limit << 20),
        cost_estimate=pl.CostEstimate(flops=flops, bytes_accessed=4 << 20, transcendentals=0),
        name=name,
    )(*operands)


def scaled_kernel(c_ref, xl_ref, y_ref, q_ref, s_ref, send0, send1, keep, q_buf, s_buf, sems):
    c = c_ref[0]
    scales = pltpu.make_async_copy(s_ref.at[0], s_buf, sems.at[8])
    scales.start()
    copies = []
    for step in range(4):
        for side, core in enumerate((1 - c, c)):
            start = pl.multiple_of((step % 2 * 2 + core) * TILE, TILE)
            copies.append(
                pltpu.make_async_copy(
                    q_ref.at[0, pl.ds(step // 2 * 256, 256), pl.ds(start, TILE)],
                    q_buf.at[2 * step + side],
                    sems.at[2 * step + side],
                )
            )
            copies[-1].start()
    scales.wait()
    for step in range(4):
        for side, core in enumerate((1 - c, c)):
            copies[2 * step + side].wait()
            start = pl.multiple_of((step % 2 * 2 + core) * TILE, TILE)
            for r in range(2):
                rows = slice(r * 128, r * 128 + 128)
                row = step // 2 * 2 + r
                scale = s_buf[row : row + 1, pl.ds(start, TILE)]
                value = q_buf[2 * step + side, rows, :].astype(F32) * scale
                if side:
                    keep[step, rows, :] = value
                else:
                    (send0, send1)[step // 2][step % 2, rows, :] = value.astype(BF16)


def scaled_parts(at, quant, scale):
    return pl.pallas_call(
        scaled_kernel,
        in_specs=[SMEM] * 3 + [HBM] * 2,
        out_specs=[VMEM] * 3,
        out_shape=[
            jax.ShapeDtypeStruct((2, 256, TILE), BF16),
            jax.ShapeDtypeStruct((2, 256, TILE), BF16),
            jax.ShapeDtypeStruct((4, 256, TILE), F32),
        ],
        scratch_shapes=[
            pltpu.VMEM((8, 256, TILE), BF16),
            pltpu.VMEM((4, 4 * TILE), F32),
            pltpu.SemaphoreType.DMA((9,)),
        ],
        compiler_params=pltpu.CompilerParams(vmem_limit_bytes=8 << 20),
        name="scaled",
    )(*at, in_hbm(quant), in_hbm(scale))


def pair_kernel(half, xl_ref, keep, arrived, to_inner, kept):
    xl = xl_ref[0]
    to_inner[...] = (keep[2 * half + 1 - xl] + arrived[1 - xl].astype(F32)).astype(BF16)
    kept[...] = keep[2 * half + xl] + arrived[xl].astype(F32)


def pieces_kernel(c_ref, xl_ref, tile, tile_s, kept, sent):
    core, xl = c_ref[0], xl_ref[0]
    for out, half in ((kept, xl), (sent, 1 - xl)):
        rows = pl.ds(pl.multiple_of((2 * half + core) * PIECE, PIECE), PIECE)
        out[:, :TILE] = tile[rows, :]
        out[:, TILE:] = tile_s[rows, :]


def halves_kernel(c_ref, first, second, far_first, far_second):
    core = c_ref[0]
    far_first[...] = first[pl.ds(pl.multiple_of(128 * (1 - core), 128), 128), :]
    far_second[...] = second[pl.ds(pl.multiple_of(128 * core, 128), 128), :]


def update_kernel(squares, tile, own, from_in, from_out, update):
    total = jnp.sum(jnp.sum(squares[...], axis=1, keepdims=True), axis=0, keepdims=True)
    gain = math.sqrt(M) / (1.5 * (jnp.sqrt(total) + EPSILON))
    linear, cubic = (math.sqrt(M) * 1.5) * gain, (math.sqrt(M) * 0.5) * gain * gain * gain
    product = add(own[...], from_in[...], from_out[...])
    update[...] = linear * tile[...].astype(F32) - cubic * product


def momentum_kernel(kept0, kept1, arrived0, arrived1, momentum, new_ref, tile_ref, squares_ref):
    total = jnp.zeros((8, TILE), F32)
    for half, (kept, arrived) in enumerate(((kept0, arrived0), (kept1, arrived1))):
        rows = slice(half * 256, half * 256 + 256)
        gradient = kept[...] + arrived[...].astype(F32)
        new = BETA * momentum[rows, :] + gradient
        nesterov = gradient + BETA * new
        new_ref[rows, :] = new
        tile_ref[rows, :] = nesterov.astype(BF16)
        total = total + jnp.sum((nesterov * nesterov).reshape(32, 8, TILE), axis=0)
    squares_ref[...] = total[:, :128] + total[:, 128:256] + total[:, 256:384] + total[:, 384:]


def together(steps, v, *arrays):
    for axis, bit in steps:
        v = swap_add(v, axis, bit)
    return lax.optimization_barrier((v, *arrays))


def start_sum(far0, far1):
    return yhop(far0, 1), yhop(far1, -1)


def body(grad_partial, grad_scale, momentum):
    depth = lax.axis_index("depth").astype(jnp.int32)
    at = [v.reshape(1) for v in (depth & 1, depth >> 1, lax.axis_index("col").astype(jnp.int32))]
    c, xl, y = at
    send0, send1, keep = scaled_parts(at, grad_partial, grad_scale)
    arrived = [sib(send0), sib(send1)]
    pairs = [
        call(
            functools.partial(pair_kernel, h),
            [xl, keep, arrived[h]],
            [((256, TILE), BF16), ((256, TILE), F32)],
            1 << 20,
            name="pair",
        )
        for h in range(2)
    ]
    arrived = [inner(p[0]) for p in pairs]
    new_momentum, tile, v = call(
        momentum_kernel,
        [pairs[0][1], pairs[1][1], *arrived, momentum],
        [((TILE, TILE), F32), ((TILE, TILE), BF16), ((8, 128), F32)],
        1 << 20,
        name="momentum",
    )

    tile_s = sib(tile)

    a, b = call(
        pieces_kernel, [c, xl, tile, tile_s], [((PIECE, 1024), BF16)] * 2, 1 << 16, name="pieces"
    )

    b = inner(b)
    ra, la = zhop(a, 1), zhop(a, -1)
    t_out = outer(tile)
    v, b = together([("depth", 1)], v, b)
    r2 = zhop(jnp.concatenate([b, ra], axis=0), 1)
    l2 = zhop(jnp.concatenate([la, b], axis=0), -1)
    t_in = inner(lax.optimization_barrier((tile, b))[0])
    v, r2, l2, t_out = together([("col", 1)], v, r2, l2, t_out)
    v, t_in, r2, l2 = lax.optimization_barrier((v, t_in, r2, l2))
    r3, l3 = zhop(r2, 1), zhop(l2, -1)
    v, t_in, t_out, t_in_s, t_out_s = lax.optimization_barrier(
        (v, t_in, t_out, sib(t_in), sib(t_out))
    )
    far_a, far_b = outer(t_in[:256]), inner(t_out[256:])
    v, far_a, far_b = together([("col", 2)], v, far_a, far_b)
    r4_b, l4_b = zhop(r3[:128], 1), zhop(l3[128:], -1)
    r4_a = zhop(r3[128:], 1)
    l5_b = zhop(l4_b, -1)
    t_in, t_in_s, t_out, t_out_s = (in_hbm(t) for t in (t_in, t_in_s, t_out, t_out_s))
    tiles = [tile, tile_s, t_in, t_in_s, far_a, far_b, sib(far_a), sib(far_b), t_out, t_out_s]
    joined0, right0, left0, own0, far0, far1, panel = gram(
        y,
        tiles,
        [in_hbm(t) for t in (a, b, ra, la, r2, l2)] + [r3, l3],
        [
            [[(0, 0, 128)], [(1, 0, 128)]],
            [[(2, 0, 128)], [(4, 0, 128)]],
            [[(3, 0, 128)], [(5, 128, 128)]],
            [[(4, 128, 128)], [(6, 0, 128)]],
            [[(5, 0, 128)], [(7, 128, 128)]],
        ],
    )
    l4_b, far0, far1 = lax.optimization_barrier((l4_b, far0, far1))
    from_left0, from_right0 = start_sum(far0, far1)
    r4_b, l4_b, panel, from_left0 = lax.optimization_barrier((r4_b, l4_b, panel, from_left0))
    joined1, right1, left1, own1, far0, far1 = gram(
        y,
        [panel],
        [r3, l3, r4_b, l4_b],
        [[[(0, 128, 128)], [(2, 0, 128)]], [[(1, 0, 128)], [(3, 0, 128)]]],
    )
    from_left1, from_right1 = start_sum(far0, far1)
    r4_a, l5_b, from_left0, from_right0 = lax.optimization_barrier(
        (r4_a, l5_b, from_left0, from_right0)
    )
    joined2, right2, left2, own2, far2 = gram(
        y, [panel], [r4_a, l5_b], [[[(0, 0, 128)], [(1, 0, 128)]]], far_parts=1
    )
    first, second = call(
        near_kernel,
        [c, right0, right1, right2, left0, left1, left2]
        + [from_left0, from_left1, from_right0, from_right1],
        [((256, 1024), BF16)] * 2,
        1 << 20,
        name="near",
    )
    v, first, second = lax.optimization_barrier((v, first, second))
    first, second = mixed(first, True), mixed(second, False)
    from_far = lax.ppermute(far2, "col", [(i, i ^ 2) for i in range(4)])
    v, first, second = together([("depth", 2)], v, first, second)
    (own,) = call(
        own_kernel,
        [own0, own1, own2, first, second, from_far],
        [((256, 1024), BF16)],
        1 << 20,
        name="own",
    )
    v, own = lax.optimization_barrier((v, own))
    first, second = mixed(own, True), mixed(own, False)
    v, first, second = together([("row", 1)], v, first, second)
    far_first, far_second = call(
        halves_kernel, [c, first, second], [((128, 1024), BF16)] * 2, 1 << 16, name="halves"
    )
    far_first, far_second = mixed(far_first, True), mixed(far_second, False)
    v, far_first, far_second = together([("row", 2)], v, far_first, far_second)

    far, whole, theirs, mine = call(
        far_kernel,
        [c, y, own, first, second, far_first, far_second, joined0, joined1, joined2],
        [((TILE, TILE), BF16), ((1024, 1024), BF16)] + [((2, 1024, TILE), BF16)] * 2,
        1 << 29,
        name="far",
    )
    far = sib(far)
    rest = call(rest_kernel, [whole, theirs], [((TILE, TILE), BF16)] * 3, 3 << 29, name="rest")
    rest = [sib(t) for t in rest]
    upper, lower = call(
        far_sum_kernel, [whole, mine, far], [((256, TILE), BF16)] * 2, 1 << 29, name="far_sum"
    )
    v, upper, lower = lax.optimization_barrier((v, upper, lower))
    a1, b1 = inner(upper), outer(lower)
    t_own, t_in, t_out = call(
        rest_sum_kernel,
        [whole, mine, *rest],
        [((TILE, TILE), F32)] + [((TILE, TILE), BF16)] * 2,
        3 << 29,
        name="rest_sum",
    )
    v, a1, b1 = together([("row", 4)], v, a1, b1)
    to_out = jnp.concatenate([add(t_out[:256], a1).astype(BF16), t_out[256:]], 0)
    to_in = jnp.concatenate([t_in[:256], add(t_in[256:], b1).astype(BF16)], 0)
    v, to_in, to_out = lax.optimization_barrier((v, to_in, to_out))
    from_in, from_out = inner(to_in), outer(to_out)
    v = swap_add(v, "row", 8)
    (update,) = call(
        update_kernel,
        [v, tile, t_own, from_in, from_out],
        [((TILE, TILE), F32)],
        1 << 20,
        name="update",
    )
    return (new_momentum, update)


def solution(mesh):
    placed = (P("depth", "row", "col"), P("depth", "row", "col"), P("row", ("col", "depth")))
    return jax.shard_map(
        body,
        mesh=mesh,
        in_specs=placed,
        out_specs=(P("row", ("col", "depth")), P("row", ("col", "depth"))),
        check_vma=False,
    )
```

```python
import functools
import math

import jax
import jax.numpy as jnp
from jax import lax
from jax.experimental import pallas as pl
from jax.experimental.pallas import tpu as pltpu
from jax.sharding import PartitionSpec as P

M = 8192
BETA = 0.95
EPSILON = 1e-07
F32 = jnp.float32
BF16 = jnp.bfloat16

NY = 4
TILE = 512
PIECE = 128
ZPERM = {
    s: [(r * 4 + d, (r + 2 * s * (1 - 2 * (d % 2))) % 16 * 4 + d) for r in range(16) for d in range(4)]
    for s in (1, -1)
}
YPERM = {s: [(y, (y + s) % 4) for y in range(4)] for s in (1, -1)}
SIB = [(d, d ^ 1) for d in range(4)]
INNER = [(d, d ^ 2) for d in range(4)]
OUTER = [(r * 4 + d, (r ^ 1) * 4 + (d ^ 2)) for r in range(16) for d in range(4)]


def sib(v):
    return lax.ppermute(v, "depth", SIB)


def inner(v):
    return lax.ppermute(v, "depth", INNER)


def outer(v):
    return lax.ppermute(v, ("row", "depth"), OUTER)


def across(v):
    return lax.ppermute(v, "row", [(r, r ^ 1) for r in range(16)])


def zhop(v, s):
    return lax.ppermute(v, ("row", "depth"), ZPERM[s])


def yhop(v, s):
    return lax.ppermute(v, "col", YPERM[s])


def in_hbm(v):
    return pltpu.with_memory_space_constraint(v, pltpu.HBM)


def mixed(v, first):
    step = {0: -1, 1: 1} if first else {0: 1, 1: -1}
    pairs = [(y * 4 + d, (y + step[d % 2]) % 4 * 4 + d) for y in range(4) for d in range(4)]
    return lax.ppermute(v, ("col", "depth"), pairs)


def swap_add(v, axis, bit):
    return v + lax.ppermute(v, axis, [(i, i ^ bit) for i in range(lax.axis_size(axis))])


def add(*vs):
    total = vs[0].astype(F32)
    for v in vs[1:]:
        total = total + v.astype(F32)
    return total


VMEM = pl.BlockSpec(memory_space=pltpu.VMEM)
SMEM = pl.BlockSpec(memory_space=pltpu.SMEM)
HBM = pl.BlockSpec(memory_space=pltpu.HBM)
ANY = pl.BlockSpec(memory_space=pl.ANY)


def gram_kernel(sources, with_panel, y_ref, *refs):
    n_tiles = 10 if with_panel else 1
    n_in = n_tiles + 1 + max(i for piece in sources for parts in piece for i, _, _ in parts)
    tiles, parts_in, outs = refs[:n_tiles], refs[n_tiles:n_in], list(refs[n_in:])
    held, sems = outs[-2:]
    joined, right, left, own, *far = outs[:-2]
    copies = []

    def copy(source, target):
        copies.append(pltpu.make_async_copy(source, target, sems.at[len(copies)]))
        copies[-1].start()

    for p, piece in enumerate(sources):
        for half, parts in enumerate(piece):
            row = p * PIECE
            for i, start, size in parts:
                copy(
                    parts_in[i].at[pl.ds(start, size)],
                    joined.at[pl.ds(row, size), pl.ds(half * 1024, 1024)],
                )
                row += size
    late = 0
    if with_panel:
        panel = far.pop()
        for i in range(4):
            copy(tiles[i], panel.at[pl.ds(0, TILE), pl.ds(i * TILE, TILE)])
        late = len(copies)
        for i in range(2):
            for part in range(2):
                copy(
                    tiles[4 + 2 * i + part],
                    panel.at[pl.ds(TILE + 256 * part, 256), pl.ds(i * TILE, TILE)],
                )
            copy(tiles[8 + i], panel.at[pl.ds(TILE, TILE), pl.ds((2 + i) * TILE, TILE)])
        late -= len(copies)
    else:
        panel = tiles[0]
    for c in copies[: late or None]:
        c.wait()
    y = y_ref[0]
    for block in range(4):
        if late and block == 2:
            for c in copies[late:]:
                c.wait()
        held[lax.rem(block + 4 - y, 4)] = lax.dot_general(
            panel[block * 256 : block * 256 + 256, :],
            joined[...],
            (((1,), (1,)), ((), ())),
            preferred_element_type=F32,
        ).astype(BF16)
    own[...] = held[0]
    right[...] = held[1]
    left[...] = held[3]
    rows = 256 // len(far)
    for i, out in enumerate(far):
        out[...] = held[2, i * rows : (i + 1) * rows]


def gram(y, tiles, arrays, sources, far_parts=2):
    n = len(sources) * PIECE
    with_panel = len(tiles) > 1
    shapes = [(n, 2048)] + [(256, n)] * 3 + [(256 // far_parts, n)] * far_parts
    n_copies = sum(len(parts) for piece in sources for parts in piece)
    if with_panel:
        shapes.append((1024, 2048))
        n_copies += 10
    return pl.pallas_call(
        functools.partial(gram_kernel, sources, with_panel),
        out_shape=[jax.ShapeDtypeStruct(s, BF16) for s in shapes],
        in_specs=[SMEM] + ([ANY] * 10 if with_panel else [VMEM]) + [ANY] * len(arrays),
        out_specs=[VMEM] * len(shapes),
        scratch_shapes=[
            pltpu.VMEM((4, 256, n), BF16),
            pltpu.SemaphoreType.DMA((n_copies,)),
        ],
        compiler_params=pltpu.CompilerParams(vmem_limit_bytes=8 << 20),
        cost_estimate=pl.CostEstimate(
            flops=2 * 1024 * 2048 * n, bytes_accessed=8 << 20, transcendentals=0
        ),
        name="gram",
    )(y, *tiles, *arrays)


def near_kernel(c_ref, *refs):
    rights, lefts, from_left, from_right = refs[0:3], refs[3:6], refs[6:8], refs[8:10]
    first, second = refs[10:]
    left_first = c_ref[0] == 0
    at = 0
    for i in range(3):
        cols = slice(at, at + rights[i].shape[1])
        for rows in (slice(0, 128), slice(128, 256)):
            to_right, to_left = rights[i][rows, :], lefts[i][rows, :]
            if i < 2 and rows.start == 0:
                to_right = add(to_right, from_left[i][...]).astype(BF16)
            if i < 2 and rows.start == 128:
                to_left = add(to_left, from_right[i][...]).astype(BF16)
            first[rows, cols] = jnp.where(left_first, to_left, to_right)
            second[rows, cols] = jnp.where(left_first, to_right, to_left)
        at = cols.stop


def own_kernel(own0, own1, own2, from_left, from_right, from_far, total):
    at = 0
    for i, own in enumerate((own0, own1, own2)):
        cols = slice(at, at + own.shape[1])
        value = add(own[...], from_left[:, cols], from_right[:, cols])
        if i == 2:
            value = value + from_far[...].astype(F32)
        total[:, cols] = value.astype(BF16)
        at = cols.stop


def far_kernel(c_ref, y_ref, own, first, second, far_first, far_second, joined0, joined1, joined2, far, whole, theirs, mine):
    y, core = y_ref[0], c_ref[0]

    def rows(k):
        return pl.multiple_of(lax.rem(y + k, 4) * 256, 256)

    for k, part in ((0, own), (1 + 2 * core, first), (3 - 2 * core, second)):
        whole[pl.ds(rows(k), 256), :] = part[...]
    for offset, part in ((1 - core, far_first), (core, far_second)):
        whole[pl.ds(pl.multiple_of(rows(2) + 128 * offset, 128), 128), :] = part[...]
    at = 0
    for joined in (joined0, joined1, joined2):
        size = joined.shape[0]
        for half in range(2):
            start = half * 1024
            mine[half, at : at + size, :] = joined[:, start : start + TILE]
            theirs[half, at : at + size, :] = joined[:, start + TILE : start + 2 * TILE]
        at += size
    far[...] = jnp.dot(whole[512:], theirs[0], preferred_element_type=F32).astype(BF16)


def rest_kernel(whole, theirs, own, near, out):
    own[...] = jnp.dot(whole[:512], theirs[0], preferred_element_type=F32).astype(BF16)
    near[...] = jnp.dot(whole[:512], theirs[1], preferred_element_type=F32).astype(BF16)
    out[...] = jnp.dot(whole[512:], theirs[1], preferred_element_type=F32).astype(BF16)


def far_sum_kernel(whole, mine, arrived, upper, lower):
    total = jnp.dot(whole[512:], mine[0], preferred_element_type=F32) + arrived[...].astype(F32)
    upper[...] = total[:256].astype(BF16)
    lower[...] = total[256:].astype(BF16)


def rest_sum_kernel(whole, mine, a_own, a_near, a_out, own, near, out):
    def term(rows, half, arrived):
        return jnp.dot(whole[rows], mine[half], preferred_element_type=F32) + arrived[...].astype(F32)

    own[...] = term(slice(0, 512), 0, a_own)
    near[...] = term(slice(0, 512), 1, a_near).astype(BF16)
    out[...] = term(slice(512, 1024), 1, a_out).astype(BF16)


def call(kernel, operands, shapes, flops, limit=8, name=None):
    return pl.pallas_call(
        kernel,
        out_shape=[jax.ShapeDtypeStruct(*s) for s in shapes],
        in_specs=[SMEM if v.dtype == jnp.int32 else VMEM for v in operands],
        out_specs=[VMEM] * len(shapes),
        compiler_params=pltpu.CompilerParams(vmem_limit_bytes=limit << 20),
        cost_estimate=pl.CostEstimate(flops=flops, bytes_accessed=4 << 20, transcendentals=0),
        name=name,
    )(*operands)


def scaled_kernel(first, c_ref, y_ref, q_ref, s_ref, send, keep, q_buf, s_buf, sems):
    c = c_ref[0]
    scales = pltpu.make_async_copy(s_ref.at[0], s_buf, sems.at[4])
    scales.start()
    copies = []
    for half in range(2):
        for side, core in enumerate((1 - c, c)):
            start = pl.multiple_of((half * 2 + core) * TILE, TILE)
            copies.append(
                pltpu.make_async_copy(
                    q_ref.at[0, pl.ds(first * 128, 256), pl.ds(start, TILE)],
                    q_buf.at[2 * half + side],
                    sems.at[2 * half + side],
                )
            )
            copies[-1].start()
    scales.wait()
    for half in range(2):
        for side, core in enumerate((1 - c, c)):
            copies[2 * half + side].wait()
            start = pl.multiple_of((half * 2 + core) * TILE, TILE)
            for r in range(2):
                rows = slice(r * 128, r * 128 + 128)
                scale = s_buf[first + r : first + r + 1, pl.ds(start, TILE)]
                value = q_buf[2 * half + side, rows, :].astype(F32) * scale
                if side:
                    keep[half, rows, :] = value
                else:
                    send[half, rows, :] = value.astype(BF16)


def scaled_part(c, y, quant, scale, half):
    return pl.pallas_call(
        functools.partial(scaled_kernel, 2 * half),
        in_specs=[SMEM] * 2 + [HBM] * 2,
        out_specs=[VMEM] * 2,
        out_shape=[
            jax.ShapeDtypeStruct((2, 256, TILE), BF16),
            jax.ShapeDtypeStruct((2, 256, TILE), F32),
        ],
        scratch_shapes=[
            pltpu.VMEM((4, 256, TILE), BF16),
            pltpu.VMEM((4, 4 * TILE), F32),
            pltpu.SemaphoreType.DMA((5,)),
        ],
        compiler_params=pltpu.CompilerParams(vmem_limit_bytes=8 << 20),
        name="scaled",
    )(c, y, in_hbm(quant), in_hbm(scale))


def pair_kernel(xl_ref, keep, arrived, to_inner, kept):
    xl = xl_ref[0]
    to_inner[...] = (keep[1 - xl] + arrived[1 - xl].astype(F32)).astype(BF16)
    kept[...] = keep[xl] + arrived[xl].astype(F32)


def pieces_kernel(c_ref, xl_ref, tile, tile_s, kept, sent):
    core, xl = c_ref[0], xl_ref[0]
    for out, half in ((kept, xl), (sent, 1 - xl)):
        rows = pl.ds(pl.multiple_of((2 * half + core) * PIECE, PIECE), PIECE)
        out[:, :TILE] = tile[rows, :]
        out[:, TILE:] = tile_s[rows, :]


def halves_kernel(c_ref, first, second, far_first, far_second):
    core = c_ref[0]
    far_first[...] = first[pl.ds(pl.multiple_of(128 * (1 - core), 128), 128), :]
    far_second[...] = second[pl.ds(pl.multiple_of(128 * core, 128), 128), :]


def update_kernel(squares, tile, own, from_in, from_out, update):
    total = jnp.sum(jnp.sum(squares[...], axis=1, keepdims=True), axis=0, keepdims=True)
    gain = math.sqrt(M) / (1.5 * (jnp.sqrt(total) + EPSILON))
    linear, cubic = (math.sqrt(M) * 1.5) * gain, (math.sqrt(M) * 0.5) * gain * gain * gain
    product = add(own[...], from_in[...], from_out[...])
    update[...] = linear * tile[...].astype(F32) - cubic * product


def momentum_kernel(kept0, kept1, arrived0, arrived1, momentum, new_ref, tile_ref, squares_ref):
    total = jnp.zeros((8, TILE), F32)
    for half, (kept, arrived) in enumerate(((kept0, arrived0), (kept1, arrived1))):
        rows = slice(half * 256, half * 256 + 256)
        gradient = kept[...] + arrived[...].astype(F32)
        new = BETA * momentum[rows, :] + gradient
        nesterov = gradient + BETA * new
        new_ref[rows, :] = new
        tile_ref[rows, :] = nesterov.astype(BF16)
        total = total + jnp.sum((nesterov * nesterov).reshape(32, 8, TILE), axis=0)
    squares_ref[...] = total[:, :128] + total[:, 128:256] + total[:, 256:384] + total[:, 384:]


def together(steps, v, *arrays):
    for axis, bit in steps:
        v = swap_add(v, axis, bit)
    return lax.optimization_barrier((v, *arrays))


def start_sum(far0, far1):
    return yhop(far0, 1), yhop(far1, -1)


def body(grad_partial, grad_scale, momentum):
    depth = lax.axis_index("depth").astype(jnp.int32)
    at = [v.reshape(1) for v in (depth & 1, depth >> 1, lax.axis_index("col").astype(jnp.int32))]
    c, xl, y = at
    parts = [scaled_part(c, y, grad_partial, grad_scale, h) for h in range(2)]
    arrived = [sib(p[0]) for p in parts]
    pairs = [
        call(
            pair_kernel,
            [xl, parts[h][1], arrived[h]],
            [((256, TILE), BF16), ((256, TILE), F32)],
            1 << 20,
            name="pair",
        )
        for h in range(2)
    ]
    arrived = [inner(p[0]) for p in pairs]
    new_momentum, tile, v = call(
        momentum_kernel,
        [pairs[0][1], pairs[1][1], *arrived, momentum],
        [((TILE, TILE), F32), ((TILE, TILE), BF16), ((8, 128), F32)],
        1 << 20,
        name="momentum",
    )

    tile_s = sib(tile)

    a, b = call(
        pieces_kernel, [c, xl, tile, tile_s], [((PIECE, 1024), BF16)] * 2, 1 << 16, name="pieces"
    )

    b = inner(b)
    ra, la = zhop(a, 1), zhop(a, -1)
    t_out = outer(tile)
    v, b = together([("depth", 1)], v, b)
    r2 = zhop(jnp.concatenate([b, ra], axis=0), 1)
    l2 = zhop(jnp.concatenate([la, b], axis=0), -1)
    t_in = inner(lax.optimization_barrier((tile, b))[0])
    v, r2, l2, t_out = together([("col", 1)], v, r2, l2, t_out)
    v, t_in, r2, l2 = lax.optimization_barrier((v, t_in, r2, l2))
    r3, l3 = zhop(r2, 1), zhop(l2, -1)
    v, t_in, t_out, t_in_s, t_out_s = lax.optimization_barrier(
        (v, t_in, t_out, sib(t_in), sib(t_out))
    )
    far_a, far_b = outer(t_in[:256]), inner(t_out[256:])
    v, far_a, far_b = together([("col", 2)], v, far_a, far_b)
    r4_b, l4_b = zhop(r3[:128], 1), zhop(l3[128:], -1)
    r4_a = zhop(r3[128:], 1)
    l5_b = zhop(l4_b, -1)
    t_in, t_in_s, t_out, t_out_s = (in_hbm(t) for t in (t_in, t_in_s, t_out, t_out_s))
    tiles = [tile, tile_s, t_in, t_in_s, far_a, far_b, sib(far_a), sib(far_b), t_out, t_out_s]
    joined0, right0, left0, own0, far0, far1, panel = gram(
        y,
        tiles,
        [in_hbm(t) for t in (a, b, ra, la, r2, l2)] + [r3, l3],
        [
            [[(0, 0, 128)], [(1, 0, 128)]],
            [[(2, 0, 128)], [(4, 0, 128)]],
            [[(3, 0, 128)], [(5, 128, 128)]],
            [[(4, 128, 128)], [(6, 0, 128)]],
            [[(5, 0, 128)], [(7, 128, 128)]],
        ],
    )
    l4_b, far0, far1 = lax.optimization_barrier((l4_b, far0, far1))
    from_left0, from_right0 = start_sum(far0, far1)
    r4_b, l4_b, panel, from_left0 = lax.optimization_barrier((r4_b, l4_b, panel, from_left0))
    joined1, right1, left1, own1, far0, far1 = gram(
        y,
        [panel],
        [r3, l3, r4_b, l4_b],
        [[[(0, 128, 128)], [(2, 0, 128)]], [[(1, 0, 128)], [(3, 0, 128)]]],
    )
    from_left1, from_right1 = start_sum(far0, far1)
    r4_a, l5_b, from_left0, from_right0 = lax.optimization_barrier(
        (r4_a, l5_b, from_left0, from_right0)
    )
    joined2, right2, left2, own2, far2 = gram(
        y, [panel], [r4_a, l5_b], [[[(0, 0, 128)], [(1, 0, 128)]]], far_parts=1
    )
    first, second = call(
        near_kernel,
        [c, right0, right1, right2, left0, left1, left2]
        + [from_left0, from_left1, from_right0, from_right1],
        [((256, 1024), BF16)] * 2,
        1 << 20,
        name="near",
    )
    v, first, second = lax.optimization_barrier((v, first, second))
    first, second = mixed(first, True), mixed(second, False)
    from_far = lax.ppermute(far2, "col", [(i, i ^ 2) for i in range(4)])
    v, first, second = together([("depth", 2)], v, first, second)
    (own,) = call(
        own_kernel,
        [own0, own1, own2, first, second, from_far],
        [((256, 1024), BF16)],
        1 << 20,
        name="own",
    )
    v, own = lax.optimization_barrier((v, own))
    first, second = mixed(own, True), mixed(own, False)
    v, first, second = together([("row", 1)], v, first, second)
    far_first, far_second = call(
        halves_kernel, [c, first, second], [((128, 1024), BF16)] * 2, 1 << 16, name="halves"
    )
    far_first, far_second = mixed(far_first, True), mixed(far_second, False)
    v, far_first, far_second = together([("row", 2)], v, far_first, far_second)

    far, whole, theirs, mine = call(
        far_kernel,
        [c, y, own, first, second, far_first, far_second, joined0, joined1, joined2],
        [((TILE, TILE), BF16), ((1024, 1024), BF16)] + [((2, 1024, TILE), BF16)] * 2,
        1 << 29,
        name="far",
    )
    far = sib(far)
    rest = call(rest_kernel, [whole, theirs], [((TILE, TILE), BF16)] * 3, 3 << 29, name="rest")
    rest = [sib(t) for t in rest]
    upper, lower = call(
        far_sum_kernel, [whole, mine, far], [((256, TILE), BF16)] * 2, 1 << 29, name="far_sum"
    )
    v, upper, lower = lax.optimization_barrier((v, upper, lower))
    a1, b1 = inner(upper), outer(lower)
    t_own, t_in, t_out = call(
        rest_sum_kernel,
        [whole, mine, *rest],
        [((TILE, TILE), F32)] + [((TILE, TILE), BF16)] * 2,
        3 << 29,
        name="rest_sum",
    )
    v, a1, b1 = together([("row", 4)], v, a1, b1)
    to_out = jnp.concatenate([add(t_out[:256], a1).astype(BF16), t_out[256:]], 0)
    to_in = jnp.concatenate([t_in[:256], add(t_in[256:], b1).astype(BF16)], 0)
    v, to_in, to_out = lax.optimization_barrier((v, to_in, to_out))
    from_in, from_out = inner(to_in), outer(to_out)
    v = swap_add(v, "row", 8)
    (update,) = call(
        update_kernel,
        [v, tile, t_own, from_in, from_out],
        [((TILE, TILE), F32)],
        1 << 20,
        name="update",
    )
    return (new_momentum, update)


def solution(mesh):
    placed = (P("depth", "row", "col"), P("depth", "row", "col"), P("row", ("col", "depth")))
    return jax.shard_map(
        body,
        mesh=mesh,
        in_specs=placed,
        out_specs=(P("row", ("col", "depth")), P("row", ("col", "depth"))),
        check_vma=False,
    )
```

```python
import functools
import math

import jax
import jax.numpy as jnp
from jax import lax
from jax.experimental import pallas as pl
from jax.experimental.pallas import tpu as pltpu
from jax.sharding import PartitionSpec as P

M = 8192
BETA = 0.95
EPSILON = 1e-07
F32 = jnp.float32
BF16 = jnp.bfloat16

NY = 4
TILE = 512
PIECE = 128
ZPERM = {s: [(r, (r + 2 * s) % 16) for r in range(16)] for s in (1, -1)}
YPERM = {s: [(y, (y + s) % 4) for y in range(4)] for s in (1, -1)}
SIB = [(d, d ^ 1) for d in range(4)]
INNER = [(d, d ^ 2) for d in range(4)]
OUTER = [(r * 4 + d, (r ^ 1) * 4 + (d ^ 2)) for r in range(16) for d in range(4)]


def sib(v):
    return lax.ppermute(v, "depth", SIB)


def inner(v):
    return lax.ppermute(v, "depth", INNER)


def outer(v):
    return lax.ppermute(v, ("row", "depth"), OUTER)


def across(v):
    return lax.ppermute(v, "row", [(r, r ^ 1) for r in range(16)])


def zhop(v, s):
    return lax.ppermute(v, "row", ZPERM[s])


def yhop(v, s):
    return lax.ppermute(v, "col", YPERM[s])


def in_hbm(v):
    return pltpu.with_memory_space_constraint(v, pltpu.HBM)


def mixed(v, first):
    step = {0: -1, 1: 1} if first else {0: 1, 1: -1}
    pairs = [(y * 4 + d, (y + step[d % 2]) % 4 * 4 + d) for y in range(4) for d in range(4)]
    return lax.ppermute(v, ("col", "depth"), pairs)


def swap_add(v, axis, bit):
    return v + lax.ppermute(v, axis, [(i, i ^ bit) for i in range(lax.axis_size(axis))])


def add(*vs):
    total = vs[0].astype(F32)
    for v in vs[1:]:
        total = total + v.astype(F32)
    return total


VMEM = pl.BlockSpec(memory_space=pltpu.VMEM)
SMEM = pl.BlockSpec(memory_space=pltpu.SMEM)
HBM = pl.BlockSpec(memory_space=pltpu.HBM)
ANY = pl.BlockSpec(memory_space=pl.ANY)


def gram_kernel(sources, with_panel, y_ref, *refs):
    n_tiles = 10 if with_panel else 1
    n_in = n_tiles + 1 + max(i for piece in sources for parts in piece for i, _, _ in parts)
    tiles, parts_in, outs = refs[:n_tiles], refs[n_tiles:n_in], list(refs[n_in:])
    held, sems = outs[-2:]
    joined, right, left, own, *far = outs[:-2]
    copies = []

    def copy(source, target):
        copies.append(pltpu.make_async_copy(source, target, sems.at[len(copies)]))
        copies[-1].start()

    for p, piece in enumerate(sources):
        for half, parts in enumerate(piece):
            row = p * PIECE
            for i, start, size in parts:
                copy(
                    parts_in[i].at[pl.ds(start, size)],
                    joined.at[pl.ds(row, size), pl.ds(half * 1024, 1024)],
                )
                row += size
    late = 0
    if with_panel:
        panel = far.pop()
        for i in range(4):
            copy(tiles[i], panel.at[pl.ds(0, TILE), pl.ds(i * TILE, TILE)])
        late = len(copies)
        for i in range(2):
            for part in range(2):
                copy(
                    tiles[4 + 2 * i + part],
                    panel.at[pl.ds(TILE + 256 * part, 256), pl.ds(i * TILE, TILE)],
                )
            copy(tiles[8 + i], panel.at[pl.ds(TILE, TILE), pl.ds((2 + i) * TILE, TILE)])
        late -= len(copies)
    else:
        panel = tiles[0]
    for c in copies[: late or None]:
        c.wait()
    y = y_ref[0]
    for block in range(4):
        if late and block == 2:
            for c in copies[late:]:
                c.wait()
        held[lax.rem(block + 4 - y, 4)] = lax.dot_general(
            panel[block * 256 : block * 256 + 256, :],
            joined[...],
            (((1,), (1,)), ((), ())),
            preferred_element_type=F32,
        ).astype(BF16)
    own[...] = held[0]
    right[...] = held[1]
    left[...] = held[3]
    rows = 256 // len(far)
    for i, out in enumerate(far):
        out[...] = held[2, i * rows : (i + 1) * rows]


def gram(y, tiles, arrays, sources, far_parts=2):
    n = len(sources) * PIECE
    with_panel = len(tiles) > 1
    shapes = [(n, 2048)] + [(256, n)] * 3 + [(256 // far_parts, n)] * far_parts
    n_copies = sum(len(parts) for piece in sources for parts in piece)
    if with_panel:
        shapes.append((1024, 2048))
        n_copies += 10
    return pl.pallas_call(
        functools.partial(gram_kernel, sources, with_panel),
        out_shape=[jax.ShapeDtypeStruct(s, BF16) for s in shapes],
        in_specs=[SMEM] + ([ANY] * 10 if with_panel else [VMEM]) + [ANY] * len(arrays),
        out_specs=[VMEM] * len(shapes),
        scratch_shapes=[
            pltpu.VMEM((4, 256, n), BF16),
            pltpu.SemaphoreType.DMA((n_copies,)),
        ],
        compiler_params=pltpu.CompilerParams(vmem_limit_bytes=8 << 20),
        cost_estimate=pl.CostEstimate(
            flops=2 * 1024 * 2048 * n, bytes_accessed=8 << 20, transcendentals=0
        ),
        name="gram",
    )(y, *tiles, *arrays)


def near_kernel(c_ref, *refs):
    rights, lefts, from_left, from_right = refs[0:3], refs[3:6], refs[6:8], refs[8:10]
    first, second = refs[10:]
    left_first = c_ref[0] == 0
    at = 0
    for i in range(3):
        cols = slice(at, at + rights[i].shape[1])
        for rows in (slice(0, 128), slice(128, 256)):
            to_right, to_left = rights[i][rows, :], lefts[i][rows, :]
            if i < 2 and rows.start == 0:
                to_right = add(to_right, from_left[i][...]).astype(BF16)
            if i < 2 and rows.start == 128:
                to_left = add(to_left, from_right[i][...]).astype(BF16)
            first[rows, cols] = jnp.where(left_first, to_left, to_right)
            second[rows, cols] = jnp.where(left_first, to_right, to_left)
        at = cols.stop


def own_kernel(own0, own1, own2, from_left, from_right, from_far, total):
    at = 0
    for i, own in enumerate((own0, own1, own2)):
        cols = slice(at, at + own.shape[1])
        value = add(own[...], from_left[:, cols], from_right[:, cols])
        if i == 2:
            value = value + from_far[...].astype(F32)
        total[:, cols] = value.astype(BF16)
        at = cols.stop


def far_kernel(c_ref, y_ref, own, first, second, far_first, far_second, joined0, joined1, joined2, far, whole, theirs, mine):
    y, core = y_ref[0], c_ref[0]

    def rows(k):
        return pl.multiple_of(lax.rem(y + k, 4) * 256, 256)

    for k, part in ((0, own), (1 + 2 * core, first), (3 - 2 * core, second)):
        whole[pl.ds(rows(k), 256), :] = part[...]
    for offset, part in ((1 - core, far_first), (core, far_second)):
        whole[pl.ds(pl.multiple_of(rows(2) + 128 * offset, 128), 128), :] = part[...]
    at = 0
    for joined in (joined0, joined1, joined2):
        size = joined.shape[0]
        for half in range(2):
            start = half * 1024
            mine[half, at : at + size, :] = joined[:, start : start + TILE]
            theirs[half, at : at + size, :] = joined[:, start + TILE : start + 2 * TILE]
        at += size
    far[...] = jnp.dot(whole[512:], theirs[0], preferred_element_type=F32).astype(BF16)


def rest_kernel(whole, theirs, own, near, out):
    own[...] = jnp.dot(whole[:512], theirs[0], preferred_element_type=F32).astype(BF16)
    near[...] = jnp.dot(whole[:512], theirs[1], preferred_element_type=F32).astype(BF16)
    out[...] = jnp.dot(whole[512:], theirs[1], preferred_element_type=F32).astype(BF16)


def far_sum_kernel(whole, mine, arrived, upper, lower):
    total = jnp.dot(whole[512:], mine[0], preferred_element_type=F32) + arrived[...].astype(F32)
    upper[...] = total[:256].astype(BF16)
    lower[...] = total[256:].astype(BF16)


def rest_sum_kernel(whole, mine, a_own, a_near, a_out, own, near, out):
    def term(rows, half, arrived):
        return jnp.dot(whole[rows], mine[half], preferred_element_type=F32) + arrived[...].astype(F32)

    own[...] = term(slice(0, 512), 0, a_own)
    near[...] = term(slice(0, 512), 1, a_near).astype(BF16)
    out[...] = term(slice(512, 1024), 1, a_out).astype(BF16)


def call(kernel, operands, shapes, flops, limit=8, name=None):
    return pl.pallas_call(
        kernel,
        out_shape=[jax.ShapeDtypeStruct(*s) for s in shapes],
        in_specs=[SMEM if v.dtype == jnp.int32 else VMEM for v in operands],
        out_specs=[VMEM] * len(shapes),
        compiler_params=pltpu.CompilerParams(vmem_limit_bytes=limit << 20),
        cost_estimate=pl.CostEstimate(flops=flops, bytes_accessed=4 << 20, transcendentals=0),
        name=name,
    )(*operands)


def scaled_kernel(c_ref, xl_ref, y_ref, q_ref, s_ref, send0, send1, keep, q_buf, s_buf, sems):
    c = c_ref[0]
    scales = pltpu.make_async_copy(s_ref.at[0], s_buf, sems.at[8])
    scales.start()
    copies = []
    for step in range(4):
        for side, core in enumerate((1 - c, c)):
            start = pl.multiple_of((step % 2 * 2 + core) * TILE, TILE)
            copies.append(
                pltpu.make_async_copy(
                    q_ref.at[0, pl.ds(step // 2 * 256, 256), pl.ds(start, TILE)],
                    q_buf.at[2 * step + side],
                    sems.at[2 * step + side],
                )
            )
            copies[-1].start()
    scales.wait()
    for step in range(4):
        for side, core in enumerate((1 - c, c)):
            copies[2 * step + side].wait()
            start = pl.multiple_of((step % 2 * 2 + core) * TILE, TILE)
            for r in range(2):
                rows = slice(r * 128, r * 128 + 128)
                row = step // 2 * 2 + r
                scale = s_buf[row : row + 1, pl.ds(start, TILE)]
                value = q_buf[2 * step + side, rows, :].astype(F32) * scale
                if side:
                    keep[step, rows, :] = value
                else:
                    (send0, send1)[step // 2][step % 2, rows, :] = value.astype(BF16)


def scaled_parts(at, quant, scale):
    return pl.pallas_call(
        scaled_kernel,
        in_specs=[SMEM] * 3 + [HBM] * 2,
        out_specs=[VMEM] * 3,
        out_shape=[
            jax.ShapeDtypeStruct((2, 256, TILE), BF16),
            jax.ShapeDtypeStruct((2, 256, TILE), BF16),
            jax.ShapeDtypeStruct((4, 256, TILE), F32),
        ],
        scratch_shapes=[
            pltpu.VMEM((8, 256, TILE), BF16),
            pltpu.VMEM((4, 4 * TILE), F32),
            pltpu.SemaphoreType.DMA((9,)),
        ],
        compiler_params=pltpu.CompilerParams(vmem_limit_bytes=8 << 20),
        name="scaled",
    )(*at, in_hbm(quant), in_hbm(scale))


def pair_kernel(half, xl_ref, keep, arrived, to_inner, kept):
    xl = xl_ref[0]
    to_inner[...] = (keep[2 * half + 1 - xl] + arrived[1 - xl].astype(F32)).astype(BF16)
    kept[...] = keep[2 * half + xl] + arrived[xl].astype(F32)


def pieces_kernel(c_ref, xl_ref, tile, tile_s, kept, sent):
    core, xl = c_ref[0], xl_ref[0]
    for out, half in ((kept, xl), (sent, 1 - xl)):
        rows = pl.ds(pl.multiple_of((2 * half + core) * PIECE, PIECE), PIECE)
        out[:, :TILE] = tile[rows, :]
        out[:, TILE:] = tile_s[rows, :]


def halves_kernel(c_ref, first, second, far_first, far_second):
    core = c_ref[0]
    far_first[...] = first[pl.ds(pl.multiple_of(128 * (1 - core), 128), 128), :]
    far_second[...] = second[pl.ds(pl.multiple_of(128 * core, 128), 128), :]


def update_kernel(squares, tile, own, from_in, from_out, update, held, sems):
    total = jnp.sum(jnp.sum(squares[...], axis=1, keepdims=True), axis=0, keepdims=True)
    gain = math.sqrt(M) / (1.5 * (jnp.sqrt(total) + EPSILON))
    linear, cubic = (math.sqrt(M) * 1.5) * gain, (math.sqrt(M) * 0.5) * gain * gain * gain
    copies = []
    for i in range(4):
        rows = pl.ds(i * 128, 128)
        product = add(own[rows, :], from_in[rows, :], from_out[rows, :])
        held[rows, :] = linear * tile[rows, :].astype(F32) - cubic * product
        copies.append(pltpu.make_async_copy(held.at[rows], update.at[rows], sems.at[i]))
        copies[-1].start()
    for copy in copies:
        copy.wait()


def momentum_kernel(
    kept0, kept1, arrived0, arrived1, momentum, new_ref, tile_ref, squares_ref, held, sems
):
    total = jnp.zeros((8, TILE), F32)
    copies = []
    for half, (kept, arrived) in enumerate(((kept0, arrived0), (kept1, arrived1))):
        rows = slice(half * 256, half * 256 + 256)
        gradient = kept[...] + arrived[...].astype(F32)
        new = BETA * momentum[rows, :] + gradient
        nesterov = gradient + BETA * new
        held[rows, :] = new
        copies.append(
            pltpu.make_async_copy(
                held.at[pl.ds(half * 256, 256)], new_ref.at[pl.ds(half * 256, 256)], sems.at[half]
            )
        )
        copies[-1].start()
        tile_ref[rows, :] = nesterov.astype(BF16)
        total = total + jnp.sum((nesterov * nesterov).reshape(32, 8, TILE), axis=0)
    squares_ref[...] = total[:, :128] + total[:, 128:256] + total[:, 256:384] + total[:, 384:]
    for copy in copies:
        copy.wait()


def together(steps, v, *arrays):
    for axis, bit in steps:
        v = swap_add(v, axis, bit)
    return lax.optimization_barrier((v, *arrays))


def start_sum(far0, far1):
    return yhop(far0, 1), yhop(far1, -1)


def body(grad_partial, grad_scale, momentum):
    depth = lax.axis_index("depth").astype(jnp.int32)
    at = [v.reshape(1) for v in (depth & 1, depth >> 1, lax.axis_index("col").astype(jnp.int32))]
    c, xl, y = at
    send0, send1, keep = scaled_parts(at, grad_partial, grad_scale)
    arrived = [sib(send0), sib(send1)]
    pairs = [
        call(
            functools.partial(pair_kernel, h),
            [xl, keep, arrived[h]],
            [((256, TILE), BF16), ((256, TILE), F32)],
            1 << 20,
            name="pair",
        )
        for h in range(2)
    ]
    arrived = [inner(p[0]) for p in pairs]
    new_momentum, tile, v = pl.pallas_call(
        momentum_kernel,
        out_shape=[
            jax.ShapeDtypeStruct((TILE, TILE), F32),
            jax.ShapeDtypeStruct((TILE, TILE), BF16),
            jax.ShapeDtypeStruct((8, 128), F32),
        ],
        in_specs=[VMEM] * 5,
        out_specs=[ANY, VMEM, VMEM],
        scratch_shapes=[pltpu.VMEM((TILE, TILE), F32), pltpu.SemaphoreType.DMA((2,))],
        compiler_params=pltpu.CompilerParams(vmem_limit_bytes=8 << 20),
        cost_estimate=pl.CostEstimate(flops=1 << 20, bytes_accessed=4 << 20, transcendentals=0),
        name="momentum",
    )(pairs[0][1], pairs[1][1], *arrived, momentum)

    tile_s = sib(tile)

    a, b = call(
        pieces_kernel, [c, xl, tile, tile_s], [((PIECE, 1024), BF16)] * 2, 1 << 16, name="pieces"
    )

    b = inner(b)
    ra, la = zhop(a, 1), zhop(a, -1)
    t_out = outer(tile)
    v, b = together([("depth", 1)], v, b)
    r2 = zhop(jnp.concatenate([b, ra], axis=0), 1)
    l2 = zhop(jnp.concatenate([la, b], axis=0), -1)
    t_in = inner(lax.optimization_barrier((tile, b))[0])
    v, r2, l2, t_out = together([("col", 1)], v, r2, l2, t_out)
    v, t_in, r2, l2 = lax.optimization_barrier((v, t_in, r2, l2))
    r3, l3 = zhop(r2, 1), zhop(l2, -1)
    v, t_in, t_out, t_in_s, t_out_s = lax.optimization_barrier(
        (v, t_in, t_out, sib(t_in), sib(t_out))
    )
    far_a, far_b = outer(t_in[:256]), inner(t_out[256:])
    v, far_a, far_b = together([("col", 2)], v, far_a, far_b)
    r4_b, l4_b = zhop(r3[:128], 1), zhop(l3[128:], -1)
    r4_a = zhop(r3[128:], 1)
    l5_b = zhop(l4_b, -1)
    t_in, t_in_s, t_out, t_out_s = (in_hbm(t) for t in (t_in, t_in_s, t_out, t_out_s))
    tiles = [tile, tile_s, t_in, t_in_s, far_a, far_b, sib(far_a), sib(far_b), t_out, t_out_s]
    joined0, right0, left0, own0, far0, far1, panel = gram(
        y,
        tiles,
        [in_hbm(t) for t in (a, b, ra, la, r2, l2)] + [r3, l3],
        [
            [[(0, 0, 128)], [(1, 0, 128)]],
            [[(2, 0, 128)], [(4, 0, 128)]],
            [[(3, 0, 128)], [(5, 128, 128)]],
            [[(4, 128, 128)], [(6, 0, 128)]],
            [[(5, 0, 128)], [(7, 128, 128)]],
        ],
    )
    l4_b, far0, far1 = lax.optimization_barrier((l4_b, far0, far1))
    from_left0, from_right0 = start_sum(far0, far1)
    r4_b, l4_b, panel, from_left0 = lax.optimization_barrier((r4_b, l4_b, panel, from_left0))
    joined1, right1, left1, own1, far0, far1 = gram(
        y,
        [panel],
        [r3, l3, r4_b, l4_b],
        [[[(0, 128, 128)], [(2, 0, 128)]], [[(1, 0, 128)], [(3, 0, 128)]]],
    )
    from_left1, from_right1 = start_sum(far0, far1)
    r4_a, l5_b, from_left0, from_right0 = lax.optimization_barrier(
        (r4_a, l5_b, from_left0, from_right0)
    )
    joined2, right2, left2, own2, far2 = gram(
        y, [panel], [r4_a, l5_b], [[[(0, 0, 128)], [(1, 0, 128)]]], far_parts=1
    )
    first, second = call(
        near_kernel,
        [c, right0, right1, right2, left0, left1, left2]
        + [from_left0, from_left1, from_right0, from_right1],
        [((256, 1024), BF16)] * 2,
        1 << 20,
        name="near",
    )
    v, first, second = lax.optimization_barrier((v, first, second))
    first, second = mixed(first, True), mixed(second, False)
    from_far = lax.ppermute(far2, "col", [(i, i ^ 2) for i in range(4)])
    v, first, second = together([("depth", 2)], v, first, second)
    (own,) = call(
        own_kernel,
        [own0, own1, own2, first, second, from_far],
        [((256, 1024), BF16)],
        1 << 20,
        name="own",
    )
    v, own = lax.optimization_barrier((v, own))
    first, second = mixed(own, True), mixed(own, False)
    v, first, second = together([("row", 1)], v, first, second)
    far_first, far_second = call(
        halves_kernel, [c, first, second], [((128, 1024), BF16)] * 2, 1 << 16, name="halves"
    )
    far_first, far_second = mixed(far_first, True), mixed(far_second, False)
    v, far_first, far_second = together([("row", 2)], v, far_first, far_second)

    far, whole, theirs, mine = call(
        far_kernel,
        [c, y, own, first, second, far_first, far_second, joined0, joined1, joined2],
        [((TILE, TILE), BF16), ((1024, 1024), BF16)] + [((2, 1024, TILE), BF16)] * 2,
        1 << 29,
        name="far",
    )
    far = sib(far)
    rest = call(rest_kernel, [whole, theirs], [((TILE, TILE), BF16)] * 3, 3 << 29, name="rest")
    rest = [sib(t) for t in rest]
    upper, lower = call(
        far_sum_kernel, [whole, mine, far], [((256, TILE), BF16)] * 2, 1 << 29, name="far_sum"
    )
    v, upper, lower = lax.optimization_barrier((v, upper, lower))
    a1, b1 = inner(upper), outer(lower)
    t_own, t_in, t_out = call(
        rest_sum_kernel,
        [whole, mine, *rest],
        [((TILE, TILE), F32)] + [((TILE, TILE), BF16)] * 2,
        3 << 29,
        name="rest_sum",
    )
    v, a1, b1 = together([("row", 4)], v, a1, b1)
    to_out = jnp.concatenate([add(t_out[:256], a1).astype(BF16), t_out[256:]], 0)
    to_in = jnp.concatenate([t_in[:256], add(t_in[256:], b1).astype(BF16)], 0)
    v, to_in, to_out = lax.optimization_barrier((v, to_in, to_out))
    from_in, from_out = inner(to_in), outer(to_out)
    v = swap_add(v, "row", 8)
    update = pl.pallas_call(
        update_kernel,
        out_shape=jax.ShapeDtypeStruct((TILE, TILE), F32),
        in_specs=[VMEM] * 5,
        out_specs=ANY,
        scratch_shapes=[pltpu.VMEM((TILE, TILE), F32), pltpu.SemaphoreType.DMA((4,))],
        compiler_params=pltpu.CompilerParams(vmem_limit_bytes=8 << 20),
        name="update",
    )(v, tile, t_own, from_in, from_out)
    return (new_momentum, update)


def solution(mesh):
    placed = (P("depth", "row", "col"), P("depth", "row", "col"), P("row", ("col", "depth")))
    return jax.shard_map(
        body,
        mesh=mesh,
        in_specs=placed,
        out_specs=(P("row", ("col", "depth")), P("row", ("col", "depth"))),
        check_vma=False,
    )
```
